32 devices in a mesh: dp: 4 (over y, x), expert: 8 (over z, core).
Axes of the slice: x: 2, y: 2, z: 4, core: 2. Of those that a mesh axis runs over, the one named last changes fastest.
Arguments:
- tokens: bfloat16 [256, 2560], P(('dp', 'expert')), may hold values from -6 to 6
- routes: int32 [256, 6], P(('dp', 'expert')), may hold values from 0 to 7, all different within a row; in each aligned block of 8 rows (0 to 7, 8 to 15, ...) at most 7 rows name the same one
- router: float32 [2560, 8], replicated, may hold values from -0.125 to 0.125
- w_gate: bfloat16 [2560, 8192], P(None, 'expert'), may hold values from -0.125 to 0.125
- w_up: bfloat16 [2560, 8192], P(None, 'expert'), may hold values from -0.125 to 0.125
- w_down: bfloat16 [2560, 8192], P(None, 'expert'), may hold values from -0.1875 to 0.1875
- cotangent: bfloat16 [256, 2560], P(('dp', 'expert')), may hold values from -6 to 6
Outputs:
- mixed: bfloat16 [256, 2560], P(('dp', 'expert'))
- grad_tokens: bfloat16 [256, 2560], P(('dp', 'expert'))
- grad_router: float32 [2560, 8], replicated
- grad_gate: float32 [2560, 8192], P('dp', 'expert')
- grad_up: float32 [2560, 8192], P('dp', 'expert')
- grad_down: float32 [2560, 8192], P('dp', 'expert')
The draws below stay inside these ranges and needn't reach their ends.
Inputs may be any that keep to these rules, and one draw needn't show every extreme that they name: `routes`: each row names 6 different experts. Among the rows of one device no expert is named more than 7 times, and in every draw some expert is named exactly 7 times by the rows of some device.
All inputs are finite; a program needn't handle non-finite values.
Results may differ from the reference program's by a relative error of at most 0.02.
Values may be sent and summed in bfloat16 or wider, within the bound.
No kernel may reach another device: no remote copies, remote signals or barrier semaphores. Data moves between devices by JAX's collectives and lax.ppermute only.
A program may use at most 128 MiB of HBM per device.

```python
import math
import jax
import jax.numpy as jnp
import numpy as np
from jax import lax

D = 2560
FFW = 1024
TOP = 6
EXPERTS = 8
TOK_DEV = 8
HSPLIT = 1
FF_DEV = 1024
TOKENS = 256
CAP = 7
N_DP = 4
N_EXPERT = 8


def strengthened(result, stream_key, source, target, blocks, factor):
    owner, partner = [(jnp.arange(result.shape[dim]) // (result.shape[dim] // blocks)).reshape([-1 if axis == dim else 1 for axis in range(result.ndim)]) for dim in (source, target)]
    chosen = jax.random.permutation(stream_key, blocks)[partner]
    strong = (owner == chosen) | (owner == (partner + blocks // 2) % blocks)
    return jnp.where(strong, factor * result, result)


def steps_of(rng, shape, split, least, largest):
    gain, own = 1.0, jax.random.fold_in(rng, 6)
    for dim, blocks in split:
        draws = jnp.exp(jax.random.uniform(jax.random.fold_in(own, dim), (blocks,), jnp.float32, least / len(split), largest / len(split)))
        gain = gain * jnp.repeat(draws, shape[dim] // blocks).reshape([-1 if axis == dim else 1 for axis in range(len(shape))])
    return gain


def deal_out(own_key, own, number, rows, count, top, limit, slope):
    order = jax.random.permutation(own_key, count)
    crowded, usual = portions_of(count, rows * top, limit, slope, True), portions_of(count, rows * top, limit, slope, False)
    places = jnp.arange(count)

    def named(lengths, offset_by):
        used = int((lengths > 0).sum())
        fixed = max(1, used // 4)
        moved = fixed + (places - fixed + offset_by * (used - fixed)) % max(1, count - fixed)
        return jnp.zeros((count,), jnp.int32).at[order[jnp.where(places < fixed, places, moved)]].set(jnp.asarray(lengths, jnp.int32))

    lengths = jnp.where(number % 4 == 0, named(crowded, number // 4), named(usual, number - number // 4 - 1))
    mixed = jax.random.permutation(jax.random.fold_in(own, 3), count)
    source_of, receiver = mixed[0:count // 2 * 2:2], mixed[1:count // 2 * 2:2]
    room = jnp.minimum(lengths[source_of] - 1, limit - lengths[receiver]) // 2
    room = jnp.where((source_of == order[0]) | (receiver == order[0]) | (lengths[receiver] == 0), 0, jnp.maximum(room, 0))
    moved = jax.random.randint(jax.random.fold_in(own, 4), (count // 2,), 0, 1 << 20) % (room + 1)
    lengths = lengths.at[source_of].add(-moved).at[receiver].add(moved)
    members = jnp.searchsorted(jnp.cumsum(lengths), jnp.arange(rows * top), side="right").astype(jnp.int32)
    table = members.reshape(top, rows).T
    table = table[jax.random.permutation(jax.random.fold_in(own, 1), rows)]
    offset_by = jax.random.randint(jax.random.fold_in(own, 2), (rows, 1), 0, top)
    return jnp.take_along_axis(table, (jnp.arange(top)[None, :] + offset_by) % top, axis=1)


def portions_of(number_of, total, most, skew, full):
    weights = [(1 << 20) // math.isqrt(rank ** skew) + 1 for rank in range(1, number_of + 1)]
    largest = most if full else min(most, max(-(-total // number_of), total * weights[0] // sum(weights)))
    least = 1 if total - largest >= number_of - 1 else 0
    counts, surplus = [largest] + [least] * (number_of - 1), total - largest - least * (number_of - 1)
    while surplus > 0:
        candidates = [i for i in range(1, number_of) if counts[i] < largest] or [i for i in range(1, number_of) if counts[i] < most]
        whole, remaining = sum([weights[i] for i in candidates]), surplus
        for i in candidates:
            more = min(most - counts[i], max(1, remaining * weights[i] // whole), surplus)
            counts[i] = counts[i] + more
            surplus = surplus - more
    return np.array(counts)


def bell_draw(own_key, dims, width, reach, pieces=(), held_as=jnp.bfloat16):
    level = steps_of(own_key, dims, pieces, -0.22, 0.18) if pieces else 1.0
    drawn = jax.random.normal(own_key, dims, jnp.float32) * width * level
    return jnp.minimum(jnp.maximum(drawn, -reach), reach).astype(held_as)


def noise_with(rng, dims, scale, reach, pieces, heavy, kind=jnp.bfloat16):
    drawn = scale * jax.random.normal(rng, dims, jnp.float32)
    if pieces:
        drawn = drawn * steps_of(rng, dims, pieces, -0.22, 0.18)
    return jnp.clip(strengthened(drawn, jax.random.fold_in(rng, 3), *heavy), -reach, reach).astype(kind)


def setup_inputs(seed: int = 0) -> dict:
    seeds = jax.random.split(jax.random.key(seed), 8)
    tokens = noise_with(seeds[0], (TOKENS, D), 1.0, 6.0, ((0, 32),), (0, 1, 32, 2.75))
    routes_keys = jax.random.split(jax.random.fold_in(seeds[1], 1), TOKENS // TOK_DEV)
    routes_turns = jax.random.permutation(jax.random.fold_in(seeds[1], 3), TOKENS // TOK_DEV)
    routes = jax.vmap(lambda own, number: deal_out(jax.random.fold_in(seeds[1], 2), own, number, TOK_DEV, EXPERTS, TOP, CAP, 2))(routes_keys, routes_turns).reshape((TOKENS, TOP))
    router = bell_draw(seeds[2], (D, EXPERTS), D ** -0.5, 0.125, (), jnp.float32)
    w_gate = bell_draw(seeds[3], (D, EXPERTS * FFW), D ** -0.5, 0.125, ((1, 8),))
    w_up = bell_draw(seeds[4], (D, EXPERTS * FFW), D ** -0.5, 0.125, ((1, 8),))
    w_down = bell_draw(seeds[5], (D, EXPERTS * FFW), FFW ** -0.5, 0.1875, ((1, 8),))
    cotangent = bell_draw(seeds[6], (TOKENS, D), 1.0, 6.0, ((0, 32),))
    return {"tokens": tokens, "routes": routes, "router": router, "w_gate": w_gate, "w_up": w_up, "w_down": w_down, "cotangent": cotangent}


def expert_hidden(inputs, gate_matrix, up_matrix):
    gate_pre = jnp.dot(inputs, gate_matrix, preferred_element_type=jnp.float32)
    up_pre = jnp.dot(inputs, up_matrix, preferred_element_type=jnp.float32)
    hidden = (jax.nn.silu(gate_pre) * up_pre).astype(jnp.bfloat16)
    return gate_pre, up_pre, hidden


def block_down(hidden, down_matrix):
    total = jnp.zeros((hidden.shape[0], D), jnp.float32)
    for block in range(HSPLIT):
        lo = block * FF_DEV
        piece = jnp.dot(hidden[:, lo:lo + FF_DEV], down_matrix[:, lo:lo + FF_DEV].T,
                        preferred_element_type=jnp.float32).astype(jnp.bfloat16)
        total = total + lax.optimization_barrier(piece).astype(jnp.float32)
    return total.astype(jnp.bfloat16)


def expert_backward(slot_grad, gate_pre, up_pre, gate_matrix, up_matrix, down_matrix):
    hidden_grad = jnp.dot(slot_grad, down_matrix, preferred_element_type=jnp.float32)
    sigma = jax.nn.sigmoid(gate_pre)
    gate_grad = (hidden_grad * up_pre * sigma * (1.0 + gate_pre * (1.0 - sigma))).astype(jnp.bfloat16)
    up_grad = (hidden_grad * gate_pre * sigma).astype(jnp.bfloat16)
    total = jnp.zeros((slot_grad.shape[0], D), jnp.float32)
    for block in range(HSPLIT):
        lo = block * FF_DEV
        piece = jnp.dot(gate_grad[:, lo:lo + FF_DEV], gate_matrix[:, lo:lo + FF_DEV].T, preferred_element_type=jnp.float32)
        piece = piece + jnp.dot(up_grad[:, lo:lo + FF_DEV], up_matrix[:, lo:lo + FF_DEV].T, preferred_element_type=jnp.float32)
        total = total + lax.optimization_barrier(piece.astype(jnp.bfloat16)).astype(jnp.float32)
    return gate_grad, up_grad, total.astype(jnp.bfloat16)


def stacked(weight):
    return weight.reshape(D, EXPERTS, FFW).transpose(1, 0, 2)


def unstacked(grad):
    return grad.transpose(1, 0, 2).reshape(D, EXPERTS * FFW)


def group_sum(left, right):
    group_rows = N_EXPERT * CAP
    left_wide = left.astype(jnp.float32).reshape(N_DP, group_rows, left.shape[1])
    right_wide = right.astype(jnp.float32).reshape(N_DP, group_rows, right.shape[1])
    parts = jnp.einsum("grd,grf->gdf", left_wide, right_wide, precision=lax.Precision.HIGHEST)
    return jnp.sum(parts.astype(jnp.bfloat16).astype(jnp.float32), axis=0)


def reference(tokens, routes, router, w_gate, w_up, w_down, cotangent):
    blocks = TOKENS // TOK_DEV
    highest = lax.Precision.HIGHEST
    tokens_wide = tokens.astype(jnp.float32)
    logits = jnp.dot(tokens_wide, router, precision=highest)
    expert_ids = jnp.arange(EXPERTS, dtype=jnp.int32)
    choose = routes[:, :, None] == expert_ids[None, None, :]
    choose_f = choose.astype(jnp.float32)
    picked = jnp.sum(choose_f * logits[:, None, :], axis=2)
    affinity = jax.nn.sigmoid(picked)
    denominator = jnp.sum(affinity, axis=1, keepdims=True)
    gate_values = affinity / denominator

    choose_i = choose.astype(jnp.int32).reshape(blocks, TOK_DEV, TOP, EXPERTS)
    per_token = jnp.sum(choose_i, axis=2)
    before = jnp.cumsum(per_token, axis=1) - per_token
    position = jnp.sum(choose_i * before[:, :, None, :], axis=3).reshape(TOKENS, TOP)
    block_index = (jnp.arange(TOKENS, dtype=jnp.int32) // TOK_DEV)[:, None]
    flat_slot = routes * (blocks * CAP) + block_index * CAP + position
    slot_total = EXPERTS * blocks * CAP
    sources = jnp.full((slot_total + 1,), TOKENS * TOP, dtype=jnp.int32)
    sources = sources.at[flat_slot.reshape(-1)].set(jnp.arange(TOKENS * TOP, dtype=jnp.int32))
    sources = sources[:slot_total].reshape(EXPERTS, blocks * CAP)

    tokens_pad = jnp.concatenate([tokens, jnp.zeros((1, D), jnp.bfloat16)], axis=0)
    cotangent_pad = jnp.concatenate([cotangent, jnp.zeros((1, D), jnp.bfloat16)], axis=0)
    gates_pad = jnp.concatenate([gate_values.reshape(-1), jnp.zeros((1,), jnp.float32)], axis=0)

    def expert_step(carry, inputs):
        mixed_acc, input_acc, pull_acc = carry
        gate_matrix, up_matrix, down_matrix, slot_source = inputs
        token_of = slot_source // TOP
        expert_rows = tokens_pad[token_of]
        grad_rows = cotangent_pad[token_of]
        slot_gate = gates_pad[slot_source]
        gate_pre, up_pre, hidden = expert_hidden(expert_rows, gate_matrix, up_matrix)
        output = block_down(hidden, down_matrix)
        output_wide = lax.optimization_barrier(output).astype(jnp.float32)
        mixed_acc = mixed_acc.at[token_of].add(slot_gate[:, None] * output_wide)
        pull_acc = pull_acc.at[slot_source].set(jnp.sum(grad_rows.astype(jnp.float32) * output_wide, axis=1))
        slot_grad = (slot_gate[:, None] * grad_rows.astype(jnp.float32)).astype(jnp.bfloat16)
        gate_grad, up_grad, input_grad = expert_backward(slot_grad, gate_pre, up_pre, gate_matrix, up_matrix, down_matrix)
        input_acc = input_acc.at[token_of].add(lax.optimization_barrier(input_grad).astype(jnp.float32))
        part_gate = group_sum(expert_rows, gate_grad)
        part_up = group_sum(expert_rows, up_grad)
        part_down = group_sum(slot_grad, hidden)
        return (mixed_acc, input_acc, pull_acc), (part_gate, part_up, part_down)

    start_carry = (jnp.zeros((TOKENS + 1, D), jnp.float32), jnp.zeros((TOKENS + 1, D), jnp.float32),
                   jnp.zeros((TOKENS * TOP + 1,), jnp.float32))
    final_carry, grads = lax.scan(expert_step, start_carry,
                                  (stacked(w_gate), stacked(w_up), stacked(w_down), sources))
    mixed_acc, input_acc, pull_acc = final_carry
    grad_gate, grad_up, grad_down = grads

    mixed = mixed_acc[:TOKENS].astype(jnp.bfloat16)
    gate_pull = pull_acc[:TOKENS * TOP].reshape(TOKENS, TOP)
    mean_pull = jnp.sum(gate_values * gate_pull, axis=1, keepdims=True)
    logit_grad = (gate_pull - mean_pull) / denominator * affinity * (1.0 - affinity)
    per_logit = jnp.sum(choose_f * logit_grad[:, :, None], axis=1)
    grad_router = jnp.dot(tokens_wide.T, per_logit, precision=highest)
    router_back = jnp.dot(per_logit, router.T, precision=highest)
    grad_tokens = (input_acc[:TOKENS] + router_back).astype(jnp.bfloat16)
    return (mixed, grad_tokens, grad_router, unstacked(grad_gate), unstacked(grad_up), unstacked(grad_down))
```

```python
import jax
import jax.numpy as jnp
from jax import lax
from jax.sharding import PartitionSpec as P

F32 = jnp.float32
BF16 = jnp.bfloat16
LANES = 128
GATHER_BYTES = 8 << 20


def swap(x, axis, mask):
    count = lax.axis_size(axis)
    return lax.ppermute(x, axis, [(i, i ^ mask) for i in range(count)])


def ordered(stack, index):
    count = stack.shape[0]
    rest = stack.shape[1:]
    bit = 1
    while bit < count:
        halves = stack.reshape((count // (2 * bit), 2, bit) + rest)
        flipped = (index // bit) % 2 == 1
        stack = jnp.where(flipped, halves[:, ::-1], halves).reshape((count,) + rest)
        bit *= 2
    return stack


def exact_dot(left, right, contract):
    parts = []
    rest = right
    for _ in range(3):
        part = lax.reduce_precision(rest, 8, 7)
        parts.append(part.astype(BF16))
        rest = rest - part
    return sum(
        lax.dot_general(left, part, contract, preferred_element_type=F32) for part in parts[::-1]
    )


def gates_of(rows, chosen, router):
    experts = router.shape[1]
    logits = exact_dot(rows, router, (((1,), (0,)), ((), ())))
    ids = jnp.arange(experts, dtype=BF16)
    picked = jnp.any(chosen[:, :, None] == ids[None, None, :], axis=1)
    affinity = jnp.where(picked, jax.nn.sigmoid(logits), 0.0)
    denominator = jnp.sum(affinity, axis=1, keepdims=True)
    return picked, affinity, denominator, affinity / denominator


def forward(rows, w_gate, w_up):
    gate_pre = jnp.dot(rows, w_gate, preferred_element_type=F32)
    up_pre = jnp.dot(rows, w_up, preferred_element_type=F32)
    sigma = jax.nn.sigmoid(gate_pre)
    return gate_pre, up_pre, sigma


def hidden_grads(slot_grad, gate_pre, up_pre, sigma, w_down):
    hidden_grad = jnp.dot(slot_grad, w_down, preferred_element_type=F32)
    gate_grad = (hidden_grad * up_pre * sigma * (1.0 + gate_pre * (1.0 - sigma))).astype(BF16)
    up_grad = (hidden_grad * gate_pre * sigma).astype(BF16)
    return gate_grad, up_grad


def local(tokens, routes, router, w_gate, w_up, w_down, cotangent):
    tok_count, features = tokens.shape
    experts = router.shape[1]
    fanout = routes.shape[1]
    hidden_units = w_gate.shape[1]
    devices = lax.axis_size("expert")
    groups = lax.axis_size("dp")
    sharing = devices // experts
    chips = devices // 2
    group_rows = devices * tok_count
    me = lax.axis_index("expert")
    group = lax.axis_index("dp")
    core, chip = me % 2, me // 2
    own_expert = me // sharing
    whole = groups * group_rows * features * 4 <= GATHER_BYTES

    def over_chips(x):
        return ordered(jnp.stack([x] + [swap(x, "expert", 2 * m) for m in range(1, chips)]), chip)

    def both_cores(x):
        pair = ordered(jnp.stack([x, swap(x, "expert", 1)]), core)
        return jnp.swapaxes(pair, 0, 1).reshape(-1, x.shape[-1])

    def over_groups(x):
        return [swap(x, "dp", m) for m in range(1, groups)]

    routes_wide = jnp.pad(routes.astype(BF16), ((0, 0), (0, LANES - fanout)))
    message = jnp.concatenate([tokens, routes_wide], axis=1)
    message_core = over_chips(message)
    grads_core = over_chips(cotangent)
    own_message = both_cores(message_core)
    own_cot = both_cores(grads_core)

    rows = own_message[:, :features]
    picked, affinity, denominator, gates = gates_of(
        rows, own_message[:, features : features + fanout], router
    )

    def own_column(table):
        return lax.dynamic_slice_in_dim(table, own_expert, 1, axis=1)

    slot_gate = own_column(gates)
    gate_pre, up_pre, sigma = forward(rows, w_gate, w_up)
    hidden = (gate_pre * sigma * up_pre).astype(BF16)
    output = lax.dot_general(hidden, w_down, (((1,), (1,)), ((), ())), preferred_element_type=F32)
    cot_wide = own_cot.astype(F32)
    pull = jnp.sum(cot_wide * output, axis=1)
    mixed_part = (slot_gate * output).astype(BF16)
    slot_grad = (slot_gate * cot_wide).astype(BF16)
    gate_grad, up_grad = hidden_grads(slot_grad, gate_pre, up_pre, sigma, w_down)
    contract = (((1,), (1,)), ((), ()))
    input_part = (
        lax.dot_general(gate_grad, w_gate, contract, preferred_element_type=F32)
        + lax.dot_general(up_grad, w_up, contract, preferred_element_type=F32)
    ).astype(BF16)

    def give_back(part):
        parts = part.reshape(chips, 2, tok_count, -1)
        keep = lax.dynamic_index_in_dim(parts, core, 1, keepdims=False).astype(F32)
        send = lax.dynamic_index_in_dim(parts, 1 - core, 1, keepdims=False)
        summed = (keep + swap(send, "expert", 1).astype(F32)).astype(BF16)
        total = lax.dynamic_index_in_dim(summed, chip, 0, keepdims=False).astype(F32)
        for m in range(1, chips):
            piece = lax.dynamic_index_in_dim(summed, chip ^ m, 0, keepdims=False)
            total = total + swap(piece, "expert", 2 * m).astype(F32)
        return total

    mixed = give_back(mixed_part).astype(BF16)
    input_sum = give_back(input_part)

    pulls = both_cores(over_chips(pull[None, :]))
    pulls = jnp.sum(pulls.reshape(experts, sharing, group_rows), axis=1).T
    mean_pull = jnp.sum(gates * pulls, axis=1, keepdims=True)
    logit_grad = (pulls - mean_pull) / denominator * affinity * (1.0 - affinity)
    logit_grad = jnp.where(picked, logit_grad, 0.0)
    own_logit = lax.dynamic_slice_in_dim(logit_grad, me * tok_count, tok_count, axis=0)
    router_back = lax.dot_general(
        own_logit, router, (((1,), (1,)), ((), ())), precision=lax.Precision.HIGHEST
    )
    grad_tokens = (input_sum + router_back).astype(BF16)

    first = (((0,), (0,)), ((), ()))
    if whole:
        far_rows, far_slot, far_gate, far_up, far_hidden = [], [], [], [], []
        far_message = over_groups(message_core)
        far_cot = over_groups(grads_core)
        far_message = jnp.concatenate([both_cores(x) for x in far_message], axis=0)
        far_cot = jnp.concatenate([both_cores(x) for x in far_cot], axis=0)
        far_rows = far_message[:, :features]
        far_gates = gates_of(far_rows, far_message[:, features : features + fanout], router)[3]
        far_pre, far_up, far_sigma = forward(far_rows, w_gate, w_up)
        far_hidden = (far_pre * far_sigma * far_up).astype(BF16)
        far_slot = (own_column(far_gates) * far_cot.astype(F32)).astype(BF16)
        far_gate_grad, far_up_grad = hidden_grads(far_slot, far_pre, far_up, far_sigma, w_down)
        width = features // groups

        def cut(x):
            return lax.dynamic_slice_in_dim(x, group * width, width, axis=1)

        all_rows = jnp.concatenate([rows, far_rows])
        rows_cut = cut(all_rows)
        slot_cut = cut(jnp.concatenate([slot_grad, far_slot]))
        grad_gate = lax.dot_general(
            rows_cut, jnp.concatenate([gate_grad, far_gate_grad]), first, preferred_element_type=F32
        )
        grad_up = lax.dot_general(
            rows_cut, jnp.concatenate([up_grad, far_up_grad]), first, preferred_element_type=F32
        )
        grad_down = lax.dot_general(
            slot_cut, jnp.concatenate([hidden, far_hidden]), first, preferred_element_type=F32
        )
        logit_all = jnp.stack([logit_grad] + over_groups(logit_grad))
        logit_all = ordered(logit_all, group).reshape(-1, experts)
        in_order = ordered(all_rows.reshape(groups, group_rows, features), group)
        grad_router = exact_dot(in_order.reshape(-1, features), logit_all, first)
    else:
        grad_router = lax.psum(
            exact_dot(tokens, own_logit, first), ("dp", "expert")
        )
        parts = [
            lax.dot_general(left, right, first, preferred_element_type=F32)
            for left, right in ((rows, gate_grad), (rows, up_grad), (slot_grad, hidden))
        ]
        summed = lax.psum_scatter(
            jnp.concatenate(parts, axis=1).astype(BF16), "dp", scatter_dimension=0, tiled=True
        ).astype(F32)
        grad_gate, grad_up, grad_down = jnp.split(summed, 3, axis=1)
    return (mixed, grad_tokens, grad_router, grad_gate, grad_up, grad_down)


def solution(mesh):
    return jax.shard_map(
        local,
        mesh=mesh,
        in_specs=(
            P(("dp", "expert"), None),
            P(("dp", "expert"), None),
            P(),
            P(None, "expert"),
            P(None, "expert"),
            P(None, "expert"),
            P(("dp", "expert"), None),
        ),
        out_specs=(
            P(("dp", "expert"), None),
            P(("dp", "expert"), None),
            P(),
            P("dp", "expert"),
            P("dp", "expert"),
            P("dp", "expert"),
        ),
        check_vma=False,
    )
```

```python
import jax
import jax.numpy as jnp
from jax import lax
from jax.sharding import PartitionSpec as P

F32 = jnp.float32
BF16 = jnp.bfloat16
LANES = 128
GATHER_BYTES = 8 << 20


def swap(x, axis, mask):
    count = lax.axis_size(axis)
    return lax.ppermute(x, axis, [(i, i ^ mask) for i in range(count)])


def exact_dot(left, right, contract):
    parts = []
    rest = right
    for _ in range(3):
        part = lax.reduce_precision(rest, 8, 7)
        parts.append(part.astype(BF16))
        rest = rest - part
    return sum(
        lax.dot_general(left, part, contract, preferred_element_type=F32) for part in parts[::-1]
    )


def gates_of(rows, chosen, router):
    experts = router.shape[1]
    logits = exact_dot(rows, router, (((1,), (0,)), ((), ())))
    ids = jnp.arange(experts, dtype=BF16)
    picked = jnp.any(chosen[:, :, None] == ids[None, None, :], axis=1)
    affinity = jnp.where(picked, jax.nn.sigmoid(logits), 0.0)
    denominator = jnp.sum(affinity, axis=1, keepdims=True)
    return picked, affinity, denominator, affinity / denominator


def local(tokens, routes, router, w_gate, w_up, w_down, cotangent):
    tok_count, features = tokens.shape
    experts = router.shape[1]
    fanout = routes.shape[1]
    hidden_units = w_gate.shape[1]
    devices = lax.axis_size("expert")
    groups = lax.axis_size("dp")
    sharing = devices // experts
    chips = devices // 2
    group_rows = devices * tok_count
    me = lax.axis_index("expert")
    group = lax.axis_index("dp")
    core, chip = me % 2, me // 2
    own_expert = me // sharing
    whole = groups * group_rows * features * 4 <= GATHER_BYTES

    def over_chips(x):
        out = jnp.zeros((chips,) + x.shape, x.dtype)
        for m in range(chips):
            piece = x if m == 0 else swap(x, "expert", 2 * m)
            out = lax.dynamic_update_index_in_dim(out, piece, chip ^ m, 0)
        return out

    def over_cores(x):
        other = swap(x, "expert", 1)
        return jnp.where(core == 0, jnp.stack([x, other]), jnp.stack([other, x]))

    routes_wide = jnp.pad(routes.astype(BF16), ((0, 0), (0, LANES - fanout)))
    message = jnp.concatenate([tokens, cotangent, routes_wide], axis=1)
    width = message.shape[1]
    by_chip = over_chips(message)
    by_core = over_cores(by_chip)
    own = by_core.reshape(group_rows, width)

    def own_column(table):
        return lax.dynamic_slice_in_dim(table, own_expert, 1, axis=1)

    def backward_rows(batch):
        rows = batch[:, :features]
        cot = batch[:, features : 2 * features]
        tables = gates_of(rows, batch[:, 2 * features : 2 * features + fanout], router)
        slot_gate = own_column(tables[3])
        gate_pre = jnp.dot(rows, w_gate, preferred_element_type=F32)
        up_pre = jnp.dot(rows, w_up, preferred_element_type=F32)
        sigma = jax.nn.sigmoid(gate_pre)
        silu = gate_pre * sigma
        hidden = silu * up_pre
        raw = jnp.dot(cot, w_down, preferred_element_type=F32)
        pull = jnp.sum(hidden * raw, axis=1)
        hidden_grad = slot_gate * raw
        gate_grad = (hidden_grad * up_pre * sigma * (1.0 + gate_pre * (1.0 - sigma))).astype(BF16)
        up_grad = (hidden_grad * silu).astype(BF16)
        gated = (slot_gate * hidden).astype(BF16)
        return rows, cot, tables, gate_grad, up_grad, gated, pull

    rows, cot, tables, gate_grad, up_grad, gated, pull = backward_rows(own)
    contract = (((1,), (1,)), ((), ()))
    mixed_part = lax.dot_general(gated, w_down, contract, preferred_element_type=F32)
    input_part = lax.dot_general(
        gate_grad, w_gate, contract, preferred_element_type=F32
    ) + lax.dot_general(up_grad, w_up, contract, preferred_element_type=F32)
    part = jnp.concatenate([mixed_part.astype(BF16), input_part.astype(BF16)], axis=1)
    part = part.reshape(2, chips, tok_count, 2 * features)
    keep = lax.dynamic_index_in_dim(part, core, 0, keepdims=False).astype(F32)
    send = lax.dynamic_index_in_dim(part, 1 - core, 0, keepdims=False)
    summed = (keep + swap(send, "expert", 1).astype(F32)).astype(BF16)
    total = lax.dynamic_index_in_dim(summed, chip, 0, keepdims=False).astype(F32)
    for m in range(1, chips):
        piece = lax.dynamic_index_in_dim(summed, chip ^ m, 0, keepdims=False)
        total = total + swap(piece, "expert", 2 * m).astype(F32)
    mixed = total[:, :features].astype(BF16)
    input_sum = total[:, features:]

    def logit_grads(pull, tables):
        picked, affinity, denominator, gates = tables
        pulls = over_cores(over_chips(pull))
        pulls = jnp.swapaxes(pulls, 0, 1).reshape(experts, sharing, -1)
        pulls = jnp.sum(pulls, axis=1).T
        mean_pull = jnp.sum(gates * pulls, axis=1, keepdims=True)
        grads = (pulls - mean_pull) / denominator * affinity * (1.0 - affinity)
        return jnp.where(picked, grads, 0.0)

    first = (((0,), (0,)), ((), ()))
    place = core * chips + chip
    if whole:
        by_group = jnp.zeros((groups,) + by_chip.shape, BF16)
        for m in range(groups):
            piece = by_chip if m == 0 else swap(by_chip, "dp", m)
            by_group = lax.dynamic_update_index_in_dim(by_group, piece, group ^ m, 0)
        batch = over_cores(by_group).reshape(-1, width)
        rows, cot, tables, gate_grad, up_grad, gated, pull = backward_rows(batch)
        portion = features // groups
        rows_cut = lax.dynamic_slice_in_dim(rows, group * portion, portion, axis=1)
        cot_cut = lax.dynamic_slice_in_dim(cot, group * portion, portion, axis=1)
        grad_gate, grad_up, grad_down = [
            lax.dot_general(left, right, first, preferred_element_type=F32)
            for left, right in ((rows_cut, gate_grad), (rows_cut, up_grad), (cot_cut, gated))
        ]
        logit_grad = logit_grads(pull, tables)
        grad_router = exact_dot(rows, logit_grad, first)
        place = (core * groups + group) * chips + chip
    else:
        logit_grad = logit_grads(pull, tables)
        own_logit = lax.dynamic_slice_in_dim(logit_grad, place * tok_count, tok_count, axis=0)
        grad_router = lax.psum(exact_dot(tokens, own_logit, first), ("dp", "expert"))
        parts = [
            lax.dot_general(left, right, first, preferred_element_type=F32)
            for left, right in ((rows, gate_grad), (rows, up_grad), (cot, gated))
        ]
        summed = lax.psum_scatter(
            jnp.concatenate(parts, axis=1).astype(BF16), "dp", scatter_dimension=0, tiled=True
        ).astype(F32)
        grad_gate, grad_up, grad_down = jnp.split(summed, 3, axis=1)
    own_logit = lax.dynamic_slice_in_dim(logit_grad, place * tok_count, tok_count, axis=0)
    router_back = lax.dot_general(
        own_logit, router, (((1,), (1,)), ((), ())), precision=lax.Precision.HIGHEST
    )
    grad_tokens = (input_sum + router_back).astype(BF16)
    return (mixed, grad_tokens, grad_router, grad_gate, grad_up, grad_down)


def solution(mesh):
    return jax.shard_map(
        local,
        mesh=mesh,
        in_specs=(
            P(("dp", "expert"), None),
            P(("dp", "expert"), None),
            P(),
            P(None, "expert"),
            P(None, "expert"),
            P(None, "expert"),
            P(("dp", "expert"), None),
        ),
        out_specs=(
            P(("dp", "expert"), None),
            P(("dp", "expert"), None),
            P(),
            P("dp", "expert"),
            P("dp", "expert"),
            P("dp", "expert"),
        ),
        check_vma=False,
    )
```

```python
import jax
import jax.numpy as jnp
from jax import lax
from jax.experimental import pallas as pl
from jax.experimental.pallas import tpu as pltpu
from jax.sharding import PartitionSpec as P

F32 = jnp.float32
BF16 = jnp.bfloat16
LANES = 128
STEP = 256
GATHER_BYTES = 8 << 20
VMEM_LIMIT = 24 << 20
HIGHEST = lax.Precision.HIGHEST
LAST = (((1,), (1,)), ((), ()))
FIRST = (((0,), (0,)), ((), ()))
IN_VMEM = pl.BlockSpec(memory_space=pltpu.VMEM)
IN_SMEM = pl.BlockSpec(memory_space=pltpu.SMEM)


def dot(left, right, contract=(((1,), (0,)), ((), ()))):
    return lax.dot_general(left, right, contract, preferred_element_type=F32)


def swap(x, axis, mask):
    count = lax.axis_size(axis)
    return lax.ppermute(x, axis, [(i, i ^ mask) for i in range(count)])


def three_parts(x):
    parts = []
    for _ in range(3):
        part = lax.reduce_precision(x, 8, 7)
        parts.append(part.astype(BF16))
        x = x - part
    return parts


def exact_dot(left, right, contract):
    return sum(dot(left, part, contract) for part in three_parts(right)[::-1])


def gates_of(rows, chosen, router):
    logits = exact_dot(rows, router, (((1,), (0,)), ((), ())))
    picked = chosen > 0.5
    affinity = jnp.where(picked, jax.nn.sigmoid(logits), 0.0)
    denominator = jnp.sum(affinity, axis=1, keepdims=True)
    return picked, affinity, denominator, affinity / denominator


def place_rows(x_ref, core, mine_ref, theirs_ref):
    half = mine_ref.shape[0]
    x_ref[pl.ds(pl.multiple_of(core * half, half), half), :] = mine_ref[...]
    x_ref[pl.ds(pl.multiple_of((1 - core) * half, half), half), :] = theirs_ref[...]


def gate_tables(x_ref, parts_ref, features, experts):
    logits = dot(parts_ref[...], x_ref[:, :features], LAST)
    logits = logits[2 * experts :] + logits[experts : 2 * experts] + logits[:experts]
    unit = lax.broadcasted_iota(jnp.int32, (experts, LANES), 0) == lax.broadcasted_iota(
        jnp.int32, (experts, LANES), 1
    )
    picked = dot(unit.astype(BF16), x_ref[:, 2 * features :], LAST) > 0.5
    affinity = jnp.where(picked, 1.0 / (1.0 + jnp.exp(-logits)), 0.0)
    denominator = jnp.sum(affinity, axis=0, keepdims=True)
    return affinity, denominator, affinity / denominator


def slot_gates(gates, expert):
    own = lax.broadcasted_iota(jnp.int32, (gates.shape[0], LANES), 0) == expert
    return lax.dot_general(
        gates, own.astype(F32), FIRST, precision=HIGHEST, preferred_element_type=F32
    )


def hidden_step(start, x_ref, slot_gate, w_gate_ref, w_up_ref, w_down_ref, grads, pull_ref):
    features = w_gate_ref.shape[0]
    at = pl.ds(pl.multiple_of(start, STEP), STEP)
    gate_pre = dot(x_ref[:, :features], w_gate_ref[:, at])
    up_pre = dot(x_ref[:, :features], w_up_ref[:, at])
    raw = dot(x_ref[:, features : 2 * features], w_down_ref[:, at])
    sigma = 1.0 / (1.0 + jnp.exp(-gate_pre))
    silu = gate_pre * sigma
    hidden = silu * up_pre
    slot = jnp.tile(slot_gate, (1, STEP // LANES))
    hidden_grad = slot * raw
    gate_grad_ref, up_grad_ref, gated_ref = grads
    gate_grad = hidden_grad * up_pre * sigma * (1.0 + gate_pre * (1.0 - sigma))
    gate_grad_ref[:, at] = gate_grad.astype(BF16)
    up_grad_ref[:, at] = (hidden_grad * silu).astype(BF16)
    gated_ref[:, at] = (slot * hidden).astype(BF16)
    if pull_ref is not None:
        pulled = hidden * raw
        for lane in range(0, STEP, LANES):
            pull_ref[...] += pulled[:, lane : lane + LANES]


def own_kernel(
    at_ref, mine_ref, theirs_ref, parts_ref, w_gate_ref, w_up_ref, w_down_ref,
    keep_ref, send_ref, x_ref, gate_grad_ref, up_grad_ref, gated_ref, back_ref,
):
    features, hidden_units = w_gate_ref.shape
    experts = parts_ref.shape[0] // 3
    core = at_ref[0]
    place_rows(x_ref, core, mine_ref, theirs_ref)
    gates = gate_tables(x_ref, parts_ref, features, experts)[2]
    slot_gate = slot_gates(gates, at_ref[1])
    grads = (gate_grad_ref, up_grad_ref, gated_ref)

    @pl.loop(0, hidden_units // STEP)
    def _(i):
        hidden_step(
            i * STEP, x_ref, slot_gate, w_gate_ref, w_up_ref, w_down_ref, grads, None
        )

    @pl.loop(0, features // STEP)
    def _(i):
        at = pl.ds(pl.multiple_of(i * STEP, STEP), STEP)
        later = pl.ds(pl.multiple_of(features + i * STEP, STEP), STEP)
        back_ref[:, at] = dot(gated_ref[...], w_down_ref[at, :], LAST).astype(BF16)
        back = dot(gate_grad_ref[...], w_gate_ref[at, :], LAST)
        back_ref[:, later] = (back + dot(up_grad_ref[...], w_up_ref[at, :], LAST)).astype(BF16)

    half = keep_ref.shape[0]
    keep_ref[...] = back_ref[pl.ds(pl.multiple_of(core * half, half), half), :]
    send_ref[...] = back_ref[pl.ds(pl.multiple_of((1 - core) * half, half), half), :]


def all_kernel(
    at_ref, mine_ref, theirs_ref, parts_ref, w_gate_ref, w_up_ref, w_down_ref,
    x_ref, gate_grad_ref, up_grad_ref, gated_ref, pull_ref, table_ref, sums_ref,
):
    features, hidden_units = w_gate_ref.shape
    experts = parts_ref.shape[0] // 3
    place_rows(x_ref, at_ref[0], mine_ref, theirs_ref)
    affinity, denominator, gates = gate_tables(x_ref, parts_ref, features, experts)
    table_ref[0] = affinity
    table_ref[1] = gates
    table_ref[2] = jnp.broadcast_to(denominator, affinity.shape)
    slot_gate = slot_gates(gates, at_ref[1])
    sums_ref[...] = jnp.zeros_like(sums_ref)
    grads = (gate_grad_ref, up_grad_ref, gated_ref)

    @pl.loop(0, hidden_units // STEP)
    def _(i):
        hidden_step(
            i * STEP, x_ref, slot_gate, w_gate_ref, w_up_ref, w_down_ref, grads, sums_ref
        )

    ones = jnp.ones((pull_ref.shape[0], LANES), F32)
    pull_ref[...] = lax.dot_general(
        ones, sums_ref[...], LAST, precision=HIGHEST, preferred_element_type=F32
    )


def weight_kernel(
    at_ref, x_ref, gate_grad_ref, up_grad_ref, gated_ref, gate_ref, up_ref, down_ref,
    gate_out, up_out, down_out, sems,
):
    features = (x_ref.shape[1] - LANES) // 2
    portion = gate_ref.shape[0]
    first = at_ref[2] * portion
    copies = []
    for k, row in enumerate(range(0, portion, LANES)):
        at = pl.ds(pl.multiple_of(first + row, LANES), LANES)
        later = pl.ds(pl.multiple_of(features + first + row, LANES), LANES)
        rows, cot = x_ref[:, at].T, x_ref[:, later].T
        here = pl.ds(row, LANES)
        for j, (left, right, out, target) in enumerate(
            (
                (rows, gate_grad_ref, gate_out, gate_ref),
                (rows, up_grad_ref, up_out, up_ref),
                (cot, gated_ref, down_out, down_ref),
            )
        ):
            out[here, :] = dot(left, right[...])
            copy = pltpu.make_async_copy(out.at[here, :], target.at[here, :], sems.at[k, j])
            copy.start()
            copies.append(copy)
    for copy in copies:
        copy.wait()


def last_kernel(
    at_ref, x_ref, table_ref, pulls_ref, router_ref, back_refs,
    mixed_ref, tokens_ref, router_grad_ref,
):
    experts, features = router_ref.shape
    affinity, gates, denominator = table_ref[0], table_ref[1], table_ref[2]
    pulls = pulls_ref[...]
    mean_pull = jnp.sum(gates * pulls, axis=0, keepdims=True)
    grads = (pulls - mean_pull) / denominator * affinity * (1.0 - affinity)
    rest, parts = grads, []
    for _ in range(3):
        parts.append(rest.astype(BF16).astype(F32))
        rest = rest - parts[-1]
    stacked = jnp.concatenate(parts, axis=0).astype(BF16)
    total = dot(stacked, x_ref[:, :features])
    router_grad_ref[...] = (
        total[2 * experts :] + total[experts : 2 * experts] + total[:experts]
    )
    count = mixed_ref.shape[0]
    shape = (count, pulls.shape[1])
    row = lax.broadcasted_iota(jnp.int32, shape, 0) + at_ref[3] * count
    own = (lax.broadcasted_iota(jnp.int32, shape, 1) == row).astype(F32)
    own_grads = lax.dot_general(own, grads, LAST, precision=HIGHEST, preferred_element_type=F32)
    back = jnp.dot(own_grads, router_ref[...], precision=HIGHEST, preferred_element_type=F32)
    summed = sum(ref[...].astype(F32) for ref in back_refs)
    mixed_ref[...] = summed[:, :features].astype(BF16)
    tokens_ref[...] = (summed[:, features:] + back).astype(BF16)


def call(kernel, out_shape, in_specs, out_specs, scratch, flops, moved):
    return pl.pallas_call(
        kernel,
        out_shape=out_shape,
        in_specs=in_specs,
        out_specs=out_specs,
        scratch_shapes=scratch,
        compiler_params=pltpu.CompilerParams(vmem_limit_bytes=VMEM_LIMIT),
        cost_estimate=pl.CostEstimate(flops=flops, bytes_accessed=moved, transcendentals=0),
    )


def local(tokens, routes, router, w_gate, w_up, w_down, cotangent):
    tok_count, features = tokens.shape
    experts = router.shape[1]
    hidden_units = w_gate.shape[1]
    devices = lax.axis_size("expert")
    groups = lax.axis_size("dp")
    sharing = devices // experts
    chips = devices // 2
    group_rows = devices * tok_count
    me = lax.axis_index("expert")
    group = lax.axis_index("dp")
    core, chip = me % 2, me // 2
    own_expert = me // sharing
    whole = groups * group_rows * features * 4 <= GATHER_BYTES

    def over_chips(x):
        out = jnp.zeros((chips,) + x.shape, x.dtype)
        for m in range(chips):
            piece = x if m == 0 else swap(x, "expert", 2 * m)
            out = lax.dynamic_update_index_in_dim(out, piece, chip ^ m, 0)
        return out

    def over_cores(x):
        other = swap(x, "expert", 1)
        return jnp.where(core == 0, jnp.stack([x, other]), jnp.stack([other, x]))

    ids = jnp.arange(LANES, dtype=jnp.int32)
    picked_wide = jnp.any(routes[:, :, None] == ids[None, None, :], axis=1).astype(BF16)
    message = jnp.concatenate([tokens, cotangent, picked_wide], axis=1)
    width = message.shape[1]
    by_chip = over_chips(message)
    if whole:
        return kernels_plan(
            by_chip, router, w_gate, w_up, w_down, over_chips, over_cores,
            groups, chips, tok_count, core, chip, group, own_expert,
        )

    own = over_cores(by_chip).reshape(group_rows, width)
    rows, cot = own[:, :features], own[:, features : 2 * features]
    picked, affinity, denominator, gates = gates_of(
        rows, own[:, 2 * features : 2 * features + experts], router
    )
    slot_gate = lax.dynamic_slice_in_dim(gates, own_expert, 1, axis=1)
    gate_pre = dot(rows, w_gate)
    up_pre = dot(rows, w_up)
    sigma = jax.nn.sigmoid(gate_pre)
    silu = gate_pre * sigma
    hidden = silu * up_pre
    raw = dot(cot, w_down)
    pull = jnp.sum(hidden * raw, axis=1)
    hidden_grad = slot_gate * raw
    gate_grad = (hidden_grad * up_pre * sigma * (1.0 + gate_pre * (1.0 - sigma))).astype(BF16)
    up_grad = (hidden_grad * silu).astype(BF16)
    gated = (slot_gate * hidden).astype(BF16)
    mixed_part = dot(gated, w_down, LAST)
    input_part = dot(gate_grad, w_gate, LAST) + dot(up_grad, w_up, LAST)
    part = jnp.concatenate([mixed_part.astype(BF16), input_part.astype(BF16)], axis=1)
    part = part.reshape(2, chips, tok_count, 2 * features)
    keep = lax.dynamic_index_in_dim(part, core, 0, keepdims=False)
    send = lax.dynamic_index_in_dim(part, 1 - core, 0, keepdims=False)
    total = sum(x.astype(F32) for x in give_back(keep, send, chips, chip))
    pulls = over_cores(over_chips(pull))
    pulls = jnp.swapaxes(pulls, 0, 1).reshape(experts, sharing, -1)
    pulls = jnp.sum(pulls, axis=1).T
    mean_pull = jnp.sum(gates * pulls, axis=1, keepdims=True)
    logit_grad = (pulls - mean_pull) / denominator * affinity * (1.0 - affinity)
    logit_grad = jnp.where(picked, logit_grad, 0.0)
    place = core * chips + chip
    own_logit = lax.dynamic_slice_in_dim(logit_grad, place * tok_count, tok_count, axis=0)
    grad_router = lax.psum(exact_dot(tokens, own_logit, FIRST), ("dp", "expert"))
    router_back = lax.dot_general(own_logit, router, LAST, precision=HIGHEST)
    parts = [
        dot(left, right, FIRST)
        for left, right in ((rows, gate_grad), (rows, up_grad), (cot, gated))
    ]
    summed = lax.psum_scatter(
        jnp.concatenate(parts, axis=1).astype(BF16), "dp", scatter_dimension=0, tiled=True
    ).astype(F32)
    grad_gate, grad_up, grad_down = jnp.split(summed, 3, axis=1)
    mixed = total[:, :features].astype(BF16)
    grad_tokens = (total[:, features:] + router_back).astype(BF16)
    return (mixed, grad_tokens, grad_router, grad_gate, grad_up, grad_down)


def give_back(keep, send, chips, chip):
    summed = (keep.astype(F32) + swap(send, "expert", 1).astype(F32)).astype(BF16)
    total = [lax.dynamic_index_in_dim(summed, chip, 0, keepdims=False)]
    for m in range(1, chips):
        piece = lax.dynamic_index_in_dim(summed, chip ^ m, 0, keepdims=False)
        total.append(swap(piece, "expert", 2 * m))
    return total


def kernels_plan(
    by_chip, router, w_gate, w_up, w_down, over_chips, over_cores,
    groups, chips, tok_count, core, chip, group, own_expert,
):
    features, experts = router.shape
    hidden_units = w_gate.shape[1]
    width = by_chip.shape[-1]
    half = chips * tok_count
    group_rows = 2 * half
    count = groups * group_rows
    portion = features // groups
    place = (core * groups + group) * chips + chip
    at = jnp.stack([core, own_expert, group, place]).astype(jnp.int32)
    router_t = router.T
    parts = jnp.concatenate(three_parts(router_t), axis=0)
    weights = [
        pltpu.with_memory_space_constraint(w, pltpu.VMEM) for w in (w_gate, w_up, w_down)
    ]
    grad_scratch = [pltpu.VMEM((group_rows, hidden_units), BF16)] * 3
    matrix = 2 * features * hidden_units

    theirs = swap(by_chip, "expert", 1)
    keep, send = call(
        own_kernel,
        [jax.ShapeDtypeStruct((half, 2 * features), BF16)] * 2,
        [IN_SMEM] + [IN_VMEM] * 6,
        [IN_VMEM] * 2,
        [pltpu.VMEM((group_rows, width), BF16)]
        + grad_scratch
        + [pltpu.VMEM((group_rows, 2 * features), BF16)],
        6 * matrix * group_rows,
        6 * matrix,
    )(at, by_chip.reshape(half, width), theirs.reshape(half, width), parts, *weights)
    by_group = jnp.zeros((groups,) + by_chip.shape, BF16)
    for m in range(groups):
        piece = by_chip if m == 0 else swap(by_chip, "dp", m)
        by_group = lax.dynamic_update_index_in_dim(by_group, piece, group ^ m, 0)
    theirs = swap(by_group, "expert", 1)
    back = give_back(
        keep.reshape(chips, tok_count, -1), send.reshape(chips, tok_count, -1), chips, chip
    )

    grads = [pltpu.VMEM((count, hidden_units), BF16)] * 3
    x, gate_grad, up_grad, gated, pull, tables = call(
        all_kernel,
        [pltpu.VMEM((count, width), BF16)]
        + grads
        + [
            jax.ShapeDtypeStruct((8, count), F32),
            pltpu.VMEM((3, experts, count), F32),
        ],
        [IN_SMEM] + [IN_VMEM] * 6,
        [IN_VMEM] * 6,
        [pltpu.VMEM((count, LANES), F32)],
        3 * matrix * count,
        3 * matrix,
    )(at, by_group.reshape(groups * half, width), theirs.reshape(groups * half, width), parts, *weights)
    pulls = over_cores(over_chips(pull[0]))
    pulls = jnp.swapaxes(pulls, 0, 1).reshape(experts, count)
    blocks = portion // LANES
    result = jax.ShapeDtypeStruct((portion, hidden_units), F32)
    grad_gate, grad_up, grad_down = call(
        weight_kernel,
        [result] * 3,
        [IN_SMEM] + [IN_VMEM] * 4,
        [pl.BlockSpec(memory_space=pl.ANY)] * 3,
        [pltpu.VMEM((portion, hidden_units), F32)] * 3 + [pltpu.SemaphoreType.DMA((blocks, 3))],
        6 * portion * hidden_units * count,
        12 * portion * hidden_units,
    )(at, x, gate_grad, up_grad, gated)
    rows = jax.ShapeDtypeStruct((tok_count, features), BF16)
    mixed, grad_tokens, router_grad = call(
        last_kernel,
        [rows, rows, jax.ShapeDtypeStruct((experts, features), F32)],
        [IN_SMEM] + [IN_VMEM] * 4 + [[IN_VMEM] * chips],
        [IN_VMEM] * 3,
        [],
        6 * experts * features * count,
        2 * features * count,
    )(at, x, tables, pulls, router_t, back)
    return (mixed, grad_tokens, router_grad.T, grad_gate, grad_up, grad_down)


def solution(mesh):
    return jax.shard_map(
        local,
        mesh=mesh,
        in_specs=(
            P(("dp", "expert"), None),
            P(("dp", "expert"), None),
            P(),
            P(None, "expert"),
            P(None, "expert"),
            P(None, "expert"),
            P(("dp", "expert"), None),
        ),
        out_specs=(
            P(("dp", "expert"), None),
            P(("dp", "expert"), None),
            P(),
            P("dp", "expert"),
            P("dp", "expert"),
            P("dp", "expert"),
        ),
        check_vma=False,
    )
```

```python
import jax
import jax.numpy as jnp
from jax import lax
from jax.experimental import pallas as pl
from jax.experimental.pallas import tpu as pltpu
from jax.sharding import PartitionSpec as P

F32 = jnp.float32
BF16 = jnp.bfloat16
LANES = 128
STEP = 256
GATHER_BYTES = 8 << 20
HIGHEST = lax.Precision.HIGHEST
LAST = (((1,), (1,)), ((), ()))
FIRST = (((0,), (0,)), ((), ()))
IN_VMEM = pl.BlockSpec(memory_space=pltpu.VMEM)
IN_SMEM = pl.BlockSpec(memory_space=pltpu.SMEM)


def dot(left, right, contract=(((1,), (0,)), ((), ()))):
    return lax.dot_general(left, right, contract, preferred_element_type=F32)


def swap(x, axis, mask):
    count = lax.axis_size(axis)
    return lax.ppermute(x, axis, [(i, i ^ mask) for i in range(count)])


def in_hbm(x):
    return pltpu.with_memory_space_constraint(x, pltpu.HBM)


def three_parts(x):
    parts = []
    for _ in range(3):
        part = lax.reduce_precision(x, 8, 7)
        parts.append(part.astype(BF16))
        x = x - part
    return parts


def exact_dot(left, right, contract):
    return sum(dot(left, part, contract) for part in three_parts(right)[::-1])


def gates_of(rows, chosen, router):
    logits = exact_dot(rows, router, (((1,), (0,)), ((), ())))
    picked = chosen > 0.5
    affinity = jnp.where(picked, jax.nn.sigmoid(logits), 0.0)
    denominator = jnp.sum(affinity, axis=1, keepdims=True)
    return picked, affinity, denominator, affinity / denominator


def place_rows(x_ref, core, mine_ref, theirs_ref):
    half = mine_ref.shape[0]
    x_ref[pl.ds(pl.multiple_of(core * half, half), half), :] = mine_ref[...]
    x_ref[pl.ds(pl.multiple_of((1 - core) * half, half), half), :] = theirs_ref[...]


def gate_tables(x_ref, parts_ref, features, experts):
    logits = dot(parts_ref[...], x_ref[:, :features], LAST)
    logits = logits[2 * experts :] + logits[experts : 2 * experts] + logits[:experts]
    unit = lax.broadcasted_iota(jnp.int32, (experts, LANES), 0) == lax.broadcasted_iota(
        jnp.int32, (experts, LANES), 1
    )
    picked = dot(unit.astype(BF16), x_ref[:, 2 * features :], LAST) > 0.5
    affinity = jnp.where(picked, 1.0 / (1.0 + jnp.exp(-logits)), 0.0)
    denominator = jnp.sum(affinity, axis=0, keepdims=True)
    return affinity, denominator, affinity / denominator


def slot_gates(gates, expert):
    own = lax.broadcasted_iota(jnp.int32, (gates.shape[0], LANES), 0) == expert
    return lax.dot_general(
        gates, own.astype(F32), FIRST, precision=HIGHEST, preferred_element_type=F32
    )


def hidden_step(start, x_ref, slot_gate, w_gate_ref, w_up_ref, w_down_ref, grads, pull_ref):
    features = w_gate_ref.shape[0]
    at = pl.ds(pl.multiple_of(start, STEP), STEP)
    gate_pre = dot(x_ref[:, :features], w_gate_ref[:, at])
    up_pre = dot(x_ref[:, :features], w_up_ref[:, at])
    raw = dot(x_ref[:, features : 2 * features], w_down_ref[:, at])
    sigma = 1.0 / (1.0 + jnp.exp(-gate_pre))
    silu = gate_pre * sigma
    hidden = silu * up_pre
    slot = jnp.tile(slot_gate, (1, STEP // LANES))
    hidden_grad = slot * raw
    gate_grad_ref, up_grad_ref, gated_ref = grads
    gate_grad = hidden_grad * up_pre * sigma * (1.0 + gate_pre * (1.0 - sigma))
    gate_grad_ref[:, at] = gate_grad.astype(BF16)
    up_grad_ref[:, at] = (hidden_grad * silu).astype(BF16)
    gated_ref[:, at] = (slot * hidden).astype(BF16)
    if pull_ref is not None:
        pulled = hidden * raw
        for lane in range(0, STEP, LANES):
            pull_ref[...] += pulled[:, lane : lane + LANES]


def load_kernel(_, *refs):
    count = len(refs) // 2
    copies = [
        pltpu.make_async_copy(refs[i], refs[count + i], refs[-1].at[i]) for i in range(count)
    ]
    for copy in copies:
        copy.start()
    for copy in copies:
        copy.wait()


def own_kernel(
    at_ref, mine_ref, theirs_ref, parts_ref, w_gate_ref, w_up_ref, w_down_ref,
    keep_ref, send_ref, x_ref, gate_grad_ref, up_grad_ref, gated_ref, back_ref,
):
    features, hidden_units = w_gate_ref.shape
    experts = parts_ref.shape[0] // 3
    core = at_ref[0]
    place_rows(x_ref, core, mine_ref, theirs_ref)
    gates = gate_tables(x_ref, parts_ref, features, experts)[2]
    slot_gate = slot_gates(gates, at_ref[1])
    grads = (gate_grad_ref, up_grad_ref, gated_ref)

    @pl.loop(0, hidden_units // STEP)
    def _(i):
        hidden_step(
            i * STEP, x_ref, slot_gate, w_gate_ref, w_up_ref, w_down_ref, grads, None
        )

    @pl.loop(0, features // STEP)
    def _(i):
        at = pl.ds(pl.multiple_of(i * STEP, STEP), STEP)
        later = pl.ds(pl.multiple_of(features + i * STEP, STEP), STEP)
        back_ref[:, at] = dot(gated_ref[...], w_down_ref[at, :], LAST).astype(BF16)
        back = dot(gate_grad_ref[...], w_gate_ref[at, :], LAST)
        back_ref[:, later] = (back + dot(up_grad_ref[...], w_up_ref[at, :], LAST)).astype(BF16)

    half = keep_ref.shape[0]
    keep_ref[...] = back_ref[pl.ds(pl.multiple_of(core * half, half), half), :]
    send_ref[...] = back_ref[pl.ds(pl.multiple_of((1 - core) * half, half), half), :]


def all_kernel(
    at_ref, mine_ref, theirs_ref, parts_ref, w_gate_ref, w_up_ref, w_down_ref,
    x_ref, gate_grad_ref, up_grad_ref, gated_ref, pull_ref, table_ref, sums_ref,
):
    features, hidden_units = w_gate_ref.shape
    experts = parts_ref.shape[0] // 3
    place_rows(x_ref, at_ref[0], mine_ref, theirs_ref)
    affinity, denominator, gates = gate_tables(x_ref, parts_ref, features, experts)
    table_ref[0] = affinity
    table_ref[1] = gates
    table_ref[2] = jnp.broadcast_to(denominator, affinity.shape)
    slot_gate = slot_gates(gates, at_ref[1])
    sums_ref[...] = jnp.zeros_like(sums_ref)
    grads = (gate_grad_ref, up_grad_ref, gated_ref)

    @pl.loop(0, hidden_units // STEP)
    def _(i):
        hidden_step(
            i * STEP, x_ref, slot_gate, w_gate_ref, w_up_ref, w_down_ref, grads, sums_ref
        )

    ones = jnp.ones((pull_ref.shape[0], LANES), F32)
    pull_ref[...] = lax.dot_general(
        ones, sums_ref[...], LAST, precision=HIGHEST, preferred_element_type=F32
    )


def weight_kernel(
    at_ref, x_ref, gate_grad_ref, up_grad_ref, gated_ref, _, gate_ref, up_ref, down_ref,
    gate_out, up_out, down_out, sems,
):
    features = (x_ref.shape[1] - LANES) // 2
    portion = gate_ref.shape[0]
    first = at_ref[2] * portion
    copies = []
    for k, row in enumerate(range(0, portion, LANES)):
        at = pl.ds(pl.multiple_of(first + row, LANES), LANES)
        later = pl.ds(pl.multiple_of(features + first + row, LANES), LANES)
        rows, cot = x_ref[:, at].T, x_ref[:, later].T
        here = pl.ds(row, LANES)
        for j, (left, right, out, target) in enumerate(
            (
                (rows, gate_grad_ref, gate_out, gate_ref),
                (rows, up_grad_ref, up_out, up_ref),
                (cot, gated_ref, down_out, down_ref),
            )
        ):
            out[here, :] = dot(left, right[...])
            copy = pltpu.make_async_copy(out.at[here, :], target.at[here, :], sems.at[k, j])
            copy.start()
            copies.append(copy)
    for copy in copies:
        copy.wait()


def last_kernel(
    at_ref, x_ref, table_ref, pulls_ref, router_ref, back_refs,
    mixed_ref, tokens_ref, router_grad_ref,
):
    experts, features = router_ref.shape
    affinity, gates, denominator = table_ref[0], table_ref[1], table_ref[2]
    pulls = pulls_ref[...]
    mean_pull = jnp.sum(gates * pulls, axis=0, keepdims=True)
    grads = (pulls - mean_pull) / denominator * affinity * (1.0 - affinity)
    rest, parts = grads, []
    for _ in range(3):
        parts.append(rest.astype(BF16).astype(F32))
        rest = rest - parts[-1]
    stacked = jnp.concatenate(parts, axis=0).astype(BF16)
    total = dot(stacked, x_ref[:, :features])
    router_grad_ref[...] = (
        total[2 * experts :] + total[experts : 2 * experts] + total[:experts]
    )
    count = mixed_ref.shape[0]
    shape = (count, pulls.shape[1])
    row = lax.broadcasted_iota(jnp.int32, shape, 0) + at_ref[3] * count
    own = (lax.broadcasted_iota(jnp.int32, shape, 1) == row).astype(F32)
    own_grads = lax.dot_general(own, grads, LAST, precision=HIGHEST, preferred_element_type=F32)
    back = jnp.dot(own_grads, router_ref[...], precision=HIGHEST, preferred_element_type=F32)
    summed = sum(ref[...].astype(F32) for ref in back_refs)
    mixed_ref[...] = summed[:, :features].astype(BF16)
    tokens_ref[...] = (summed[:, features:] + back).astype(BF16)


def call(kernel, out_shape, in_specs, out_specs, scratch, limit, flops, moved):
    return pl.pallas_call(
        kernel,
        out_shape=out_shape,
        in_specs=in_specs,
        out_specs=out_specs,
        scratch_shapes=scratch,
        compiler_params=pltpu.CompilerParams(vmem_limit_bytes=limit << 20),
        cost_estimate=pl.CostEstimate(flops=flops, bytes_accessed=moved, transcendentals=0),
    )


def local(tokens, routes, router, w_gate, w_up, w_down, cotangent):
    tok_count, features = tokens.shape
    experts = router.shape[1]
    hidden_units = w_gate.shape[1]
    devices = lax.axis_size("expert")
    groups = lax.axis_size("dp")
    sharing = devices // experts
    chips = devices // 2
    group_rows = devices * tok_count
    me = lax.axis_index("expert")
    group = lax.axis_index("dp")
    core, chip = me % 2, me // 2
    own_expert = me // sharing
    whole = groups * group_rows * features * 4 <= GATHER_BYTES

    def over_chips(x):
        out = jnp.zeros((chips,) + x.shape, x.dtype)
        for m in range(chips):
            piece = x if m == 0 else swap(x, "expert", 2 * m)
            out = lax.dynamic_update_index_in_dim(out, piece, chip ^ m, 0)
        return out

    def over_cores(x):
        other = swap(x, "expert", 1)
        return jnp.where(core == 0, jnp.stack([x, other]), jnp.stack([other, x]))

    ids = jnp.arange(LANES, dtype=jnp.int32)
    picked_wide = jnp.any(routes[:, :, None] == ids[None, None, :], axis=1).astype(BF16)
    message = jnp.concatenate([tokens, cotangent, picked_wide], axis=1)
    width = message.shape[1]
    by_chip = over_chips(message)
    if whole:
        return kernels_plan(
            message, by_chip, router, w_gate, w_up, w_down, over_chips, over_cores,
            groups, chips, tok_count, core, chip, group, own_expert,
        )

    own = over_cores(by_chip).reshape(group_rows, width)
    rows, cot = own[:, :features], own[:, features : 2 * features]
    picked, affinity, denominator, gates = gates_of(
        rows, own[:, 2 * features : 2 * features + experts], router
    )
    slot_gate = lax.dynamic_slice_in_dim(gates, own_expert, 1, axis=1)
    gate_pre = dot(rows, w_gate)
    up_pre = dot(rows, w_up)
    sigma = jax.nn.sigmoid(gate_pre)
    silu = gate_pre * sigma
    hidden = silu * up_pre
    raw = dot(cot, w_down)
    pull = jnp.sum(hidden * raw, axis=1)
    hidden_grad = slot_gate * raw
    gate_grad = (hidden_grad * up_pre * sigma * (1.0 + gate_pre * (1.0 - sigma))).astype(BF16)
    up_grad = (hidden_grad * silu).astype(BF16)
    gated = (slot_gate * hidden).astype(BF16)
    mixed_part = dot(gated, w_down, LAST)
    input_part = dot(gate_grad, w_gate, LAST) + dot(up_grad, w_up, LAST)
    part = jnp.concatenate([mixed_part.astype(BF16), input_part.astype(BF16)], axis=1)
    part = part.reshape(2, chips, tok_count, 2 * features)
    keep = lax.dynamic_index_in_dim(part, core, 0, keepdims=False)
    send = lax.dynamic_index_in_dim(part, 1 - core, 0, keepdims=False)
    back = give_back(send_back(keep, send, chips, chip))
    total = sum(x.astype(F32) for x in back)
    pulls = over_cores(over_chips(pull))
    pulls = jnp.swapaxes(pulls, 0, 1).reshape(experts, sharing, -1)
    pulls = jnp.sum(pulls, axis=1).T
    mean_pull = jnp.sum(gates * pulls, axis=1, keepdims=True)
    logit_grad = (pulls - mean_pull) / denominator * affinity * (1.0 - affinity)
    logit_grad = jnp.where(picked, logit_grad, 0.0)
    place = core * chips + chip
    own_logit = lax.dynamic_slice_in_dim(logit_grad, place * tok_count, tok_count, axis=0)
    grad_router = lax.psum(exact_dot(tokens, own_logit, FIRST), ("dp", "expert"))
    router_back = lax.dot_general(own_logit, router, LAST, precision=HIGHEST)
    parts = [
        dot(left, right, FIRST)
        for left, right in ((rows, gate_grad), (rows, up_grad), (cot, gated))
    ]
    summed = lax.psum_scatter(
        jnp.concatenate(parts, axis=1).astype(BF16), "dp", scatter_dimension=0, tiled=True
    ).astype(F32)
    grad_gate, grad_up, grad_down = jnp.split(summed, 3, axis=1)
    mixed = total[:, :features].astype(BF16)
    grad_tokens = (total[:, features:] + router_back).astype(BF16)
    return (mixed, grad_tokens, grad_router, grad_gate, grad_up, grad_down)


def send_back(keep, send, chips, chip):
    summed = (keep.astype(F32) + swap(send, "expert", 1).astype(F32)).astype(BF16)
    return [
        lax.dynamic_index_in_dim(summed, chip ^ m, 0, keepdims=False) for m in range(chips)
    ]


def give_back(pieces):
    return [
        piece if m == 0 else swap(piece, "expert", 2 * m) for m, piece in enumerate(pieces)
    ]


def kernels_plan(
    message, by_chip, router, w_gate, w_up, w_down, over_chips, over_cores,
    groups, chips, tok_count, core, chip, group, own_expert,
):
    features, experts = router.shape
    hidden_units = w_gate.shape[1]
    width = by_chip.shape[-1]
    half = chips * tok_count
    group_rows = 2 * half
    count = groups * group_rows
    portion = features // groups
    place = (core * groups + group) * chips + chip
    at = jnp.stack([core, own_expert, group, place]).astype(jnp.int32)
    router_t = router.T
    parts = jnp.concatenate(three_parts(router_t), axis=0)
    weights = call(
        load_kernel,
        [pltpu.VMEM(w.shape, w.dtype) for w in (w_gate, w_up, w_down)],
        [IN_VMEM] + [pl.BlockSpec(memory_space=pltpu.HBM)] * 3,
        [IN_VMEM] * 3,
        [pltpu.SemaphoreType.DMA((3,))],
        2,
        0,
        6 * features * hidden_units,
    )(message[:, 2 * features :], *[in_hbm(w) for w in (w_gate, w_up, w_down)])
    grad_scratch = [pltpu.VMEM((group_rows, hidden_units), BF16)] * 3
    matrix = 2 * features * hidden_units

    theirs = swap(by_chip, "expert", 1)
    keep, send = call(
        own_kernel,
        [jax.ShapeDtypeStruct((half, 2 * features), BF16)] * 2,
        [IN_SMEM] + [IN_VMEM] * 6,
        [IN_VMEM] * 2,
        [pltpu.VMEM((group_rows, width), BF16)]
        + grad_scratch
        + [pltpu.VMEM((group_rows, 2 * features), BF16)],
        8,
        6 * matrix * group_rows,
        6 * matrix,
    )(at, by_chip.reshape(half, width), theirs.reshape(half, width), parts, *weights)
    by_group = jnp.zeros((groups,) + by_chip.shape, BF16)
    for m in range(groups):
        piece = by_chip if m == 0 else swap(by_chip, "dp", m)
        by_group = lax.dynamic_update_index_in_dim(by_group, piece, group ^ m, 0)
    theirs = swap(by_group, "expert", 1)
    pieces = send_back(
        keep.reshape(chips, tok_count, -1), send.reshape(chips, tok_count, -1), chips, chip
    )
    back = give_back(pieces)

    grads = [pltpu.VMEM((count, hidden_units), BF16)] * 3
    x, gate_grad, up_grad, gated, pull, tables = call(
        all_kernel,
        [pltpu.VMEM((count, width), BF16)]
        + grads
        + [
            jax.ShapeDtypeStruct((8, count), F32),
            pltpu.VMEM((3, experts, count), F32),
        ],
        [IN_SMEM] + [IN_VMEM] * 6,
        [IN_VMEM] * 6,
        [pltpu.VMEM((count, LANES), F32)],
        8,
        3 * matrix * count,
        3 * matrix,
    )(
        at,
        by_group.reshape(groups * half, width),
        theirs.reshape(groups * half, width),
        parts,
        *weights,
    )
    pulls = over_cores(over_chips(pull[0]))
    pulls = jnp.swapaxes(pulls, 0, 1).reshape(experts, count)
    blocks = portion // LANES
    result = jax.ShapeDtypeStruct((portion, hidden_units), F32)
    grad_gate, grad_up, grad_down = call(
        weight_kernel,
        [result] * 3,
        [IN_SMEM] + [IN_VMEM] * 4 + [[pl.BlockSpec(memory_space=pl.ANY)] * (chips - 1)],
        [pl.BlockSpec(memory_space=pl.ANY)] * 3,
        [pltpu.VMEM((portion, hidden_units), F32)] * 3 + [pltpu.SemaphoreType.DMA((blocks, 3))],
        14,
        6 * portion * hidden_units * count,
        12 * portion * hidden_units,
    )(at, x, gate_grad, up_grad, gated, back[1:])
    rows = jax.ShapeDtypeStruct((tok_count, features), BF16)
    mixed, grad_tokens, router_grad = call(
        last_kernel,
        [rows, rows, jax.ShapeDtypeStruct((experts, features), F32)],
        [IN_SMEM] + [IN_VMEM] * 4 + [[IN_VMEM] * chips],
        [IN_VMEM] * 3,
        [],
        6,
        6 * experts * features * count,
        2 * features * count,
    )(at, x, tables, pulls, router_t, back)
    return (mixed, grad_tokens, router_grad.T, grad_gate, grad_up, grad_down)


def solution(mesh):
    return jax.shard_map(
        local,
        mesh=mesh,
        in_specs=(
            P(("dp", "expert"), None),
            P(("dp", "expert"), None),
            P(),
            P(None, "expert"),
            P(None, "expert"),
            P(None, "expert"),
            P(("dp", "expert"), None),
        ),
        out_specs=(
            P(("dp", "expert"), None),
            P(("dp", "expert"), None),
            P(),
            P("dp", "expert"),
            P("dp", "expert"),
            P("dp", "expert"),
        ),
        check_vma=False,
    )
```

```python
import jax
import jax.numpy as jnp
from jax import lax
from jax.experimental import pallas as pl
from jax.experimental.pallas import tpu as pltpu
from jax.sharding import PartitionSpec as P

F32 = jnp.float32
BF16 = jnp.bfloat16
LANES = 128
STEP = 256
GATHER_BYTES = 8 << 20
HIGHEST = lax.Precision.HIGHEST
LAST = (((1,), (1,)), ((), ()))
FIRST = (((0,), (0,)), ((), ()))
IN_VMEM = pl.BlockSpec(memory_space=pltpu.VMEM)
IN_SMEM = pl.BlockSpec(memory_space=pltpu.SMEM)


def dot(left, right, contract=(((1,), (0,)), ((), ()))):
    return lax.dot_general(left, right, contract, preferred_element_type=F32)


def swap(x, axis, mask):
    count = lax.axis_size(axis)
    return lax.ppermute(x, axis, [(i, i ^ mask) for i in range(count)])


def in_hbm(x):
    return pltpu.with_memory_space_constraint(x, pltpu.HBM)


def three_parts(x):
    parts = []
    for _ in range(3):
        part = lax.reduce_precision(x, 8, 7)
        parts.append(part.astype(BF16))
        x = x - part
    return parts


def exact_dot(left, right, contract):
    return sum(dot(left, part, contract) for part in three_parts(right)[::-1])


def gates_of(rows, chosen, router):
    logits = exact_dot(rows, router, (((1,), (0,)), ((), ())))
    picked = chosen > 0.5
    affinity = jnp.where(picked, jax.nn.sigmoid(logits), 0.0)
    denominator = jnp.sum(affinity, axis=1, keepdims=True)
    return picked, affinity, denominator, affinity / denominator


def place_rows(x_ref, first, core, mine_ref, theirs_ref):
    half = mine_ref.shape[0]
    x_ref[pl.ds(pl.multiple_of(first + core * half, half), half), :] = mine_ref[...]
    x_ref[pl.ds(pl.multiple_of(first + (1 - core) * half, half), half), :] = theirs_ref[...]


def gate_tables(x, parts_ref, experts):
    features = parts_ref.shape[1]
    logits = dot(parts_ref[...], x[:, :features], LAST)
    logits = logits[2 * experts :] + logits[experts : 2 * experts] + logits[:experts]
    unit = lax.broadcasted_iota(jnp.int32, (experts, LANES), 0) == lax.broadcasted_iota(
        jnp.int32, (experts, LANES), 1
    )
    picked = dot(unit.astype(BF16), x[:, 2 * features :], LAST) > 0.5
    affinity = jnp.where(picked, 1.0 / (1.0 + jnp.exp(-logits)), 0.0)
    denominator = jnp.sum(affinity, axis=0, keepdims=True)
    return affinity, denominator, affinity / denominator


def slot_gates(gates, expert):
    own = lax.broadcasted_iota(jnp.int32, (gates.shape[0], LANES), 0) == expert
    return lax.dot_general(
        gates, own.astype(F32), FIRST, precision=HIGHEST, preferred_element_type=F32
    )


def hidden_step(at, x, slot_gate, w_gate_ref, w_up_ref, w_down_ref):
    features = w_gate_ref.shape[0]
    gate_pre = dot(x[:, :features], w_gate_ref[:, at])
    up_pre = dot(x[:, :features], w_up_ref[:, at])
    raw = dot(x[:, features : 2 * features], w_down_ref[:, at])
    sigma = 1.0 / (1.0 + jnp.exp(-gate_pre))
    silu = gate_pre * sigma
    hidden = silu * up_pre
    slot = jnp.tile(slot_gate, (1, STEP // LANES))
    hidden_grad = slot * raw
    gate_grad = hidden_grad * up_pre * sigma * (1.0 + gate_pre * (1.0 - sigma))
    grads = (gate_grad, hidden_grad * silu, slot * hidden)
    return [grad.astype(BF16) for grad in grads], hidden * raw


def load_kernel(_, *refs):
    count = len(refs) // 2
    copies = [
        pltpu.make_async_copy(refs[i], refs[count + i], refs[-1].at[i]) for i in range(count)
    ]
    for copy in copies:
        copy.start()
    for copy in copies:
        copy.wait()


def order_kernel(at_ref, piece_refs, out_ref):
    for m, ref in enumerate(piece_refs):
        out_ref[at_ref[3] ^ m] = ref[...]


def own_kernel(
    at_ref, mine_ref, theirs_ref, parts_ref, w_gate_ref, w_up_ref, w_down_ref,
    keep_ref, send_ref, gate_grad_ref, up_grad_ref, gated_ref, pull_ref, table_ref,
    x_ref, back_ref,
):
    features, hidden_units = w_gate_ref.shape
    experts = parts_ref.shape[0] // 3
    core = at_ref[0]
    place_rows(x_ref, 0, core, mine_ref, theirs_ref)
    affinity, denominator, gates = gate_tables(x_ref, parts_ref, experts)
    table_ref[0] = affinity
    table_ref[1] = gates
    table_ref[2] = jnp.broadcast_to(denominator, affinity.shape)
    slot_gate = slot_gates(gates, at_ref[1])
    pulls = jnp.zeros(slot_gate.shape, F32)
    for start in range(0, hidden_units, STEP):
        at = pl.ds(start, STEP)
        grads, pulled = hidden_step(at, x_ref, slot_gate, w_gate_ref, w_up_ref, w_down_ref)
        gate_grad_ref[:, at], up_grad_ref[:, at], gated_ref[:, at] = grads
        pulls += sum(pulled[:, lane : lane + LANES] for lane in range(0, STEP, LANES))
    ones = jnp.ones((pull_ref.shape[0], LANES), F32)
    pull_ref[...] = lax.dot_general(
        ones, pulls, LAST, precision=HIGHEST, preferred_element_type=F32
    )
    for start in range(0, features, STEP):
        at = pl.ds(start, STEP)
        later = pl.ds(features + start, STEP)
        back_ref[:, at] = dot(gated_ref[...], w_down_ref[at, :], LAST).astype(BF16)
        back = dot(gate_grad_ref[...], w_gate_ref[at, :], LAST)
        back_ref[:, later] = (back + dot(up_grad_ref[...], w_up_ref[at, :], LAST)).astype(BF16)

    half = keep_ref.shape[0]
    keep_ref[...] = back_ref[pl.ds(pl.multiple_of(core * half, half), half), :]
    send_ref[...] = back_ref[pl.ds(pl.multiple_of((1 - core) * half, half), half), :]


def pair_kernel(at_ref, keep_ref, other_ref, pull_ref, other_pull_ref, pair_ref, out_refs):
    for m, ref in enumerate(out_refs):
        chip = at_ref[3] ^ m
        ref[...] = (keep_ref[chip].astype(F32) + other_ref[chip].astype(F32)).astype(BF16)
    row = lax.broadcasted_iota(jnp.int32, pull_ref.shape, 0)
    pair_ref[...] = jnp.where(row % 2 == at_ref[0], pull_ref[...], other_pull_ref[...])


def logit_kernel(at_ref, table_ref, pair_refs, out_ref):
    affinity, gates, denominator = table_ref[0], table_ref[1], table_ref[2]
    chip = lax.broadcasted_iota(jnp.int32, affinity.shape, 0) // 2
    pulls = jnp.zeros(affinity.shape, F32)
    for m, ref in enumerate(pair_refs):
        pulls = jnp.where(chip == at_ref[3] ^ m, ref[...], pulls)
    mean_pull = jnp.sum(gates * pulls, axis=0, keepdims=True)
    out_ref[...] = (pulls - mean_pull) / denominator * affinity * (1.0 - affinity)


def weight_kernel(
    at_ref, mine_refs, theirs_refs, parts_ref, w_gate_ref, w_up_ref, w_down_ref,
    own_refs, logit_refs, gate_ref, up_ref, down_ref, router_ref,
    x_ref, turned_ref, grad_refs, out_refs, sems,
):
    features, hidden_units = w_gate_ref.shape
    experts = parts_ref.shape[0] // 3
    portion = gate_ref.shape[0]
    group_rows = own_refs[0].shape[0]
    for m, (mine_ref, theirs_ref) in enumerate(zip(mine_refs, theirs_refs)):
        place_rows(x_ref, m * group_rows, at_ref[0], mine_ref, theirs_ref)
    first = at_ref[2] * portion
    for half in range(2):
        for row in range(0, portion, LANES):
            at = pl.ds(pl.multiple_of(half * features + first + row, LANES), LANES)
            turned_ref[half, row : row + LANES, :] = x_ref[:, at].T
    far = x_ref.at[group_rows:, :]
    slot_gate = slot_gates(gate_tables(far, parts_ref, experts)[2], at_ref[1])
    copies = []
    for step, start in enumerate(range(0, hidden_units, STEP)):
        at = pl.ds(start, STEP)
        grads, _ = hidden_step(at, far, slot_gate, w_gate_ref, w_up_ref, w_down_ref)
        targets = (gate_ref, up_ref, down_ref)
        for j, (own_ref, grad) in enumerate(zip(own_refs, grads)):
            grad_refs[j][:group_rows, at] = own_ref[:, at]
            grad_refs[j][group_rows:, at] = grad
            out_refs[j][:, at] = dot(turned_ref[j // 2], grad_refs[j][:, at])
            copy = pltpu.make_async_copy(
                out_refs[j].at[:, at], targets[j].at[:, at], sems.at[step, j]
            )
            copy.start()
            copies.append(copy)
    totals = []
    for m, ref in enumerate(logit_refs):
        rest, parts = ref[...], []
        for _ in range(3):
            parts.append(rest.astype(BF16).astype(F32))
            rest = rest - parts[-1]
        stacked = jnp.concatenate(parts, axis=0).astype(BF16)
        total = dot(stacked, x_ref[m * group_rows : (m + 1) * group_rows, :features])
        totals.append(total[2 * experts :] + total[experts : 2 * experts] + total[:experts])
    while len(totals) > 1:
        totals = [totals[i] + totals[i + 1] for i in range(0, len(totals), 2)]
    router_ref[...] = totals[0]
    for copy in copies:
        copy.wait()


def last_kernel(at_ref, logit_ref, router_ref, back_refs, mixed_ref, tokens_ref):
    features = router_ref.shape[1]
    count = mixed_ref.shape[0]
    chips = len(back_refs)
    grads = logit_ref[...]
    shape = (count, grads.shape[1])
    row = lax.broadcasted_iota(jnp.int32, shape, 0) + (at_ref[0] * chips + at_ref[3]) * count
    own = (lax.broadcasted_iota(jnp.int32, shape, 1) == row).astype(F32)
    own_grads = lax.dot_general(own, grads, LAST, precision=HIGHEST, preferred_element_type=F32)
    back = jnp.dot(own_grads, router_ref[...], precision=HIGHEST, preferred_element_type=F32)
    summed = sum(ref[...].astype(F32) for ref in back_refs)
    mixed_ref[...] = summed[:, :features].astype(BF16)
    tokens_ref[...] = (summed[:, features:] + back).astype(BF16)


def call(kernel, out_shape, in_specs, out_specs, scratch=(), limit=4, flops=0, moved=1 << 17):
    return pl.pallas_call(
        kernel,
        out_shape=out_shape,
        in_specs=in_specs,
        out_specs=out_specs,
        scratch_shapes=scratch,
        compiler_params=pltpu.CompilerParams(vmem_limit_bytes=limit << 20),
        cost_estimate=pl.CostEstimate(flops=flops, bytes_accessed=moved, transcendentals=0),
    )


def local(tokens, routes, router, w_gate, w_up, w_down, cotangent):
    tok_count, features = tokens.shape
    experts = router.shape[1]
    hidden_units = w_gate.shape[1]
    devices = lax.axis_size("expert")
    groups = lax.axis_size("dp")
    sharing = devices // experts
    chips = devices // 2
    group_rows = devices * tok_count
    me = lax.axis_index("expert")
    group = lax.axis_index("dp")
    core, chip = me % 2, me // 2
    own_expert = me // sharing
    whole = sharing == 1 and groups * group_rows * features * 4 <= GATHER_BYTES

    def over_chips(x):
        out = jnp.zeros((chips,) + x.shape, x.dtype)
        for m in range(chips):
            piece = x if m == 0 else swap(x, "expert", 2 * m)
            out = lax.dynamic_update_index_in_dim(out, piece, chip ^ m, 0)
        return out

    def over_cores(x):
        other = swap(x, "expert", 1)
        return jnp.where(core == 0, jnp.stack([x, other]), jnp.stack([other, x]))

    ids = jnp.arange(LANES, dtype=jnp.int32)
    picked_wide = jnp.any(routes[:, :, None] == ids[None, None, :], axis=1).astype(BF16)
    message = jnp.concatenate([tokens, cotangent, picked_wide], axis=1)
    width = message.shape[1]
    if whole:
        return kernels_plan(message, router, w_gate, w_up, w_down)

    by_chip = over_chips(message)
    own = over_cores(by_chip).reshape(group_rows, width)
    rows, cot = own[:, :features], own[:, features : 2 * features]
    picked, affinity, denominator, gates = gates_of(
        rows, own[:, 2 * features : 2 * features + experts], router
    )
    slot_gate = lax.dynamic_slice_in_dim(gates, own_expert, 1, axis=1)
    gate_pre = dot(rows, w_gate)
    up_pre = dot(rows, w_up)
    sigma = jax.nn.sigmoid(gate_pre)
    silu = gate_pre * sigma
    hidden = silu * up_pre
    raw = dot(cot, w_down)
    pull = jnp.sum(hidden * raw, axis=1)
    hidden_grad = slot_gate * raw
    gate_grad = (hidden_grad * up_pre * sigma * (1.0 + gate_pre * (1.0 - sigma))).astype(BF16)
    up_grad = (hidden_grad * silu).astype(BF16)
    gated = (slot_gate * hidden).astype(BF16)
    mixed_part = dot(gated, w_down, LAST)
    input_part = dot(gate_grad, w_gate, LAST) + dot(up_grad, w_up, LAST)
    part = jnp.concatenate([mixed_part.astype(BF16), input_part.astype(BF16)], axis=1)
    part = part.reshape(2, chips, tok_count, 2 * features)
    keep = lax.dynamic_index_in_dim(part, core, 0, keepdims=False)
    send = lax.dynamic_index_in_dim(part, 1 - core, 0, keepdims=False)
    back = give_back(send_back(keep, send, chips, chip))
    total = sum(x.astype(F32) for x in back)
    pulls = over_cores(over_chips(pull))
    pulls = jnp.swapaxes(pulls, 0, 1).reshape(experts, sharing, -1)
    pulls = jnp.sum(pulls, axis=1).T
    mean_pull = jnp.sum(gates * pulls, axis=1, keepdims=True)
    logit_grad = (pulls - mean_pull) / denominator * affinity * (1.0 - affinity)
    logit_grad = jnp.where(picked, logit_grad, 0.0)
    place = core * chips + chip
    own_logit = lax.dynamic_slice_in_dim(logit_grad, place * tok_count, tok_count, axis=0)
    grad_router = lax.psum(exact_dot(tokens, own_logit, FIRST), ("dp", "expert"))
    router_back = lax.dot_general(own_logit, router, LAST, precision=HIGHEST)
    parts = [
        dot(left, right, FIRST)
        for left, right in ((rows, gate_grad), (rows, up_grad), (cot, gated))
    ]
    summed = lax.psum_scatter(
        jnp.concatenate(parts, axis=1).astype(BF16), "dp", scatter_dimension=0, tiled=True
    ).astype(F32)
    grad_gate, grad_up, grad_down = jnp.split(summed, 3, axis=1)
    mixed = total[:, :features].astype(BF16)
    grad_tokens = (total[:, features:] + router_back).astype(BF16)
    return (mixed, grad_tokens, grad_router, grad_gate, grad_up, grad_down)


def send_back(keep, send, chips, chip):
    summed = (keep.astype(F32) + swap(send, "expert", 1).astype(F32)).astype(BF16)
    return [
        lax.dynamic_index_in_dim(summed, chip ^ m, 0, keepdims=False) for m in range(chips)
    ]


def give_back(pieces):
    return [
        piece if m == 0 else swap(piece, "expert", 2 * m) for m, piece in enumerate(pieces)
    ]


def kernels_plan(message, router, w_gate, w_up, w_down):
    features, experts = router.shape
    hidden_units = w_gate.shape[1]
    tok_count, width = message.shape
    groups = lax.axis_size("dp")
    chips = lax.axis_size("expert") // 2
    me = lax.axis_index("expert")
    half = chips * tok_count
    group_rows = 2 * half
    portion = features // groups
    at = jnp.stack([me % 2, me, lax.axis_index("dp"), me // 2]).astype(jnp.int32)
    router_t = router.T
    parts = jnp.concatenate(three_parts(router_t), axis=0)
    matrix = 2 * features * hidden_units
    weight_kinds = [pltpu.VMEM(w.shape, w.dtype) for w in (w_gate, w_up, w_down)]
    small = jax.ShapeDtypeStruct((experts, group_rows), F32)
    in_hbm_spec = pl.BlockSpec(memory_space=pltpu.HBM)

    pieces = [message] + [swap(message, "expert", 2 * m) for m in range(1, chips)]
    weights = call(
        load_kernel,
        weight_kinds,
        [IN_SMEM] + [in_hbm_spec] * 3,
        [IN_VMEM] * 3,
        [pltpu.SemaphoreType.DMA((3,))],
        moved=3 * matrix,
    )(at, *[in_hbm(w) for w in (w_gate, w_up, w_down)])
    by_chip = call(
        order_kernel,
        jax.ShapeDtypeStruct((chips, tok_count, width), BF16),
        [IN_SMEM, [IN_VMEM] * chips],
        IN_VMEM,
    )(at, pieces)
    mine = [by_chip] + [swap(by_chip, "dp", m) for m in range(1, groups)]
    theirs = [swap(x, "expert", 1) for x in mine]
    mine, theirs = [[x.reshape(half, width) for x in xs] for xs in (mine, theirs)]

    rows = jax.ShapeDtypeStruct((half, 2 * features), BF16)
    grad = jax.ShapeDtypeStruct((group_rows, hidden_units), BF16)
    keep, send, *own, pull, tables = call(
        own_kernel,
        [rows] * 2 + [grad] * 3 + [small, jax.ShapeDtypeStruct((3,) + small.shape, F32)],
        [IN_SMEM] + [IN_VMEM] * 6,
        [IN_VMEM] * 7,
        [pltpu.VMEM((group_rows, width), BF16), pltpu.VMEM((group_rows, 2 * features), BF16)],
        8,
        6 * matrix * group_rows,
        6 * matrix,
    )(at, mine[0], theirs[0], parts, *weights)
    rows = jax.ShapeDtypeStruct((tok_count, 2 * features), BF16)
    keep, send = [x.reshape(chips, tok_count, -1) for x in (keep, send)]
    pair, pieces = call(
        pair_kernel,
        [small, [rows] * chips],
        [IN_SMEM] + [IN_VMEM] * 4,
        [IN_VMEM, [IN_VMEM] * chips],
    )(at, keep, swap(send, "expert", 1), pull, swap(pull, "expert", 1))
    pairs = [pair] + [swap(pair, "expert", 2 * m) for m in range(1, chips)]
    back = give_back(pieces)
    logit = call(
        logit_kernel, small, [IN_SMEM, IN_VMEM, [IN_VMEM] * chips], IN_VMEM
    )(at, tables, pairs)
    logits = [logit] + [swap(logit, "dp", m) for m in range(1, groups)]

    count = groups * group_rows
    result = jax.ShapeDtypeStruct((portion, hidden_units), F32)
    grad_gate, grad_up, grad_down, router_grad = call(
        weight_kernel,
        [result] * 3 + [jax.ShapeDtypeStruct((experts, features), F32)],
        [IN_SMEM, [IN_VMEM] * groups, [IN_VMEM] * groups]
        + [IN_VMEM] * 4
        + [[IN_VMEM] * 3, [IN_VMEM] * groups],
        [pl.BlockSpec(memory_space=pl.ANY)] * 3 + [IN_VMEM],
        [
            pltpu.VMEM((count, width), BF16),
            pltpu.VMEM((2, portion, count), BF16),
            [pltpu.VMEM((count, hidden_units), BF16)] * 3,
            [pltpu.VMEM((portion, hidden_units), F32)] * 3,
            pltpu.SemaphoreType.DMA((hidden_units // STEP, 3)),
        ],
        20,
        3 * matrix * count + 6 * portion * hidden_units * count,
        3 * matrix + 12 * portion * hidden_units,
    )(at, mine, theirs, parts, *weights, own, logits)
    rows = jax.ShapeDtypeStruct((tok_count, features), BF16)
    mixed, grad_tokens = call(
        last_kernel,
        [rows] * 2,
        [IN_SMEM] + [IN_VMEM] * 2 + [[IN_VMEM] * chips],
        [IN_VMEM] * 2,
    )(at, logit, router_t, back)
    return (mixed, grad_tokens, router_grad.T, grad_gate, grad_up, grad_down)


def solution(mesh):
    return jax.shard_map(
        local,
        mesh=mesh,
        in_specs=(
            P(("dp", "expert"), None),
            P(("dp", "expert"), None),
            P(),
            P(None, "expert"),
            P(None, "expert"),
            P(None, "expert"),
            P(("dp", "expert"), None),
        ),
        out_specs=(
            P(("dp", "expert"), None),
            P(("dp", "expert"), None),
            P(),
            P("dp", "expert"),
            P("dp", "expert"),
            P("dp", "expert"),
        ),
        check_vma=False,
    )
```

```python
import jax
import jax.numpy as jnp
from jax import lax
from jax.experimental import pallas as pl
from jax.experimental.pallas import tpu as pltpu
from jax.sharding import PartitionSpec as P

F32 = jnp.float32
BF16 = jnp.bfloat16
LANES = 128
STEP = 256
GATHER_BYTES = 8 << 20
HIGHEST = lax.Precision.HIGHEST
LAST = (((1,), (1,)), ((), ()))
FIRST = (((0,), (0,)), ((), ()))
IN_VMEM = pl.BlockSpec(memory_space=pltpu.VMEM)
IN_SMEM = pl.BlockSpec(memory_space=pltpu.SMEM)


def dot(left, right, contract=(((1,), (0,)), ((), ()))):
    return lax.dot_general(left, right, contract, preferred_element_type=F32)


def swap(x, axis, mask):
    count = lax.axis_size(axis)
    return lax.ppermute(x, axis, [(i, i ^ mask) for i in range(count)])


def in_hbm(x):
    return pltpu.with_memory_space_constraint(x, pltpu.HBM)


def three_parts(x):
    parts = []
    for _ in range(3):
        part = lax.reduce_precision(x, 8, 7)
        parts.append(part.astype(BF16))
        x = x - part
    return parts


def exact_dot(left, right, contract):
    return sum(dot(left, part, contract) for part in three_parts(right)[::-1])


def gates_of(rows, chosen, router):
    logits = exact_dot(rows, router, (((1,), (0,)), ((), ())))
    picked = chosen > 0.5
    affinity = jnp.where(picked, jax.nn.sigmoid(logits), 0.0)
    denominator = jnp.sum(affinity, axis=1, keepdims=True)
    return picked, affinity, denominator, affinity / denominator


def place_rows(x_ref, first, core, mine_ref, theirs_ref):
    half = mine_ref.shape[0]
    x_ref[pl.ds(pl.multiple_of(first + core * half, half), half), :] = mine_ref[...]
    x_ref[pl.ds(pl.multiple_of(first + (1 - core) * half, half), half), :] = theirs_ref[...]


def gate_tables(x, parts_ref, experts):
    features = parts_ref.shape[1]
    logits = dot(parts_ref[...], x[:, :features], LAST)
    logits = logits[2 * experts :] + logits[experts : 2 * experts] + logits[:experts]
    unit = lax.broadcasted_iota(jnp.int32, (experts, LANES), 0) == lax.broadcasted_iota(
        jnp.int32, (experts, LANES), 1
    )
    picked = dot(unit.astype(BF16), x[:, 2 * features :], LAST) > 0.5
    affinity = jnp.where(picked, 1.0 / (1.0 + jnp.exp(-logits)), 0.0)
    denominator = jnp.sum(affinity, axis=0, keepdims=True)
    return affinity, denominator, affinity / denominator


def slot_gates(gates, expert):
    own = lax.broadcasted_iota(jnp.int32, (gates.shape[0], LANES), 0) == expert
    return lax.dot_general(
        gates, own.astype(F32), FIRST, precision=HIGHEST, preferred_element_type=F32
    )


def hidden_step(at, x, slot_gate, w_gate_ref, w_up_ref, w_down_ref):
    features = w_gate_ref.shape[0]
    gate_pre = dot(x[:, :features], w_gate_ref[:, at])
    up_pre = dot(x[:, :features], w_up_ref[:, at])
    raw = dot(x[:, features : 2 * features], w_down_ref[:, at])
    sigma = 1.0 / (1.0 + jnp.exp(-gate_pre))
    silu = gate_pre * sigma
    hidden = silu * up_pre
    slot = jnp.tile(slot_gate, (1, STEP // LANES))
    hidden_grad = slot * raw
    gate_grad = hidden_grad * up_pre * sigma * (1.0 + gate_pre * (1.0 - sigma))
    grads = (gate_grad, hidden_grad * silu, slot * hidden)
    return [grad.astype(BF16) for grad in grads], hidden * raw


def load_kernel(_, *refs):
    count = len(refs) // 2
    copies = [
        pltpu.make_async_copy(refs[i], refs[count + i], refs[-1].at[i]) for i in range(count)
    ]
    for copy in copies:
        copy.start()
    for copy in copies:
        copy.wait()


def message_kernel(tokens_hbm, cot_hbm, routes_hbm, out_ref, tokens_ref, cot_ref, routes_ref, sems):
    count, features = tokens_ref.shape
    pairs = ((tokens_hbm, tokens_ref), (cot_hbm, cot_ref), (routes_hbm, routes_ref))
    copies = [pltpu.make_async_copy(*pair, sems.at[i]) for i, pair in enumerate(pairs)]
    for copy in copies:
        copy.start()
    for copy in copies:
        copy.wait()
    out_ref[:, :features] = tokens_ref[...]
    out_ref[:, features : 2 * features] = cot_ref[...]
    ids = lax.broadcasted_iota(jnp.int32, (count, LANES), 1)
    picked = jnp.zeros((count, LANES), F32)
    for k in range(routes_ref.shape[1]):
        picked += (routes_ref[:, k : k + 1] == ids).astype(F32)
    out_ref[:, 2 * features :] = picked.astype(BF16)


def order_kernel(at_ref, piece_refs, _, out_ref):
    for m, ref in enumerate(piece_refs):
        out_ref[at_ref[3] ^ m] = ref[...]


def own_kernel(
    at_ref, mine_ref, theirs_ref, parts_ref, w_gate_ref, w_up_ref, w_down_ref,
    keep_ref, send_ref, gate_grad_ref, up_grad_ref, gated_ref, pull_ref, table_ref,
    x_ref, back_ref,
):
    features, hidden_units = w_gate_ref.shape
    experts = parts_ref.shape[0] // 3
    core = at_ref[0]
    place_rows(x_ref, 0, core, mine_ref, theirs_ref)
    affinity, denominator, gates = gate_tables(x_ref, parts_ref, experts)
    table_ref[0] = affinity
    table_ref[1] = gates
    table_ref[2] = jnp.broadcast_to(denominator, affinity.shape)
    slot_gate = slot_gates(gates, at_ref[1])
    pulls = jnp.zeros(slot_gate.shape, F32)
    for start in range(0, hidden_units, STEP):
        at = pl.ds(start, STEP)
        grads, pulled = hidden_step(at, x_ref, slot_gate, w_gate_ref, w_up_ref, w_down_ref)
        gate_grad_ref[:, at], up_grad_ref[:, at], gated_ref[:, at] = grads
        pulls += sum(pulled[:, lane : lane + LANES] for lane in range(0, STEP, LANES))
    ones = jnp.ones((pull_ref.shape[0], LANES), F32)
    pull_ref[...] = lax.dot_general(
        ones, pulls, LAST, precision=HIGHEST, preferred_element_type=F32
    )
    for start in range(0, features, STEP):
        at = pl.ds(start, STEP)
        later = pl.ds(features + start, STEP)
        back_ref[:, at] = dot(gated_ref[...], w_down_ref[at, :], LAST).astype(BF16)
        back = dot(gate_grad_ref[...], w_gate_ref[at, :], LAST)
        back_ref[:, later] = (back + dot(up_grad_ref[...], w_up_ref[at, :], LAST)).astype(BF16)

    half = keep_ref.shape[0]
    keep_ref[...] = back_ref[pl.ds(pl.multiple_of(core * half, half), half), :]
    send_ref[...] = back_ref[pl.ds(pl.multiple_of((1 - core) * half, half), half), :]


def parts_of(x):
    parts = []
    for _ in range(3):
        parts.append(x.astype(BF16).astype(F32))
        x = x - parts[-1]
    return parts


def pair_kernel(at_ref, keep_ref, other_ref, pull_ref, other_pull_ref, *out_refs):
    features = keep_ref.shape[2]
    group_rows = pull_ref.shape[1]
    row = lax.broadcasted_iota(jnp.int32, pull_ref.shape, 0)
    pulls = jnp.where(row % 2 == at_ref[0], pull_ref[...], other_pull_ref[...])
    large, middle, low = parts_of(pulls)
    pulls = jnp.where(row < 2, large, jnp.where(row < 4, middle, low))
    tail = jnp.concatenate([pulls, jnp.zeros((row.shape[0], LANES - group_rows), F32)], axis=1)
    for m, ref in enumerate(out_refs):
        chip = at_ref[3] ^ m
        both = keep_ref[chip].astype(F32) + other_ref[chip].astype(F32)
        ref[:, :features] = both.astype(BF16)
        ref[:, features:] = tail.astype(BF16)


def logit_kernel(at_ref, table_ref, back_refs, _, out_ref):
    affinity, gates, denominator = table_ref[0], table_ref[1], table_ref[2]
    row = lax.broadcasted_iota(jnp.int32, affinity.shape, 0)
    width = back_refs[0].shape[1]
    pulls = jnp.zeros(affinity.shape, F32)
    for m, ref in enumerate(back_refs):
        tail = ref[:, width - LANES :].astype(F32)[:, : affinity.shape[1]]
        first = tail[0:1] + (tail[2:3] + tail[4:5])
        second = tail[1:2] + (tail[3:4] + tail[5:6])
        pulls = jnp.where(row // 2 == at_ref[3] ^ m, jnp.where(row % 2 == 0, first, second), pulls)
    mean_pull = jnp.sum(gates * pulls, axis=0, keepdims=True)
    out_ref[...] = (pulls - mean_pull) / denominator * affinity * (1.0 - affinity)


def far_kernel(
    at_ref, mine_refs, theirs_refs, parts_ref, w_gate_ref, w_up_ref, w_down_ref, own_refs,
    gate_grad_ref, up_grad_ref, gated_ref, turned_ref, x_ref,
):
    features, hidden_units = w_gate_ref.shape
    experts = parts_ref.shape[0] // 3
    grad_refs = (gate_grad_ref, up_grad_ref, gated_ref)
    portion = turned_ref.shape[1]
    group_rows = own_refs[0].shape[0]
    for m, (mine_ref, theirs_ref) in enumerate(zip(mine_refs, theirs_refs)):
        place_rows(x_ref, m * group_rows, at_ref[0], mine_ref, theirs_ref)
    first = at_ref[2] * portion
    for half in range(2):
        for row in range(0, portion, LANES):
            at = pl.ds(pl.multiple_of(half * features + first + row, LANES), LANES)
            turned_ref[half, row : row + LANES, :] = x_ref[:, at].T
    far = x_ref.at[group_rows:, :]
    slot_gate = slot_gates(gate_tables(far, parts_ref, experts)[2], at_ref[1])
    for start in range(0, hidden_units, STEP):
        at = pl.ds(start, STEP)
        grads, _ = hidden_step(at, far, slot_gate, w_gate_ref, w_up_ref, w_down_ref)
        for grad_ref, own_ref, grad in zip(grad_refs, own_refs, grads):
            grad_ref[:group_rows, at] = own_ref[:, at]
            grad_ref[group_rows:, at] = grad


def weight_kernel(turned_ref, grad_refs, _, gate_ref, up_ref, down_ref, out_refs, sems):
    target_refs = (gate_ref, up_ref, down_ref)
    copies = []
    for step, start in enumerate(range(0, grad_refs[0].shape[1], STEP)):
        at = pl.ds(start, STEP)
        for j, (grad_ref, out_ref, target_ref) in enumerate(
            zip(grad_refs, out_refs, target_refs)
        ):
            out_ref[:, at] = dot(turned_ref[j // 2], grad_ref[:, at])
            copy = pltpu.make_async_copy(
                out_ref.at[:, at], target_ref.at[:, at], sems.at[step, j]
            )
            copy.start()
            copies.append(copy)
    for copy in copies:
        copy.wait()


def last_kernel(
    at_ref, mine_refs, theirs_refs, logit_refs, router_ref, back_refs,
    mixed_ref, tokens_ref, router_grad_ref, x_ref,
):
    experts, features = router_ref.shape
    count = mixed_ref.shape[0]
    chips = len(back_refs)
    grads = logit_refs[0][...]
    shape = (count, grads.shape[1])
    row = lax.broadcasted_iota(jnp.int32, shape, 0) + (at_ref[0] * chips + at_ref[3]) * count
    own = (lax.broadcasted_iota(jnp.int32, shape, 1) == row).astype(F32)
    own_grads = lax.dot_general(own, grads, LAST, precision=HIGHEST, preferred_element_type=F32)
    back = jnp.dot(own_grads, router_ref[...], precision=HIGHEST, preferred_element_type=F32)
    summed = sum(ref[...].astype(F32) for ref in back_refs)
    mixed_ref[...] = summed[:, :features].astype(BF16)
    tokens_ref[...] = (summed[:, features : 2 * features] + back).astype(BF16)
    totals = []
    group_rows = grads.shape[1]
    for m, (mine_ref, theirs_ref) in enumerate(zip(mine_refs, theirs_refs)):
        place_rows(
            x_ref,
            m * group_rows,
            at_ref[0],
            mine_ref.at[:, :features],
            theirs_ref.at[:, :features],
        )
    for m, logit_ref in enumerate(logit_refs):
        stacked = jnp.concatenate(parts_of(logit_ref[...]), axis=0).astype(BF16)
        total = dot(stacked, x_ref[m * group_rows : (m + 1) * group_rows, :])
        totals.append(total[2 * experts :] + total[experts : 2 * experts] + total[:experts])
    while len(totals) > 1:
        totals = [totals[i] + totals[i + 1] for i in range(0, len(totals), 2)]
    router_grad_ref[...] = totals[0]


def call(kernel, out_shape, in_specs, out_specs, scratch=(), limit=4, flops=0, moved=1 << 17):
    return pl.pallas_call(
        kernel,
        out_shape=out_shape,
        in_specs=in_specs,
        out_specs=out_specs,
        scratch_shapes=scratch,
        compiler_params=pltpu.CompilerParams(vmem_limit_bytes=limit << 20),
        cost_estimate=pl.CostEstimate(flops=flops, bytes_accessed=moved, transcendentals=0),
    )


def local(tokens, routes, router, w_gate, w_up, w_down, cotangent):
    tok_count, features = tokens.shape
    experts = router.shape[1]
    hidden_units = w_gate.shape[1]
    devices = lax.axis_size("expert")
    groups = lax.axis_size("dp")
    sharing = devices // experts
    chips = devices // 2
    group_rows = devices * tok_count
    me = lax.axis_index("expert")
    group = lax.axis_index("dp")
    core, chip = me % 2, me // 2
    own_expert = me // sharing
    whole = sharing == 1 and group_rows <= LANES and groups * group_rows * features * 4 <= GATHER_BYTES

    def over_chips(x):
        out = jnp.zeros((chips,) + x.shape, x.dtype)
        for m in range(chips):
            piece = x if m == 0 else swap(x, "expert", 2 * m)
            out = lax.dynamic_update_index_in_dim(out, piece, chip ^ m, 0)
        return out

    def over_cores(x):
        other = swap(x, "expert", 1)
        return jnp.where(core == 0, jnp.stack([x, other]), jnp.stack([other, x]))

    if whole:
        return kernels_plan(tokens, routes, router, w_gate, w_up, w_down, cotangent)

    ids = jnp.arange(LANES, dtype=jnp.int32)
    picked_wide = jnp.any(routes[:, :, None] == ids[None, None, :], axis=1).astype(BF16)
    message = jnp.concatenate([tokens, cotangent, picked_wide], axis=1)
    width = message.shape[1]
    by_chip = over_chips(message)
    own = over_cores(by_chip).reshape(group_rows, width)
    rows, cot = own[:, :features], own[:, features : 2 * features]
    picked, affinity, denominator, gates = gates_of(
        rows, own[:, 2 * features : 2 * features + experts], router
    )
    slot_gate = lax.dynamic_slice_in_dim(gates, own_expert, 1, axis=1)
    gate_pre = dot(rows, w_gate)
    up_pre = dot(rows, w_up)
    sigma = jax.nn.sigmoid(gate_pre)
    silu = gate_pre * sigma
    hidden = silu * up_pre
    raw = dot(cot, w_down)
    pull = jnp.sum(hidden * raw, axis=1)
    hidden_grad = slot_gate * raw
    gate_grad = (hidden_grad * up_pre * sigma * (1.0 + gate_pre * (1.0 - sigma))).astype(BF16)
    up_grad = (hidden_grad * silu).astype(BF16)
    gated = (slot_gate * hidden).astype(BF16)
    mixed_part = dot(gated, w_down, LAST)
    input_part = dot(gate_grad, w_gate, LAST) + dot(up_grad, w_up, LAST)
    part = jnp.concatenate([mixed_part.astype(BF16), input_part.astype(BF16)], axis=1)
    part = part.reshape(2, chips, tok_count, 2 * features)
    keep = lax.dynamic_index_in_dim(part, core, 0, keepdims=False)
    send = lax.dynamic_index_in_dim(part, 1 - core, 0, keepdims=False)
    back = give_back(send_back(keep, send, chips, chip))
    total = sum(x.astype(F32) for x in back)
    pulls = over_cores(over_chips(pull))
    pulls = jnp.swapaxes(pulls, 0, 1).reshape(experts, sharing, -1)
    pulls = jnp.sum(pulls, axis=1).T
    mean_pull = jnp.sum(gates * pulls, axis=1, keepdims=True)
    logit_grad = (pulls - mean_pull) / denominator * affinity * (1.0 - affinity)
    logit_grad = jnp.where(picked, logit_grad, 0.0)
    place = core * chips + chip
    own_logit = lax.dynamic_slice_in_dim(logit_grad, place * tok_count, tok_count, axis=0)
    grad_router = lax.psum(exact_dot(tokens, own_logit, FIRST), ("dp", "expert"))
    router_back = lax.dot_general(own_logit, router, LAST, precision=HIGHEST)
    parts = [
        dot(left, right, FIRST)
        for left, right in ((rows, gate_grad), (rows, up_grad), (cot, gated))
    ]
    summed = lax.psum_scatter(
        jnp.concatenate(parts, axis=1).astype(BF16), "dp", scatter_dimension=0, tiled=True
    ).astype(F32)
    grad_gate, grad_up, grad_down = jnp.split(summed, 3, axis=1)
    mixed = total[:, :features].astype(BF16)
    grad_tokens = (total[:, features:] + router_back).astype(BF16)
    return (mixed, grad_tokens, grad_router, grad_gate, grad_up, grad_down)


def send_back(keep, send, chips, chip):
    summed = (keep.astype(F32) + swap(send, "expert", 1).astype(F32)).astype(BF16)
    return [
        lax.dynamic_index_in_dim(summed, chip ^ m, 0, keepdims=False) for m in range(chips)
    ]


def give_back(pieces):
    return [
        piece if m == 0 else swap(piece, "expert", 2 * m) for m, piece in enumerate(pieces)
    ]


def kernels_plan(tokens, routes, router, w_gate, w_up, w_down, cotangent):
    features, experts = router.shape
    hidden_units = w_gate.shape[1]
    tok_count = tokens.shape[0]
    width = 2 * features + LANES
    groups = lax.axis_size("dp")
    chips = lax.axis_size("expert") // 2
    me = lax.axis_index("expert")
    half = chips * tok_count
    group_rows = 2 * half
    portion = features // groups
    at = jnp.stack([me % 2, me, lax.axis_index("dp"), me // 2]).astype(jnp.int32)
    router_t = router.T
    parts = jnp.concatenate(three_parts(router_t), axis=0)
    matrix = 2 * features * hidden_units
    weight_kinds = [pltpu.VMEM(w.shape, w.dtype) for w in (w_gate, w_up, w_down)]
    small = jax.ShapeDtypeStruct((experts, group_rows), F32)
    in_hbm_spec = pl.BlockSpec(memory_space=pltpu.HBM)

    sources = (tokens, cotangent, routes)
    message = call(
        message_kernel,
        jax.ShapeDtypeStruct((tok_count, width), BF16),
        [in_hbm_spec] * 3,
        IN_VMEM,
        [pltpu.VMEM(x.shape, x.dtype) for x in sources] + [pltpu.SemaphoreType.DMA((3,))],
    )(*[in_hbm(x) for x in sources])
    pieces = [message] + [swap(message, "expert", 2 * m) for m in range(1, chips)]
    weights = call(
        load_kernel,
        weight_kinds,
        [IN_SMEM] + [in_hbm_spec] * 3,
        [IN_VMEM] * 3,
        [pltpu.SemaphoreType.DMA((3,))],
        moved=3 * matrix,
    )(at, *[in_hbm(w) for w in (w_gate, w_up, w_down)])
    by_chip = call(
        order_kernel,
        jax.ShapeDtypeStruct((chips, tok_count, width), BF16),
        [IN_SMEM, [IN_VMEM] * chips, pl.BlockSpec(memory_space=pl.ANY)],
        IN_VMEM,
    )(at, pieces, weights[0])
    mine = [by_chip] + [swap(by_chip, "dp", m) for m in range(1, groups)]
    theirs = swap(by_chip, "expert", 1)

    rows = jax.ShapeDtypeStruct((half, 2 * features), BF16)
    grad = jax.ShapeDtypeStruct((group_rows, hidden_units), BF16)
    keep, send, *own, pull, tables = call(
        own_kernel,
        [rows] * 2 + [grad] * 3 + [small, jax.ShapeDtypeStruct((3,) + small.shape, F32)],
        [IN_SMEM] + [IN_VMEM] * 6,
        [IN_VMEM] * 7,
        [pltpu.VMEM((group_rows, width), BF16), pltpu.VMEM((group_rows, 2 * features), BF16)],
        8,
        6 * matrix * group_rows,
        6 * matrix,
    )(at, by_chip.reshape(half, width), theirs.reshape(half, width), parts, *weights)
    rows = jax.ShapeDtypeStruct((tok_count, width), BF16)
    keep, send = [x.reshape(chips, tok_count, -1) for x in (keep, send)]
    pieces = call(
        pair_kernel,
        [rows] * chips,
        [IN_SMEM] + [IN_VMEM] * 4,
        [IN_VMEM] * chips,
    )(at, keep, swap(send, "expert", 1), pull, swap(pull, "expert", 1))
    back = give_back(pieces)
    _, *far = lax.optimization_barrier([pieces[0]] + mine[1:])
    mine = [by_chip] + far
    theirs = [theirs] + [swap(x, "expert", 1) for x in far]
    mine, theirs = [[x.reshape(half, width) for x in xs] for xs in (mine, theirs)]

    count = groups * group_rows
    *grads, turned = call(
        far_kernel,
        [pltpu.VMEM((count, hidden_units), BF16)] * 3 + [pltpu.VMEM((2, portion, count), BF16)],
        [IN_SMEM, [IN_VMEM] * groups, [IN_VMEM] * groups] + [IN_VMEM] * 4 + [[IN_VMEM] * 3],
        [IN_VMEM] * 4,
        [pltpu.VMEM((count, width), BF16)],
        12,
    )(at, mine, theirs, parts, *weights, own)
    logit = call(
        logit_kernel,
        small,
        [IN_SMEM, IN_VMEM, [IN_VMEM] * chips, pl.BlockSpec(memory_space=pl.ANY)],
        IN_VMEM,
    )(at, tables, back, turned)
    logits = [logit] + [swap(logit, "dp", m) for m in range(1, groups)]
    result = jax.ShapeDtypeStruct((portion, hidden_units), F32)
    grad_gate, grad_up, grad_down = call(
        weight_kernel,
        [result] * 3,
        [IN_VMEM, [IN_VMEM] * 3, pl.BlockSpec(memory_space=pl.ANY)],
        [pl.BlockSpec(memory_space=pl.ANY)] * 3,
        [
            [pltpu.VMEM((portion, hidden_units), F32)] * 3,
            pltpu.SemaphoreType.DMA((hidden_units // STEP, 3)),
        ],
        12,
        6 * portion * hidden_units * count,
        12 * portion * hidden_units,
    )(turned, grads, logit)
    rows = jax.ShapeDtypeStruct((tok_count, features), BF16)
    mixed, grad_tokens, router_grad = call(
        last_kernel,
        [rows] * 2 + [jax.ShapeDtypeStruct((experts, features), F32)],
        [IN_SMEM]
        + [[IN_VMEM] * groups] * 3
        + [IN_VMEM, [IN_VMEM] * chips],
        [IN_VMEM] * 3,
        [pltpu.VMEM((count, features), BF16)],
    )(at, mine, theirs, logits, router_t, back)
    return (mixed, grad_tokens, router_grad.T, grad_gate, grad_up, grad_down)


def solution(mesh):
    return jax.shard_map(
        local,
        mesh=mesh,
        in_specs=(
            P(("dp", "expert"), None),
            P(("dp", "expert"), None),
            P(),
            P(None, "expert"),
            P(None, "expert"),
            P(None, "expert"),
            P(("dp", "expert"), None),
        ),
        out_specs=(
            P(("dp", "expert"), None),
            P(("dp", "expert"), None),
            P(),
            P("dp", "expert"),
            P("dp", "expert"),
            P("dp", "expert"),
        ),
        check_vma=False,
    )
```

```python
import jax
import jax.numpy as jnp
from jax import lax
from jax.experimental import pallas as pl
from jax.experimental.pallas import tpu as pltpu
from jax.sharding import PartitionSpec as P

F32 = jnp.float32
BF16 = jnp.bfloat16
LANES = 128
STEP = 256
GATHER_BYTES = 8 << 20
HIGHEST = lax.Precision.HIGHEST
LAST = (((1,), (1,)), ((), ()))
FIRST = (((0,), (0,)), ((), ()))
IN_VMEM = pl.BlockSpec(memory_space=pltpu.VMEM)
IN_SMEM = pl.BlockSpec(memory_space=pltpu.SMEM)


def dot(left, right, contract=(((1,), (0,)), ((), ()))):
    return lax.dot_general(left, right, contract, preferred_element_type=F32)


def swap(x, axis, mask):
    count = lax.axis_size(axis)
    return lax.ppermute(x, axis, [(i, i ^ mask) for i in range(count)])


def in_hbm(x):
    return pltpu.with_memory_space_constraint(x, pltpu.HBM)


def three_parts(x):
    parts = []
    for _ in range(3):
        part = lax.reduce_precision(x, 8, 7)
        parts.append(part.astype(BF16))
        x = x - part
    return parts


def exact_dot(left, right, contract):
    return sum(dot(left, part, contract) for part in three_parts(right)[::-1])


def gates_of(rows, chosen, router):
    logits = exact_dot(rows, router, (((1,), (0,)), ((), ())))
    picked = chosen > 0.5
    affinity = jnp.where(picked, jax.nn.sigmoid(logits), 0.0)
    denominator = jnp.sum(affinity, axis=1, keepdims=True)
    return picked, affinity, denominator, affinity / denominator


def place_rows(x_ref, first, core, mine_ref, theirs_ref):
    half = mine_ref.shape[0]
    x_ref[pl.ds(pl.multiple_of(first + core * half, half), half), :] = mine_ref[...]
    x_ref[pl.ds(pl.multiple_of(first + (1 - core) * half, half), half), :] = theirs_ref[...]


def gate_tables(x, parts_ref, experts):
    features = parts_ref.shape[1]
    logits = dot(parts_ref[...], x[:, :features], LAST)
    logits = logits[2 * experts :] + logits[experts : 2 * experts] + logits[:experts]
    unit = lax.broadcasted_iota(jnp.int32, (experts, LANES), 0) == lax.broadcasted_iota(
        jnp.int32, (experts, LANES), 1
    )
    picked = dot(unit.astype(BF16), x[:, 2 * features :], LAST) > 0.5
    affinity = jnp.where(picked, 1.0 / (1.0 + jnp.exp(-logits)), 0.0)
    denominator = jnp.sum(affinity, axis=0, keepdims=True)
    return affinity, denominator, affinity / denominator


def slot_gates(gates, expert):
    own = lax.broadcasted_iota(jnp.int32, (gates.shape[0], LANES), 0) == expert
    return lax.dot_general(
        gates, own.astype(F32), FIRST, precision=HIGHEST, preferred_element_type=F32
    )


def hidden_step(at, x, slot_gate, w_gate_ref, w_up_ref, w_down_ref):
    features = w_gate_ref.shape[0]
    gate_pre = dot(x[:, :features], w_gate_ref[:, at])
    up_pre = dot(x[:, :features], w_up_ref[:, at])
    raw = dot(x[:, features : 2 * features], w_down_ref[:, at])
    sigma = 1.0 / (1.0 + jnp.exp(-gate_pre))
    silu = gate_pre * sigma
    hidden = silu * up_pre
    slot = jnp.tile(slot_gate, (1, STEP // LANES))
    hidden_grad = slot * raw
    gate_grad = hidden_grad * up_pre * sigma * (1.0 + gate_pre * (1.0 - sigma))
    grads = (gate_grad, hidden_grad * silu, slot * hidden)
    return [grad.astype(BF16) for grad in grads], hidden * raw


def load_kernel(_, *refs):
    count = len(refs) // 2
    copies = [
        pltpu.make_async_copy(refs[i], refs[count + i], refs[-1].at[i]) for i in range(count)
    ]
    for copy in copies:
        copy.start()
    for copy in copies:
        copy.wait()


def message_kernel(tokens_hbm, cot_hbm, routes_hbm, out_ref, tokens_ref, cot_ref, routes_ref, sems):
    count, features = tokens_ref.shape
    pairs = ((tokens_hbm, tokens_ref), (cot_hbm, cot_ref), (routes_hbm, routes_ref))
    copies = [pltpu.make_async_copy(*pair, sems.at[i]) for i, pair in enumerate(pairs)]
    for copy in copies:
        copy.start()
    for copy in copies:
        copy.wait()
    out_ref[:, :features] = tokens_ref[...]
    out_ref[:, features : 2 * features] = cot_ref[...]
    ids = lax.broadcasted_iota(jnp.int32, (count, LANES), 1)
    picked = jnp.zeros((count, LANES), F32)
    for k in range(routes_ref.shape[1]):
        picked += (routes_ref[:, k : k + 1] == ids).astype(F32)
    out_ref[:, 2 * features :] = picked.astype(BF16)


def order_kernel(at_ref, piece_refs, _, out_ref):
    for m, ref in enumerate(piece_refs):
        out_ref[at_ref[3] ^ m] = ref[...]


def own_kernel(
    at_ref, mine_ref, theirs_ref, parts_ref, w_gate_ref, w_up_ref, w_down_ref,
    keep_ref, send_ref, gate_grad_ref, up_grad_ref, gated_ref, pull_ref, table_ref,
    x_ref, back_ref,
):
    features, hidden_units = w_gate_ref.shape
    experts = parts_ref.shape[0] // 3
    core = at_ref[0]
    place_rows(x_ref, 0, core, mine_ref, theirs_ref)
    affinity, denominator, gates = gate_tables(x_ref, parts_ref, experts)
    table_ref[0] = affinity
    table_ref[1] = gates
    table_ref[2] = jnp.broadcast_to(denominator, affinity.shape)
    slot_gate = slot_gates(gates, at_ref[1])
    pulls = jnp.zeros(slot_gate.shape, F32)
    for start in range(0, hidden_units, STEP):
        at = pl.ds(start, STEP)
        grads, pulled = hidden_step(at, x_ref, slot_gate, w_gate_ref, w_up_ref, w_down_ref)
        gate_grad_ref[:, at], up_grad_ref[:, at], gated_ref[:, at] = grads
        pulls += sum(pulled[:, lane : lane + LANES] for lane in range(0, STEP, LANES))
    ones = jnp.ones((pull_ref.shape[0], LANES), F32)
    pull_ref[...] = lax.dot_general(
        ones, pulls, LAST, precision=HIGHEST, preferred_element_type=F32
    )
    for start in range(0, features, STEP):
        at = pl.ds(start, STEP)
        later = pl.ds(features + start, STEP)
        back_ref[:, at] = dot(gated_ref[...], w_down_ref[at, :], LAST).astype(BF16)
        back = dot(gate_grad_ref[...], w_gate_ref[at, :], LAST)
        back_ref[:, later] = (back + dot(up_grad_ref[...], w_up_ref[at, :], LAST)).astype(BF16)

    half = keep_ref.shape[0]
    keep_ref[...] = back_ref[pl.ds(pl.multiple_of(core * half, half), half), :]
    send_ref[...] = back_ref[pl.ds(pl.multiple_of((1 - core) * half, half), half), :]


def parts_of(x):
    parts = []
    for _ in range(3):
        parts.append(x.astype(BF16).astype(F32))
        x = x - parts[-1]
    return parts


def pair_kernel(at_ref, keep_ref, other_ref, pull_ref, other_pull_ref, *out_refs):
    features = keep_ref.shape[2]
    group_rows = pull_ref.shape[1]
    row = lax.broadcasted_iota(jnp.int32, pull_ref.shape, 0)
    pulls = jnp.where(row % 2 == at_ref[0], pull_ref[...], other_pull_ref[...])
    large, middle, low = parts_of(pulls)
    pulls = jnp.where(row < 2, large, jnp.where(row < 4, middle, low))
    tail = jnp.concatenate([pulls, jnp.zeros((row.shape[0], LANES - group_rows), F32)], axis=1)
    for m, ref in enumerate(out_refs):
        chip = at_ref[3] ^ m
        both = keep_ref[chip].astype(F32) + other_ref[chip].astype(F32)
        ref[:, :features] = both.astype(BF16)
        ref[:, features:] = tail.astype(BF16)


def logit_kernel(at_ref, table_ref, back_refs, _, out_ref):
    affinity, gates, denominator = table_ref[0], table_ref[1], table_ref[2]
    row = lax.broadcasted_iota(jnp.int32, affinity.shape, 0)
    width = back_refs[0].shape[1]
    pulls = jnp.zeros(affinity.shape, F32)
    for m, ref in enumerate(back_refs):
        tail = ref[:, width - LANES :].astype(F32)[:, : affinity.shape[1]]
        first = tail[0:1] + (tail[2:3] + tail[4:5])
        second = tail[1:2] + (tail[3:4] + tail[5:6])
        pulls = jnp.where(row // 2 == at_ref[3] ^ m, jnp.where(row % 2 == 0, first, second), pulls)
    mean_pull = jnp.sum(gates * pulls, axis=0, keepdims=True)
    out_ref[...] = (pulls - mean_pull) / denominator * affinity * (1.0 - affinity)


def far_kernel(
    at_ref, mine_refs, theirs_refs, parts_ref, w_gate_ref, w_up_ref, w_down_ref, own_refs,
    gate_grad_ref, up_grad_ref, gated_ref, turned_ref, x_ref,
):
    features, hidden_units = w_gate_ref.shape
    experts = parts_ref.shape[0] // 3
    grad_refs = (gate_grad_ref, up_grad_ref, gated_ref)
    portion = turned_ref.shape[1]
    group_rows = own_refs[0].shape[0]
    for m, (mine_ref, theirs_ref) in enumerate(zip(mine_refs, theirs_refs)):
        place_rows(x_ref, m * group_rows, at_ref[0], mine_ref, theirs_ref)
    first = at_ref[2] * portion
    for half in range(2):
        for row in range(0, portion, LANES):
            at = pl.ds(pl.multiple_of(half * features + first + row, LANES), LANES)
            turned_ref[half, row : row + LANES, :] = x_ref[:, at].T
    far = x_ref.at[group_rows:, :]
    slot_gate = slot_gates(gate_tables(far, parts_ref, experts)[2], at_ref[1])
    for start in range(0, hidden_units, STEP):
        at = pl.ds(start, STEP)
        grads, _ = hidden_step(at, far, slot_gate, w_gate_ref, w_up_ref, w_down_ref)
        for grad_ref, own_ref, grad in zip(grad_refs, own_refs, grads):
            grad_ref[:group_rows, at] = own_ref[:, at]
            grad_ref[group_rows:, at] = grad


def weight_kernel(turned_ref, grad_refs, _, gate_ref, up_ref, down_ref, out_refs, sems):
    target_refs = (gate_ref, up_ref, down_ref)
    copies = []
    for step, start in enumerate(range(0, grad_refs[0].shape[1], STEP)):
        at = pl.ds(start, STEP)
        for j, (grad_ref, out_ref, target_ref) in enumerate(
            zip(grad_refs, out_refs, target_refs)
        ):
            out_ref[:, at] = dot(turned_ref[j // 2], grad_ref[:, at])
            copy = pltpu.make_async_copy(
                out_ref.at[:, at], target_ref.at[:, at], sems.at[step, j]
            )
            copy.start()
            copies.append(copy)
    for copy in copies:
        copy.wait()


def last_kernel(
    at_ref, mine_refs, theirs_refs, logit_refs, router_ref, back_refs,
    mixed_ref, tokens_ref, router_grad_ref, x_ref,
):
    experts, features = router_ref.shape
    count = mixed_ref.shape[0]
    chips = len(back_refs)
    grads = logit_refs[0][...]
    shape = (count, grads.shape[1])
    row = lax.broadcasted_iota(jnp.int32, shape, 0) + (at_ref[0] * chips + at_ref[3]) * count
    own = (lax.broadcasted_iota(jnp.int32, shape, 1) == row).astype(F32)
    own_grads = lax.dot_general(own, grads, LAST, precision=HIGHEST, preferred_element_type=F32)
    back = jnp.dot(own_grads, router_ref[...], precision=HIGHEST, preferred_element_type=F32)
    summed = sum(ref[...].astype(F32) for ref in back_refs)
    mixed_ref[...] = summed[:, :features].astype(BF16)
    tokens_ref[...] = (summed[:, features : 2 * features] + back).astype(BF16)
    totals = []
    group_rows = grads.shape[1]
    for m, (mine_ref, theirs_ref) in enumerate(zip(mine_refs, theirs_refs)):
        place_rows(
            x_ref,
            m * group_rows,
            at_ref[0],
            mine_ref.at[:, :features],
            theirs_ref.at[:, :features],
        )
    for m, logit_ref in enumerate(logit_refs):
        stacked = jnp.concatenate(parts_of(logit_ref[...]), axis=0).astype(BF16)
        total = dot(stacked, x_ref[m * group_rows : (m + 1) * group_rows, :])
        totals.append(total[2 * experts :] + total[experts : 2 * experts] + total[:experts])
    while len(totals) > 1:
        totals = [totals[i] + totals[i + 1] for i in range(0, len(totals), 2)]
    router_grad_ref[...] = totals[0]


def call(kernel, out_shape, in_specs, out_specs, scratch=(), limit=4):
    return pl.pallas_call(
        kernel,
        out_shape=out_shape,
        in_specs=in_specs,
        out_specs=out_specs,
        scratch_shapes=scratch,
        compiler_params=pltpu.CompilerParams(vmem_limit_bytes=limit << 20),
        cost_estimate=pl.CostEstimate(flops=0, bytes_accessed=1, transcendentals=0),
    )


def local(tokens, routes, router, w_gate, w_up, w_down, cotangent):
    tok_count, features = tokens.shape
    experts = router.shape[1]
    hidden_units = w_gate.shape[1]
    devices = lax.axis_size("expert")
    groups = lax.axis_size("dp")
    sharing = devices // experts
    chips = devices // 2
    group_rows = devices * tok_count
    me = lax.axis_index("expert")
    group = lax.axis_index("dp")
    core, chip = me % 2, me // 2
    own_expert = me // sharing
    whole = sharing == 1 and group_rows <= LANES and groups * group_rows * features * 4 <= GATHER_BYTES

    def over_chips(x):
        out = jnp.zeros((chips,) + x.shape, x.dtype)
        for m in range(chips):
            piece = x if m == 0 else swap(x, "expert", 2 * m)
            out = lax.dynamic_update_index_in_dim(out, piece, chip ^ m, 0)
        return out

    def over_cores(x):
        other = swap(x, "expert", 1)
        return jnp.where(core == 0, jnp.stack([x, other]), jnp.stack([other, x]))

    if whole:
        return kernels_plan(tokens, routes, router, w_gate, w_up, w_down, cotangent)

    ids = jnp.arange(LANES, dtype=jnp.int32)
    picked_wide = jnp.any(routes[:, :, None] == ids[None, None, :], axis=1).astype(BF16)
    message = jnp.concatenate([tokens, cotangent, picked_wide], axis=1)
    width = message.shape[1]
    by_chip = over_chips(message)
    own = over_cores(by_chip).reshape(group_rows, width)
    rows, cot = own[:, :features], own[:, features : 2 * features]
    picked, affinity, denominator, gates = gates_of(
        rows, own[:, 2 * features : 2 * features + experts], router
    )
    slot_gate = lax.dynamic_slice_in_dim(gates, own_expert, 1, axis=1)
    gate_pre = dot(rows, w_gate)
    up_pre = dot(rows, w_up)
    sigma = jax.nn.sigmoid(gate_pre)
    silu = gate_pre * sigma
    hidden = silu * up_pre
    raw = dot(cot, w_down)
    pull = jnp.sum(hidden * raw, axis=1)
    hidden_grad = slot_gate * raw
    gate_grad = (hidden_grad * up_pre * sigma * (1.0 + gate_pre * (1.0 - sigma))).astype(BF16)
    up_grad = (hidden_grad * silu).astype(BF16)
    gated = (slot_gate * hidden).astype(BF16)
    mixed_part = dot(gated, w_down, LAST)
    input_part = dot(gate_grad, w_gate, LAST) + dot(up_grad, w_up, LAST)
    part = jnp.concatenate([mixed_part.astype(BF16), input_part.astype(BF16)], axis=1)
    part = part.reshape(2, chips, tok_count, 2 * features)
    keep = lax.dynamic_index_in_dim(part, core, 0, keepdims=False)
    send = lax.dynamic_index_in_dim(part, 1 - core, 0, keepdims=False)
    back = give_back(send_back(keep, send, chips, chip))
    total = sum(x.astype(F32) for x in back)
    pulls = over_cores(over_chips(pull))
    pulls = jnp.swapaxes(pulls, 0, 1).reshape(experts, sharing, -1)
    pulls = jnp.sum(pulls, axis=1).T
    mean_pull = jnp.sum(gates * pulls, axis=1, keepdims=True)
    logit_grad = (pulls - mean_pull) / denominator * affinity * (1.0 - affinity)
    logit_grad = jnp.where(picked, logit_grad, 0.0)
    place = core * chips + chip
    own_logit = lax.dynamic_slice_in_dim(logit_grad, place * tok_count, tok_count, axis=0)
    grad_router = lax.psum(exact_dot(tokens, own_logit, FIRST), ("dp", "expert"))
    router_back = lax.dot_general(own_logit, router, LAST, precision=HIGHEST)
    parts = [
        dot(left, right, FIRST)
        for left, right in ((rows, gate_grad), (rows, up_grad), (cot, gated))
    ]
    summed = lax.psum_scatter(
        jnp.concatenate(parts, axis=1).astype(BF16), "dp", scatter_dimension=0, tiled=True
    ).astype(F32)
    grad_gate, grad_up, grad_down = jnp.split(summed, 3, axis=1)
    mixed = total[:, :features].astype(BF16)
    grad_tokens = (total[:, features:] + router_back).astype(BF16)
    return (mixed, grad_tokens, grad_router, grad_gate, grad_up, grad_down)


def send_back(keep, send, chips, chip):
    summed = (keep.astype(F32) + swap(send, "expert", 1).astype(F32)).astype(BF16)
    return [
        lax.dynamic_index_in_dim(summed, chip ^ m, 0, keepdims=False) for m in range(chips)
    ]


def give_back(pieces):
    return [
        piece if m == 0 else swap(piece, "expert", 2 * m) for m, piece in enumerate(pieces)
    ]


def kernels_plan(tokens, routes, router, w_gate, w_up, w_down, cotangent):
    features, experts = router.shape
    hidden_units = w_gate.shape[1]
    tok_count = tokens.shape[0]
    width = 2 * features + LANES
    groups = lax.axis_size("dp")
    chips = lax.axis_size("expert") // 2
    me = lax.axis_index("expert")
    half = chips * tok_count
    group_rows = 2 * half
    portion = features // groups
    at = jnp.stack([me % 2, me, lax.axis_index("dp"), me // 2]).astype(jnp.int32)
    router_t = router.T
    parts = jnp.concatenate(three_parts(router_t), axis=0)
    weight_kinds = [pltpu.VMEM(w.shape, w.dtype) for w in (w_gate, w_up, w_down)]
    small = jax.ShapeDtypeStruct((experts, group_rows), F32)
    in_hbm_spec = pl.BlockSpec(memory_space=pltpu.HBM)

    sources = (tokens, cotangent, routes)
    message = call(
        message_kernel,
        jax.ShapeDtypeStruct((tok_count, width), BF16),
        [in_hbm_spec] * 3,
        IN_VMEM,
        [pltpu.VMEM(x.shape, x.dtype) for x in sources] + [pltpu.SemaphoreType.DMA((3,))],
    )(*[in_hbm(x) for x in sources])
    pieces = [message] + [swap(message, "expert", 2 * m) for m in range(1, chips)]
    weights = call(
        load_kernel,
        weight_kinds,
        [IN_SMEM] + [in_hbm_spec] * 3,
        [IN_VMEM] * 3,
        [pltpu.SemaphoreType.DMA((3,))],
    )(at, *[in_hbm(w) for w in (w_gate, w_up, w_down)])
    by_chip = call(
        order_kernel,
        jax.ShapeDtypeStruct((chips, tok_count, width), BF16),
        [IN_SMEM, [IN_VMEM] * chips, pl.BlockSpec(memory_space=pl.ANY)],
        IN_VMEM,
    )(at, pieces, weights[0])
    mine = [by_chip] + [swap(by_chip, "dp", m) for m in range(1, groups)]
    theirs = swap(by_chip, "expert", 1)

    rows = jax.ShapeDtypeStruct((half, 2 * features), BF16)
    grad = jax.ShapeDtypeStruct((group_rows, hidden_units), BF16)
    keep, send, *own, pull, tables = call(
        own_kernel,
        [rows] * 2 + [grad] * 3 + [small, jax.ShapeDtypeStruct((3,) + small.shape, F32)],
        [IN_SMEM] + [IN_VMEM] * 6,
        [IN_VMEM] * 7,
        [pltpu.VMEM((group_rows, width), BF16), pltpu.VMEM((group_rows, 2 * features), BF16)],
        8,
    )(at, by_chip.reshape(half, width), theirs.reshape(half, width), parts, *weights)
    rows = jax.ShapeDtypeStruct((tok_count, width), BF16)
    keep, send = [x.reshape(chips, tok_count, -1) for x in (keep, send)]
    pieces = call(
        pair_kernel,
        [rows] * chips,
        [IN_SMEM] + [IN_VMEM] * 4,
        [IN_VMEM] * chips,
    )(at, keep, swap(send, "expert", 1), pull, swap(pull, "expert", 1))
    back = give_back(pieces)
    _, *far = lax.optimization_barrier([pieces[0]] + mine[1:])
    mine = [by_chip] + far
    theirs = [theirs] + [swap(x, "expert", 1) for x in far]
    mine, theirs = [[x.reshape(half, width) for x in xs] for xs in (mine, theirs)]

    count = groups * group_rows
    *grads, turned = call(
        far_kernel,
        [pltpu.VMEM((count, hidden_units), BF16)] * 3 + [pltpu.VMEM((2, portion, count), BF16)],
        [IN_SMEM, [IN_VMEM] * groups, [IN_VMEM] * groups] + [IN_VMEM] * 4 + [[IN_VMEM] * 3],
        [IN_VMEM] * 4,
        [pltpu.VMEM((count, width), BF16)],
        12,
    )(at, mine, theirs, parts, *weights, own)
    logit = call(
        logit_kernel,
        small,
        [IN_SMEM, IN_VMEM, [IN_VMEM] * chips, pl.BlockSpec(memory_space=pl.ANY)],
        IN_VMEM,
    )(at, tables, back, turned)
    logits = [logit] + [swap(logit, "dp", m) for m in range(1, groups)]
    result = jax.ShapeDtypeStruct((portion, hidden_units), F32)
    grad_gate, grad_up, grad_down = call(
        weight_kernel,
        [result] * 3,
        [IN_VMEM, [IN_VMEM] * 3, pl.BlockSpec(memory_space=pl.ANY)],
        [pl.BlockSpec(memory_space=pl.ANY)] * 3,
        [
            [pltpu.VMEM((portion, hidden_units), F32)] * 3,
            pltpu.SemaphoreType.DMA((hidden_units // STEP, 3)),
        ],
        12,
    )(turned, grads, logit)
    rows = jax.ShapeDtypeStruct((tok_count, features), BF16)
    mixed, grad_tokens, router_grad = call(
        last_kernel,
        [rows] * 2 + [jax.ShapeDtypeStruct((experts, features), F32)],
        [IN_SMEM]
        + [[IN_VMEM] * groups] * 3
        + [IN_VMEM, [IN_VMEM] * chips],
        [IN_VMEM] * 3,
        [pltpu.VMEM((count, features), BF16)],
    )(at, mine, theirs, logits, router_t, back)
    return (mixed, grad_tokens, router_grad.T, grad_gate, grad_up, grad_down)


def solution(mesh):
    return jax.shard_map(
        local,
        mesh=mesh,
        in_specs=(
            P(("dp", "expert"), None),
            P(("dp", "expert"), None),
            P(),
            P(None, "expert"),
            P(None, "expert"),
            P(None, "expert"),
            P(("dp", "expert"), None),
        ),
        out_specs=(
            P(("dp", "expert"), None),
            P(("dp", "expert"), None),
            P(),
            P("dp", "expert"),
            P("dp", "expert"),
            P("dp", "expert"),
        ),
        check_vma=False,
    )
```

```python
import jax
import jax.numpy as jnp
from jax import lax
from jax.experimental import pallas as pl
from jax.experimental.pallas import tpu as pltpu
from jax.sharding import PartitionSpec as P

F32 = jnp.float32
BF16 = jnp.bfloat16
LANES = 128
STEP = 256
GATHER_BYTES = 8 << 20
HIGHEST = lax.Precision.HIGHEST
LAST = (((1,), (1,)), ((), ()))
FIRST = (((0,), (0,)), ((), ()))
IN_VMEM = pl.BlockSpec(memory_space=pltpu.VMEM)
IN_SMEM = pl.BlockSpec(memory_space=pltpu.SMEM)


def dot(left, right, contract=(((1,), (0,)), ((), ()))):
    return lax.dot_general(left, right, contract, preferred_element_type=F32)


def swap(x, axis, mask):
    count = lax.axis_size(axis)
    return lax.ppermute(x, axis, [(i, i ^ mask) for i in range(count)])


def in_hbm(x):
    return pltpu.with_memory_space_constraint(x, pltpu.HBM)


def three_parts(x):
    parts = []
    for _ in range(3):
        part = lax.reduce_precision(x, 8, 7)
        parts.append(part.astype(BF16))
        x = x - part
    return parts


def exact_dot(left, right, contract):
    return sum(dot(left, part, contract) for part in three_parts(right)[::-1])


def gates_of(rows, chosen, router):
    logits = exact_dot(rows, router, (((1,), (0,)), ((), ())))
    picked = chosen > 0.5
    affinity = jnp.where(picked, jax.nn.sigmoid(logits), 0.0)
    denominator = jnp.sum(affinity, axis=1, keepdims=True)
    return picked, affinity, denominator, affinity / denominator


def place_rows(x_ref, first, core, mine_ref, theirs_ref):
    half = mine_ref.shape[0]
    x_ref[pl.ds(pl.multiple_of(first + core * half, half), half), :] = mine_ref[...]
    x_ref[pl.ds(pl.multiple_of(first + (1 - core) * half, half), half), :] = theirs_ref[...]


def gate_tables(x, parts_ref, experts):
    features = parts_ref.shape[1]
    logits = dot(parts_ref[...], x[:, :features], LAST)
    logits = logits[2 * experts :] + logits[experts : 2 * experts] + logits[:experts]
    unit = lax.broadcasted_iota(jnp.int32, (experts, LANES), 0) == lax.broadcasted_iota(
        jnp.int32, (experts, LANES), 1
    )
    picked = dot(unit.astype(BF16), x[:, 2 * features :], LAST) > 0.5
    affinity = jnp.where(picked, 1.0 / (1.0 + jnp.exp(-logits)), 0.0)
    denominator = jnp.sum(affinity, axis=0, keepdims=True)
    return affinity, denominator, affinity / denominator


def slot_gates(gates, expert):
    own = lax.broadcasted_iota(jnp.int32, (gates.shape[0], LANES), 0) == expert
    return lax.dot_general(
        gates, own.astype(F32), FIRST, precision=HIGHEST, preferred_element_type=F32
    )


def hidden_dots(start, x, w_gate_ref, w_up_ref, w_down_ref):
    features = w_gate_ref.shape[0]
    at = pl.ds(start, STEP)
    gate_pre = dot(x[:, :features], w_gate_ref[:, at])
    up_pre = dot(x[:, :features], w_up_ref[:, at])
    return gate_pre, up_pre, dot(x[:, features : 2 * features], w_down_ref[:, at])


def hidden_grads(gate_pre, up_pre, raw, slot_gate):
    sigma = 1.0 / (1.0 + jnp.exp(-gate_pre))
    silu = gate_pre * sigma
    hidden = silu * up_pre
    slot = jnp.tile(slot_gate, (1, STEP // LANES))
    hidden_grad = slot * raw
    gate_grad = hidden_grad * up_pre * sigma * (1.0 + gate_pre * (1.0 - sigma))
    grads = (gate_grad, hidden_grad * silu, slot * hidden)
    return [grad.astype(BF16) for grad in grads], hidden * raw


def load_kernel(_, *refs):
    count = len(refs) // 2
    copies = [
        pltpu.make_async_copy(refs[i], refs[count + i], refs[-1].at[i]) for i in range(count)
    ]
    for copy in copies:
        copy.start()
    for copy in copies:
        copy.wait()


def message_kernel(tokens_hbm, cot_hbm, routes_hbm, out_ref, tokens_ref, cot_ref, routes_ref, sems):
    count, features = tokens_ref.shape
    pairs = ((tokens_hbm, tokens_ref), (cot_hbm, cot_ref), (routes_hbm, routes_ref))
    copies = [pltpu.make_async_copy(*pair, sems.at[i]) for i, pair in enumerate(pairs)]
    for copy in copies:
        copy.start()
    for copy in copies:
        copy.wait()
    out_ref[:, :features] = tokens_ref[...]
    out_ref[:, features : 2 * features] = cot_ref[...]
    ids = lax.broadcasted_iota(jnp.int32, (count, LANES), 1)
    picked = jnp.zeros((count, LANES), F32)
    for k in range(routes_ref.shape[1]):
        picked += (routes_ref[:, k : k + 1] == ids).astype(F32)
    out_ref[:, 2 * features :] = picked.astype(BF16)


def order_kernel(at_ref, piece_refs, _, out_ref):
    for m, ref in enumerate(piece_refs):
        out_ref[at_ref[3] ^ m] = ref[...]


def own_kernel(
    at_ref, mine_ref, theirs_ref, parts_ref, w_gate_ref, w_up_ref, w_down_ref,
    keep_ref, send_ref, gate_grad_ref, up_grad_ref, gated_ref, pull_ref, table_ref,
    x_ref, back_ref,
):
    features, hidden_units = w_gate_ref.shape
    experts = parts_ref.shape[0] // 3
    core = at_ref[0]
    place_rows(x_ref, 0, core, mine_ref, theirs_ref)
    weights = (w_gate_ref, w_up_ref, w_down_ref)
    dots = hidden_dots(0, x_ref, *weights)
    affinity, denominator, gates = gate_tables(x_ref, parts_ref, experts)
    table_ref[0] = affinity
    table_ref[1] = gates
    table_ref[2] = jnp.broadcast_to(denominator, affinity.shape)
    slot_gate = slot_gates(gates, at_ref[1])
    pulls = jnp.zeros(slot_gate.shape, F32)
    for start in range(0, hidden_units, STEP):
        at = pl.ds(start, STEP)
        now = dots
        if start + STEP < hidden_units:
            dots = hidden_dots(start + STEP, x_ref, *weights)
        grads, pulled = hidden_grads(*now, slot_gate)
        gate_grad_ref[:, at], up_grad_ref[:, at], gated_ref[:, at] = grads
        pulls += sum(pulled[:, lane : lane + LANES] for lane in range(0, STEP, LANES))
    ones = jnp.ones((pull_ref.shape[0], LANES), F32)
    pull_ref[...] = lax.dot_general(
        ones, pulls, LAST, precision=HIGHEST, preferred_element_type=F32
    )
    for start in range(0, features, STEP):
        at = pl.ds(start, STEP)
        later = pl.ds(features + start, STEP)
        back_ref[:, at] = dot(gated_ref[...], w_down_ref[at, :], LAST).astype(BF16)
        back = dot(gate_grad_ref[...], w_gate_ref[at, :], LAST)
        back_ref[:, later] = (back + dot(up_grad_ref[...], w_up_ref[at, :], LAST)).astype(BF16)

    half = keep_ref.shape[0]
    keep_ref[...] = back_ref[pl.ds(pl.multiple_of(core * half, half), half), :]
    send_ref[...] = back_ref[pl.ds(pl.multiple_of((1 - core) * half, half), half), :]


def parts_of(x):
    parts = []
    for _ in range(3):
        parts.append(x.astype(BF16).astype(F32))
        x = x - parts[-1]
    return parts


def pair_kernel(at_ref, keep_ref, other_ref, pull_ref, other_pull_ref, *out_refs):
    features = keep_ref.shape[2]
    group_rows = pull_ref.shape[1]
    row = lax.broadcasted_iota(jnp.int32, pull_ref.shape, 0)
    pulls = jnp.where(row % 2 == at_ref[0], pull_ref[...], other_pull_ref[...])
    large, middle, low = parts_of(pulls)
    pulls = jnp.where(row < 2, large, jnp.where(row < 4, middle, low))
    tail = jnp.concatenate([pulls, jnp.zeros((row.shape[0], LANES - group_rows), F32)], axis=1)
    for m, ref in enumerate(out_refs):
        chip = at_ref[3] ^ m
        both = keep_ref[chip].astype(F32) + other_ref[chip].astype(F32)
        ref[:, :features] = both.astype(BF16)
        ref[:, features:] = tail.astype(BF16)


def logit_kernel(at_ref, table_ref, back_refs, _, out_ref):
    affinity, gates, denominator = table_ref[0], table_ref[1], table_ref[2]
    row = lax.broadcasted_iota(jnp.int32, affinity.shape, 0)
    width = back_refs[0].shape[1]
    pulls = jnp.zeros(affinity.shape, F32)
    for m, ref in enumerate(back_refs):
        tail = ref[:, width - LANES :].astype(F32)[:, : affinity.shape[1]]
        first = tail[0:1] + (tail[2:3] + tail[4:5])
        second = tail[1:2] + (tail[3:4] + tail[5:6])
        pulls = jnp.where(row // 2 == at_ref[3] ^ m, jnp.where(row % 2 == 0, first, second), pulls)
    mean_pull = jnp.sum(gates * pulls, axis=0, keepdims=True)
    out_ref[...] = (pulls - mean_pull) / denominator * affinity * (1.0 - affinity)


def send_weights(start, turned_ref, grad_refs, target_refs, out_refs, sems):
    at = pl.ds(start, STEP)
    copies = []
    for j, (grad_ref, out_ref, target_ref) in enumerate(zip(grad_refs, out_refs, target_refs)):
        here = pl.ds(start % out_ref.shape[1], STEP)
        out_ref[:, here] = dot(turned_ref[j // 2], grad_ref[:, at])
        copy = pltpu.make_async_copy(
            out_ref.at[:, here], target_ref.at[:, at], sems.at[start % out_ref.shape[1] // STEP, j]
        )
        copy.start()
        copies.append(copy)
    return copies


def far_kernel(
    at_ref, mine_refs, theirs_refs, parts_ref, w_gate_ref, w_up_ref, w_down_ref, own_refs,
    gate_grad_ref, up_grad_ref, gated_ref, turned_ref, x_ref, gate_ref, up_ref, down_ref,
    out_refs, sems,
):
    features, hidden_units = w_gate_ref.shape
    experts = parts_ref.shape[0] // 3
    grad_refs = (gate_grad_ref, up_grad_ref, gated_ref)
    target_refs = (gate_ref, up_ref, down_ref)
    portion = turned_ref.shape[1]
    group_rows = own_refs[0].shape[0]
    for m, (mine_ref, theirs_ref) in enumerate(zip(mine_refs, theirs_refs)):
        place_rows(x_ref, m * group_rows, at_ref[0], mine_ref, theirs_ref)
    first = at_ref[2] * portion
    for half in range(2):
        for row in range(0, portion, LANES):
            at = pl.ds(pl.multiple_of(half * features + first + row, LANES), LANES)
            turned_ref[half, row : row + LANES, :] = x_ref[:, at].T
    far = x_ref.at[group_rows:, :]
    weights = (w_gate_ref, w_up_ref, w_down_ref)
    dots = hidden_dots(0, far, *weights)
    slot_gate = slot_gates(gate_tables(far, parts_ref, experts)[2], at_ref[1])
    copies = []
    for start in range(0, hidden_units, STEP):
        at = pl.ds(start, STEP)
        now = dots
        if start + STEP < hidden_units:
            dots = hidden_dots(start + STEP, far, *weights)
        grads, _ = hidden_grads(*now, slot_gate)
        for grad_ref, own_ref, grad in zip(grad_refs, own_refs, grads):
            grad_ref[:group_rows, at] = own_ref[:, at]
            grad_ref[group_rows:, at] = grad
        if start < out_refs[0].shape[1]:
            copies += send_weights(start, turned_ref, grad_refs, target_refs, out_refs, sems)
    for copy in copies:
        copy.wait()


def weight_kernel(
    turned_ref, grad_refs, _, begun_refs, gate_ref, up_ref, down_ref, out_refs, sems
):
    hidden_units = grad_refs[0].shape[1]
    count = out_refs[0].shape[1]
    copies = []
    for start in range(hidden_units - count, hidden_units, STEP):
        copies += send_weights(
            start, turned_ref, grad_refs, (gate_ref, up_ref, down_ref), out_refs, sems
        )
    for copy in copies:
        copy.wait()


def last_kernel(
    at_ref, x_ref, logit_refs, router_ref, back_refs, mixed_ref, tokens_ref, router_grad_ref
):
    experts, features = router_ref.shape
    group_rows = x_ref.shape[0] // len(logit_refs)
    parts = [jnp.concatenate(parts_of(ref[...]), axis=0).astype(BF16) for ref in logit_refs]
    totals = []
    for m, part in enumerate(parts):
        total = dot(part, x_ref[m * group_rows : (m + 1) * group_rows, :features])
        totals.append(total[2 * experts :] + total[experts : 2 * experts] + total[:experts])
    while len(totals) > 1:
        totals = [totals[i] + totals[i + 1] for i in range(0, len(totals), 2)]
    router_grad_ref[...] = totals[0]
    count = mixed_ref.shape[0]
    shape = (count, group_rows)
    place = at_ref[0] * len(back_refs) + at_ref[3]
    row = lax.broadcasted_iota(jnp.int32, shape, 0) + place * count
    own = (lax.broadcasted_iota(jnp.int32, shape, 1) == row).astype(BF16)
    own_grads = dot(own, parts[0], LAST)
    back = jnp.zeros((count, features), F32)
    for e in range(experts):
        column = sum(own_grads[:, i + e : i + e + 1] for i in range(0, 3 * experts, experts))
        back += column * router_ref[e : e + 1, :]
    summed = sum(ref[...].astype(F32) for ref in back_refs)
    mixed_ref[...] = summed[:, :features].astype(BF16)
    tokens_ref[...] = (summed[:, features : 2 * features] + back).astype(BF16)


def call(kernel, out_shape, in_specs, out_specs, scratch=(), limit=4, aliases={}):
    return pl.pallas_call(
        kernel,
        out_shape=out_shape,
        in_specs=in_specs,
        out_specs=out_specs,
        scratch_shapes=scratch,
        input_output_aliases=aliases,
        compiler_params=pltpu.CompilerParams(vmem_limit_bytes=limit << 20),
        cost_estimate=pl.CostEstimate(flops=0, bytes_accessed=1, transcendentals=0),
    )


def local(tokens, routes, router, w_gate, w_up, w_down, cotangent):
    tok_count, features = tokens.shape
    experts = router.shape[1]
    hidden_units = w_gate.shape[1]
    devices = lax.axis_size("expert")
    groups = lax.axis_size("dp")
    sharing = devices // experts
    chips = devices // 2
    group_rows = devices * tok_count
    me = lax.axis_index("expert")
    group = lax.axis_index("dp")
    core, chip = me % 2, me // 2
    own_expert = me // sharing
    whole = sharing == 1 and group_rows <= LANES and groups * group_rows * features * 4 <= GATHER_BYTES

    def over_chips(x):
        out = jnp.zeros((chips,) + x.shape, x.dtype)
        for m in range(chips):
            piece = x if m == 0 else swap(x, "expert", 2 * m)
            out = lax.dynamic_update_index_in_dim(out, piece, chip ^ m, 0)
        return out

    def over_cores(x):
        other = swap(x, "expert", 1)
        return jnp.where(core == 0, jnp.stack([x, other]), jnp.stack([other, x]))

    if whole:
        return kernels_plan(tokens, routes, router, w_gate, w_up, w_down, cotangent)

    ids = jnp.arange(LANES, dtype=jnp.int32)
    picked_wide = jnp.any(routes[:, :, None] == ids[None, None, :], axis=1).astype(BF16)
    message = jnp.concatenate([tokens, cotangent, picked_wide], axis=1)
    width = message.shape[1]
    by_chip = over_chips(message)
    own = over_cores(by_chip).reshape(group_rows, width)
    rows, cot = own[:, :features], own[:, features : 2 * features]
    picked, affinity, denominator, gates = gates_of(
        rows, own[:, 2 * features : 2 * features + experts], router
    )
    slot_gate = lax.dynamic_slice_in_dim(gates, own_expert, 1, axis=1)
    gate_pre = dot(rows, w_gate)
    up_pre = dot(rows, w_up)
    sigma = jax.nn.sigmoid(gate_pre)
    silu = gate_pre * sigma
    hidden = silu * up_pre
    raw = dot(cot, w_down)
    pull = jnp.sum(hidden * raw, axis=1)
    hidden_grad = slot_gate * raw
    gate_grad = (hidden_grad * up_pre * sigma * (1.0 + gate_pre * (1.0 - sigma))).astype(BF16)
    up_grad = (hidden_grad * silu).astype(BF16)
    gated = (slot_gate * hidden).astype(BF16)
    mixed_part = dot(gated, w_down, LAST)
    input_part = dot(gate_grad, w_gate, LAST) + dot(up_grad, w_up, LAST)
    part = jnp.concatenate([mixed_part.astype(BF16), input_part.astype(BF16)], axis=1)
    part = part.reshape(2, chips, tok_count, 2 * features)
    keep = lax.dynamic_index_in_dim(part, core, 0, keepdims=False)
    send = lax.dynamic_index_in_dim(part, 1 - core, 0, keepdims=False)
    back = give_back(send_back(keep, send, chips, chip))
    total = sum(x.astype(F32) for x in back)
    pulls = over_cores(over_chips(pull))
    pulls = jnp.swapaxes(pulls, 0, 1).reshape(experts, sharing, -1)
    pulls = jnp.sum(pulls, axis=1).T
    mean_pull = jnp.sum(gates * pulls, axis=1, keepdims=True)
    logit_grad = (pulls - mean_pull) / denominator * affinity * (1.0 - affinity)
    logit_grad = jnp.where(picked, logit_grad, 0.0)
    place = core * chips + chip
    own_logit = lax.dynamic_slice_in_dim(logit_grad, place * tok_count, tok_count, axis=0)
    grad_router = lax.psum(exact_dot(tokens, own_logit, FIRST), ("dp", "expert"))
    router_back = lax.dot_general(own_logit, router, LAST, precision=HIGHEST)
    parts = [
        dot(left, right, FIRST)
        for left, right in ((rows, gate_grad), (rows, up_grad), (cot, gated))
    ]
    summed = lax.psum_scatter(
        jnp.concatenate(parts, axis=1).astype(BF16), "dp", scatter_dimension=0, tiled=True
    ).astype(F32)
    grad_gate, grad_up, grad_down = jnp.split(summed, 3, axis=1)
    mixed = total[:, :features].astype(BF16)
    grad_tokens = (total[:, features:] + router_back).astype(BF16)
    return (mixed, grad_tokens, grad_router, grad_gate, grad_up, grad_down)


def send_back(keep, send, chips, chip):
    summed = (keep.astype(F32) + swap(send, "expert", 1).astype(F32)).astype(BF16)
    return [
        lax.dynamic_index_in_dim(summed, chip ^ m, 0, keepdims=False) for m in range(chips)
    ]


def give_back(pieces):
    return [
        piece if m == 0 else swap(piece, "expert", 2 * m) for m, piece in enumerate(pieces)
    ]


def kernels_plan(tokens, routes, router, w_gate, w_up, w_down, cotangent):
    features, experts = router.shape
    hidden_units = w_gate.shape[1]
    tok_count = tokens.shape[0]
    width = 2 * features + LANES
    groups = lax.axis_size("dp")
    chips = lax.axis_size("expert") // 2
    me = lax.axis_index("expert")
    half = chips * tok_count
    group_rows = 2 * half
    portion = features // groups
    at = jnp.stack([me % 2, me, lax.axis_index("dp"), me // 2]).astype(jnp.int32)
    router_t = router.T
    parts = jnp.concatenate(three_parts(router_t), axis=0)
    weight_kinds = [pltpu.VMEM(w.shape, w.dtype) for w in (w_gate, w_up, w_down)]
    small = jax.ShapeDtypeStruct((experts, group_rows), F32)
    in_hbm_spec = pl.BlockSpec(memory_space=pltpu.HBM)

    sources = (tokens, cotangent, routes)
    message = call(
        message_kernel,
        jax.ShapeDtypeStruct((tok_count, width), BF16),
        [in_hbm_spec] * 3,
        IN_VMEM,
        [pltpu.VMEM(x.shape, x.dtype) for x in sources] + [pltpu.SemaphoreType.DMA((3,))],
    )(*[in_hbm(x) for x in sources])
    pieces = [message] + [swap(message, "expert", 2 * m) for m in range(1, chips)]
    weights = call(
        load_kernel,
        weight_kinds,
        [IN_SMEM] + [in_hbm_spec] * 3,
        [IN_VMEM] * 3,
        [pltpu.SemaphoreType.DMA((3,))],
    )(at, *[in_hbm(w) for w in (w_gate, w_up, w_down)])
    by_chip = call(
        order_kernel,
        jax.ShapeDtypeStruct((chips, tok_count, width), BF16),
        [IN_SMEM, [IN_VMEM] * chips, pl.BlockSpec(memory_space=pl.ANY)],
        IN_VMEM,
    )(at, pieces, weights[0])
    mine = [by_chip] + [swap(by_chip, "dp", m) for m in range(1, groups)]
    theirs = swap(by_chip, "expert", 1)

    rows = jax.ShapeDtypeStruct((half, 2 * features), BF16)
    grad = jax.ShapeDtypeStruct((group_rows, hidden_units), BF16)
    keep, send, *own, pull, tables = call(
        own_kernel,
        [rows] * 2 + [grad] * 3 + [small, jax.ShapeDtypeStruct((3,) + small.shape, F32)],
        [IN_SMEM] + [IN_VMEM] * 6,
        [IN_VMEM] * 7,
        [pltpu.VMEM((group_rows, width), BF16), pltpu.VMEM((group_rows, 2 * features), BF16)],
        8,
    )(at, by_chip.reshape(half, width), theirs.reshape(half, width), parts, *weights)
    rows = jax.ShapeDtypeStruct((tok_count, width), BF16)
    keep, send = [x.reshape(chips, tok_count, -1) for x in (keep, send)]
    pieces = call(
        pair_kernel,
        [rows] * chips,
        [IN_SMEM] + [IN_VMEM] * 4,
        [IN_VMEM] * chips,
    )(at, keep, swap(send, "expert", 1), pull, swap(pull, "expert", 1))
    back = give_back(pieces)
    _, *far = lax.optimization_barrier([pieces[0]] + mine[1:])
    mine = [by_chip] + far
    theirs = [theirs] + [swap(x, "expert", 1) for x in far]
    mine, theirs = [[x.reshape(half, width) for x in xs] for xs in (mine, theirs)]

    count = groups * group_rows
    begun = hidden_units // (2 * STEP) * STEP
    in_vmem = [pltpu.VMEM((count, hidden_units), BF16)] * 3
    *outs, grad_gate, grad_up, grad_down = call(
        far_kernel,
        in_vmem
        + [pltpu.VMEM((2, portion, count), BF16), pltpu.VMEM((count, width), BF16)]
        + [pltpu.HBM((portion, hidden_units), F32)] * 3,
        [IN_SMEM, [IN_VMEM] * groups, [IN_VMEM] * groups] + [IN_VMEM] * 4 + [[IN_VMEM] * 3],
        [IN_VMEM] * 5 + [in_hbm_spec] * 3,
        [
            [pltpu.VMEM((portion, begun), F32)] * 3,
            pltpu.SemaphoreType.DMA((begun // STEP, 3)),
        ],
        16,
    )(at, mine, theirs, parts, *weights, own)
    *grads, turned, x = outs
    logit = call(
        logit_kernel,
        small,
        [IN_SMEM, IN_VMEM, [IN_VMEM] * chips, pl.BlockSpec(memory_space=pl.ANY)],
        IN_VMEM,
    )(at, tables, back, turned)
    logits = [logit] + [swap(logit, "dp", m) for m in range(1, groups)]
    rest = hidden_units - begun
    grad_gate, grad_up, grad_down = call(
        weight_kernel,
        [pltpu.HBM((portion, hidden_units), F32)] * 3,
        [IN_VMEM, [IN_VMEM] * 3, pl.BlockSpec(memory_space=pl.ANY), [in_hbm_spec] * 3],
        [in_hbm_spec] * 3,
        [
            [pltpu.VMEM((portion, rest), F32)] * 3,
            pltpu.SemaphoreType.DMA((rest // STEP, 3)),
        ],
        16,
        {5: 0, 6: 1, 7: 2},
    )(turned, grads, logit, [grad_gate, grad_up, grad_down])
    rows = jax.ShapeDtypeStruct((tok_count, features), BF16)
    mixed, grad_tokens, router_grad = call(
        last_kernel,
        [rows] * 2 + [jax.ShapeDtypeStruct((experts, features), F32)],
        [IN_SMEM, IN_VMEM, [IN_VMEM] * groups, IN_VMEM, [IN_VMEM] * chips],
        [IN_VMEM] * 3,
    )(at, x, logits, router_t, back)
    return (mixed, grad_tokens, router_grad.T, grad_gate, grad_up, grad_down)


def solution(mesh):
    return jax.shard_map(
        local,
        mesh=mesh,
        in_specs=(
            P(("dp", "expert"), None),
            P(("dp", "expert"), None),
            P(),
            P(None, "expert"),
            P(None, "expert"),
            P(None, "expert"),
            P(("dp", "expert"), None),
        ),
        out_specs=(
            P(("dp", "expert"), None),
            P(("dp", "expert"), None),
            P(),
            P("dp", "expert"),
            P("dp", "expert"),
            P("dp", "expert"),
        ),
        check_vma=False,
    )
```

```python
import jax
import jax.numpy as jnp
from jax import lax
from jax.experimental import pallas as pl
from jax.experimental.pallas import tpu as pltpu
from jax.sharding import PartitionSpec as P

F32 = jnp.float32
BF16 = jnp.bfloat16
LANES = 128
STEP = 256
GATHER_BYTES = 8 << 20
HIGHEST = lax.Precision.HIGHEST
LAST = (((1,), (1,)), ((), ()))
FIRST = (((0,), (0,)), ((), ()))
IN_VMEM = pl.BlockSpec(memory_space=pltpu.VMEM)
IN_SMEM = pl.BlockSpec(memory_space=pltpu.SMEM)


def dot(left, right, contract=(((1,), (0,)), ((), ()))):
    return lax.dot_general(left, right, contract, preferred_element_type=F32)


def swap(x, axis, mask):
    count = lax.axis_size(axis)
    return lax.ppermute(x, axis, [(i, i ^ mask) for i in range(count)])


def in_hbm(x):
    return pltpu.with_memory_space_constraint(x, pltpu.HBM)


def three_parts(x):
    parts = []
    for _ in range(3):
        part = lax.reduce_precision(x, 8, 7)
        parts.append(part.astype(BF16))
        x = x - part
    return parts


def exact_dot(left, right, contract):
    return sum(dot(left, part, contract) for part in three_parts(right)[::-1])


def gates_of(rows, chosen, router):
    logits = exact_dot(rows, router, (((1,), (0,)), ((), ())))
    picked = chosen > 0.5
    affinity = jnp.where(picked, jax.nn.sigmoid(logits), 0.0)
    denominator = jnp.sum(affinity, axis=1, keepdims=True)
    return picked, affinity, denominator, affinity / denominator


def place_rows(x_ref, first, core, mine_ref, theirs_ref):
    half = mine_ref.shape[0]
    x_ref[pl.ds(pl.multiple_of(first + core * half, half), half), :] = mine_ref[...]
    x_ref[pl.ds(pl.multiple_of(first + (1 - core) * half, half), half), :] = theirs_ref[...]


def gate_tables(x, parts_ref, experts):
    features = parts_ref.shape[1]
    logits = dot(parts_ref[...], x[:, :features], LAST)
    logits = logits[2 * experts :] + logits[experts : 2 * experts] + logits[:experts]
    unit = lax.broadcasted_iota(jnp.int32, (experts, LANES), 0) == lax.broadcasted_iota(
        jnp.int32, (experts, LANES), 1
    )
    picked = dot(unit.astype(BF16), x[:, 2 * features :], LAST) > 0.5
    affinity = jnp.where(picked, 1.0 / (1.0 + jnp.exp(-logits)), 0.0)
    denominator = jnp.sum(affinity, axis=0, keepdims=True)
    return affinity, denominator, affinity / denominator


def slot_gates(gates, expert):
    own = lax.broadcasted_iota(jnp.int32, (gates.shape[0], LANES), 0) == expert
    return lax.dot_general(
        gates, own.astype(F32), FIRST, precision=HIGHEST, preferred_element_type=F32
    )


def hidden_dots(start, x, w_gate_ref, w_up_ref, w_down_ref):
    features = w_gate_ref.shape[0]
    at = pl.ds(start, STEP)
    gate_pre = dot(x[:, :features], w_gate_ref[:, at])
    up_pre = dot(x[:, :features], w_up_ref[:, at])
    return gate_pre, up_pre, dot(x[:, features : 2 * features], w_down_ref[:, at])


def hidden_grads(gate_pre, up_pre, raw, slot_gate):
    sigma = 1.0 / (1.0 + jnp.exp(-gate_pre))
    silu = gate_pre * sigma
    hidden = silu * up_pre
    slot = jnp.tile(slot_gate, (1, STEP // LANES))
    hidden_grad = slot * raw
    gate_grad = hidden_grad * up_pre * sigma * (1.0 + gate_pre * (1.0 - sigma))
    grads = (gate_grad, hidden_grad * silu, slot * hidden)
    return [grad.astype(BF16) for grad in grads], hidden * raw


def load_kernel(_, *refs):
    count = len(refs) // 2
    copies = [
        pltpu.make_async_copy(refs[i], refs[count + i], refs[-1].at[i]) for i in range(count)
    ]
    for copy in copies:
        copy.start()
    for copy in copies:
        copy.wait()


def message_kernel(tokens_hbm, cot_hbm, routes_hbm, out_ref, tokens_ref, cot_ref, routes_ref, sems):
    count, features = tokens_ref.shape
    pairs = ((tokens_hbm, tokens_ref), (cot_hbm, cot_ref), (routes_hbm, routes_ref))
    copies = [pltpu.make_async_copy(*pair, sems.at[i]) for i, pair in enumerate(pairs)]
    for copy in copies:
        copy.start()
    for copy in copies:
        copy.wait()
    out_ref[:, :features] = tokens_ref[...]
    out_ref[:, features : 2 * features] = cot_ref[...]
    ids = lax.broadcasted_iota(jnp.int32, (count, LANES), 1)
    picked = jnp.zeros((count, LANES), F32)
    for k in range(routes_ref.shape[1]):
        picked += (routes_ref[:, k : k + 1] == ids).astype(F32)
    out_ref[:, 2 * features :] = picked.astype(BF16)


def order_kernel(at_ref, piece_refs, _, out_ref):
    for m, ref in enumerate(piece_refs):
        out_ref[at_ref[3] ^ m] = ref[...]


def own_kernel(
    at_ref, mine_ref, theirs_ref, parts_ref, w_gate_ref, w_up_ref, w_down_ref,
    keep_ref, send_ref, gate_grad_ref, up_grad_ref, gated_ref, pull_ref, table_ref,
    x_ref, back_ref,
):
    features, hidden_units = w_gate_ref.shape
    experts = parts_ref.shape[0] // 3
    core = at_ref[0]
    place_rows(x_ref, 0, core, mine_ref, theirs_ref)
    weights = (w_gate_ref, w_up_ref, w_down_ref)
    dots = hidden_dots(0, x_ref, *weights)
    affinity, denominator, gates = gate_tables(x_ref, parts_ref, experts)
    table_ref[0] = affinity
    table_ref[1] = gates
    table_ref[2] = jnp.broadcast_to(denominator, affinity.shape)
    slot_gate = slot_gates(gates, at_ref[1])
    pulls = jnp.zeros(slot_gate.shape, F32)
    for start in range(0, hidden_units, STEP):
        at = pl.ds(start, STEP)
        now = dots
        if start + STEP < hidden_units:
            dots = hidden_dots(start + STEP, x_ref, *weights)
        grads, pulled = hidden_grads(*now, slot_gate)
        gate_grad_ref[:, at], up_grad_ref[:, at], gated_ref[:, at] = grads
        pulls += sum(pulled[:, lane : lane + LANES] for lane in range(0, STEP, LANES))
    ones = jnp.ones((pull_ref.shape[0], LANES), F32)
    pull_ref[...] = lax.dot_general(
        ones, pulls, LAST, precision=HIGHEST, preferred_element_type=F32
    )
    for start in range(0, features, STEP):
        at = pl.ds(start, STEP)
        later = pl.ds(features + start, STEP)
        back_ref[:, at] = dot(gated_ref[...], w_down_ref[at, :], LAST).astype(BF16)
        back = dot(gate_grad_ref[...], w_gate_ref[at, :], LAST)
        back_ref[:, later] = (back + dot(up_grad_ref[...], w_up_ref[at, :], LAST)).astype(BF16)

    half = keep_ref.shape[0]
    keep_ref[...] = back_ref[pl.ds(pl.multiple_of(core * half, half), half), :]
    send_ref[...] = back_ref[pl.ds(pl.multiple_of((1 - core) * half, half), half), :]


def parts_of(x):
    parts = []
    for _ in range(3):
        parts.append(x.astype(BF16).astype(F32))
        x = x - parts[-1]
    return parts


def pair_kernel(at_ref, keep_ref, other_ref, pull_ref, other_pull_ref, *out_refs):
    features = keep_ref.shape[2]
    group_rows = pull_ref.shape[1]
    row = lax.broadcasted_iota(jnp.int32, pull_ref.shape, 0)
    pulls = jnp.where(row % 2 == at_ref[0], pull_ref[...], other_pull_ref[...])
    large, middle, low = parts_of(pulls)
    pulls = jnp.where(row < 2, large, jnp.where(row < 4, middle, low))
    tail = jnp.concatenate([pulls, jnp.zeros((row.shape[0], LANES - group_rows), F32)], axis=1)
    for m, ref in enumerate(out_refs):
        chip = at_ref[3] ^ m
        both = keep_ref[chip].astype(F32) + other_ref[chip].astype(F32)
        ref[:, :features] = both.astype(BF16)
        ref[:, features:] = tail.astype(BF16)


def logit_kernel(at_ref, table_ref, back_refs, _, out_ref):
    affinity, gates, denominator = table_ref[0], table_ref[1], table_ref[2]
    row = lax.broadcasted_iota(jnp.int32, affinity.shape, 0)
    width = back_refs[0].shape[1]
    pulls = jnp.zeros(affinity.shape, F32)
    for m, ref in enumerate(back_refs):
        tail = ref[:, width - LANES :].astype(F32)[:, : affinity.shape[1]]
        first = tail[0:1] + (tail[2:3] + tail[4:5])
        second = tail[1:2] + (tail[3:4] + tail[5:6])
        pulls = jnp.where(row // 2 == at_ref[3] ^ m, jnp.where(row % 2 == 0, first, second), pulls)
    mean_pull = jnp.sum(gates * pulls, axis=0, keepdims=True)
    out_ref[...] = (pulls - mean_pull) / denominator * affinity * (1.0 - affinity)


def send_weights(start, turned_ref, grad_refs, target_refs, out_refs, sems):
    at = pl.ds(start, STEP)
    copies = []
    for j, (grad_ref, out_ref, target_ref) in enumerate(zip(grad_refs, out_refs, target_refs)):
        here = pl.ds(start % out_ref.shape[1], STEP)
        out_ref[:, here] = dot(turned_ref[j // 2], grad_ref[:, at])
        copy = pltpu.make_async_copy(
            out_ref.at[:, here], target_ref.at[:, at], sems.at[start % out_ref.shape[1] // STEP, j]
        )
        copy.start()
        copies.append(copy)
    return copies


def far_kernel(
    at_ref, mine_refs, theirs_refs, parts_ref, w_gate_ref, w_up_ref, w_down_ref, own_refs,
    gate_grad_ref, up_grad_ref, gated_ref, turned_ref, x_ref, gate_ref, up_ref, down_ref,
    out_refs, sems,
):
    features, hidden_units = w_gate_ref.shape
    experts = parts_ref.shape[0] // 3
    grad_refs = (gate_grad_ref, up_grad_ref, gated_ref)
    target_refs = (gate_ref, up_ref, down_ref)
    portion = turned_ref.shape[1]
    group_rows = own_refs[0].shape[0]
    for m, (mine_ref, theirs_ref) in enumerate(zip(mine_refs, theirs_refs)):
        place_rows(x_ref, m * group_rows, at_ref[0], mine_ref, theirs_ref)
    first = at_ref[2] * portion
    for half in range(2):
        for row in range(0, portion, LANES):
            at = pl.ds(pl.multiple_of(half * features + first + row, LANES), LANES)
            turned_ref[half, row : row + LANES, :] = x_ref[:, at].T
    far = x_ref.at[group_rows:, :]
    weights = (w_gate_ref, w_up_ref, w_down_ref)
    dots = hidden_dots(0, far, *weights)
    slot_gate = slot_gates(gate_tables(far, parts_ref, experts)[2], at_ref[1])
    copies = []
    for start in range(0, hidden_units, STEP):
        at = pl.ds(start, STEP)
        now = dots
        if start + STEP < hidden_units:
            dots = hidden_dots(start + STEP, far, *weights)
        grads, _ = hidden_grads(*now, slot_gate)
        for grad_ref, own_ref, grad in zip(grad_refs, own_refs, grads):
            grad_ref[:group_rows, at] = own_ref[:, at]
            grad_ref[group_rows:, at] = grad
        if start < out_refs[0].shape[1]:
            copies += send_weights(start, turned_ref, grad_refs, target_refs, out_refs, sems)
    for copy in copies:
        copy.wait()


def weight_kernel(
    turned_ref, grad_refs, _, begun_refs, gate_ref, up_ref, down_ref, out_refs, sems
):
    hidden_units = grad_refs[0].shape[1]
    count = out_refs[0].shape[1]
    copies = []
    for start in range(hidden_units - count, hidden_units, STEP):
        copies += send_weights(
            start, turned_ref, grad_refs, (gate_ref, up_ref, down_ref), out_refs, sems
        )
    for copy in copies:
        copy.wait()


def last_kernel(
    at_ref, x_ref, logit_refs, router_ref, back_refs, mixed_ref, tokens_ref, router_grad_ref
):
    experts, features = router_ref.shape
    group_rows = x_ref.shape[0] // len(logit_refs)
    parts = [jnp.concatenate(parts_of(ref[...]), axis=0).astype(BF16) for ref in logit_refs]
    totals = []
    for m, part in enumerate(parts):
        total = dot(part, x_ref[m * group_rows : (m + 1) * group_rows, :features])
        totals.append(total[2 * experts :] + total[experts : 2 * experts] + total[:experts])
    while len(totals) > 1:
        totals = [totals[i] + totals[i + 1] for i in range(0, len(totals), 2)]
    router_grad_ref[...] = totals[0]
    count = mixed_ref.shape[0]
    shape = (count, group_rows)
    place = at_ref[0] * len(back_refs) + at_ref[3]
    row = lax.broadcasted_iota(jnp.int32, shape, 0) + place * count
    own = (lax.broadcasted_iota(jnp.int32, shape, 1) == row).astype(BF16)
    own_grads = dot(own, parts[0], LAST)
    back = jnp.zeros((count, features), F32)
    for e in range(experts):
        column = sum(own_grads[:, i + e : i + e + 1] for i in range(0, 3 * experts, experts))
        back += column * router_ref[e : e + 1, :]
    summed = sum(ref[...].astype(F32) for ref in back_refs)
    mixed_ref[...] = summed[:, :features].astype(BF16)
    tokens_ref[...] = (summed[:, features : 2 * features] + back).astype(BF16)


def call(kernel, out_shape, in_specs, out_specs, scratch=(), limit=4, aliases={}):
    return pl.pallas_call(
        kernel,
        out_shape=out_shape,
        in_specs=in_specs,
        out_specs=out_specs,
        scratch_shapes=scratch,
        input_output_aliases=aliases,
        compiler_params=pltpu.CompilerParams(vmem_limit_bytes=limit << 20),
        cost_estimate=pl.CostEstimate(flops=0, bytes_accessed=1, transcendentals=0),
    )


def local(tokens, routes, router, w_gate, w_up, w_down, cotangent):
    tok_count, features = tokens.shape
    experts = router.shape[1]
    hidden_units = w_gate.shape[1]
    devices = lax.axis_size("expert")
    groups = lax.axis_size("dp")
    sharing = devices // experts
    chips = devices // 2
    group_rows = devices * tok_count
    me = lax.axis_index("expert")
    group = lax.axis_index("dp")
    core, chip = me % 2, me // 2
    own_expert = me // sharing
    whole = sharing == 1 and group_rows <= LANES and groups * group_rows * features * 4 <= GATHER_BYTES

    def over_chips(x):
        out = jnp.zeros((chips,) + x.shape, x.dtype)
        for m in range(chips):
            piece = x if m == 0 else swap(x, "expert", 2 * m)
            out = lax.dynamic_update_index_in_dim(out, piece, chip ^ m, 0)
        return out

    def over_cores(x):
        other = swap(x, "expert", 1)
        return jnp.where(core == 0, jnp.stack([x, other]), jnp.stack([other, x]))

    if whole:
        return kernels_plan(tokens, routes, router, w_gate, w_up, w_down, cotangent)

    ids = jnp.arange(LANES, dtype=jnp.int32)
    picked_wide = jnp.any(routes[:, :, None] == ids[None, None, :], axis=1).astype(BF16)
    message = jnp.concatenate([tokens, cotangent, picked_wide], axis=1)
    width = message.shape[1]
    by_chip = over_chips(message)
    own = over_cores(by_chip).reshape(group_rows, width)
    rows, cot = own[:, :features], own[:, features : 2 * features]
    picked, affinity, denominator, gates = gates_of(
        rows, own[:, 2 * features : 2 * features + experts], router
    )
    slot_gate = lax.dynamic_slice_in_dim(gates, own_expert, 1, axis=1)
    gate_pre = dot(rows, w_gate)
    up_pre = dot(rows, w_up)
    sigma = jax.nn.sigmoid(gate_pre)
    silu = gate_pre * sigma
    hidden = silu * up_pre
    raw = dot(cot, w_down)
    pull = jnp.sum(hidden * raw, axis=1)
    hidden_grad = slot_gate * raw
    gate_grad = (hidden_grad * up_pre * sigma * (1.0 + gate_pre * (1.0 - sigma))).astype(BF16)
    up_grad = (hidden_grad * silu).astype(BF16)
    gated = (slot_gate * hidden).astype(BF16)
    mixed_part = dot(gated, w_down, LAST)
    input_part = dot(gate_grad, w_gate, LAST) + dot(up_grad, w_up, LAST)
    part = jnp.concatenate([mixed_part.astype(BF16), input_part.astype(BF16)], axis=1)
    part = part.reshape(2, chips, tok_count, 2 * features)
    keep = lax.dynamic_index_in_dim(part, core, 0, keepdims=False)
    send = lax.dynamic_index_in_dim(part, 1 - core, 0, keepdims=False)
    back = give_back(send_back(keep, send, chips, chip))
    total = sum(x.astype(F32) for x in back)
    pulls = over_cores(over_chips(pull))
    pulls = jnp.swapaxes(pulls, 0, 1).reshape(experts, sharing, -1)
    pulls = jnp.sum(pulls, axis=1).T
    mean_pull = jnp.sum(gates * pulls, axis=1, keepdims=True)
    logit_grad = (pulls - mean_pull) / denominator * affinity * (1.0 - affinity)
    logit_grad = jnp.where(picked, logit_grad, 0.0)
    place = core * chips + chip
    own_logit = lax.dynamic_slice_in_dim(logit_grad, place * tok_count, tok_count, axis=0)
    grad_router = lax.psum(exact_dot(tokens, own_logit, FIRST), ("dp", "expert"))
    router_back = lax.dot_general(own_logit, router, LAST, precision=HIGHEST)
    parts = [
        dot(left, right, FIRST)
        for left, right in ((rows, gate_grad), (rows, up_grad), (cot, gated))
    ]
    summed = lax.psum_scatter(
        jnp.concatenate(parts, axis=1).astype(BF16), "dp", scatter_dimension=0, tiled=True
    ).astype(F32)
    grad_gate, grad_up, grad_down = jnp.split(summed, 3, axis=1)
    mixed = total[:, :features].astype(BF16)
    grad_tokens = (total[:, features:] + router_back).astype(BF16)
    return (mixed, grad_tokens, grad_router, grad_gate, grad_up, grad_down)


def send_back(keep, send, chips, chip):
    summed = (keep.astype(F32) + swap(send, "expert", 1).astype(F32)).astype(BF16)
    return [
        lax.dynamic_index_in_dim(summed, chip ^ m, 0, keepdims=False) for m in range(chips)
    ]


def give_back(pieces):
    return [
        piece if m == 0 else swap(piece, "expert", 2 * m) for m, piece in enumerate(pieces)
    ]


def kernels_plan(tokens, routes, router, w_gate, w_up, w_down, cotangent):
    features, experts = router.shape
    hidden_units = w_gate.shape[1]
    tok_count = tokens.shape[0]
    width = 2 * features + LANES
    groups = lax.axis_size("dp")
    chips = lax.axis_size("expert") // 2
    me = lax.axis_index("expert")
    half = chips * tok_count
    group_rows = 2 * half
    portion = features // groups
    at = jnp.stack([me % 2, me, lax.axis_index("dp"), me // 2]).astype(jnp.int32)
    router_t = router.T
    weight_kinds = [pltpu.VMEM(w.shape, w.dtype) for w in (w_gate, w_up, w_down)]
    small = jax.ShapeDtypeStruct((experts, group_rows), F32)
    in_hbm_spec = pl.BlockSpec(memory_space=pltpu.HBM)

    sources = (tokens, cotangent, routes)
    message = call(
        message_kernel,
        jax.ShapeDtypeStruct((tok_count, width), BF16),
        [in_hbm_spec] * 3,
        IN_VMEM,
        [pltpu.VMEM(x.shape, x.dtype) for x in sources] + [pltpu.SemaphoreType.DMA((3,))],
    )(*[in_hbm(x) for x in sources])
    pieces = [message] + [swap(message, "expert", 2 * m) for m in range(1, chips)]
    weights = call(
        load_kernel,
        weight_kinds,
        [IN_SMEM] + [in_hbm_spec] * 3,
        [IN_VMEM] * 3,
        [pltpu.SemaphoreType.DMA((3,))],
    )(at, *[in_hbm(w) for w in (w_gate, w_up, w_down)])
    by_chip = call(
        order_kernel,
        jax.ShapeDtypeStruct((chips, tok_count, width), BF16),
        [IN_SMEM, [IN_VMEM] * chips, pl.BlockSpec(memory_space=pl.ANY)],
        IN_VMEM,
    )(at, pieces, weights[0])
    mine = [by_chip] + [swap(by_chip, "dp", m) for m in range(1, groups)]
    theirs = swap(by_chip, "expert", 1)
    _, late_router = lax.optimization_barrier([by_chip, router_t])
    parts = jnp.concatenate(three_parts(late_router), axis=0)

    rows = jax.ShapeDtypeStruct((half, 2 * features), BF16)
    grad = jax.ShapeDtypeStruct((group_rows, hidden_units), BF16)
    keep, send, *own, pull, tables = call(
        own_kernel,
        [rows] * 2 + [grad] * 3 + [small, jax.ShapeDtypeStruct((3,) + small.shape, F32)],
        [IN_SMEM] + [IN_VMEM] * 6,
        [IN_VMEM] * 7,
        [pltpu.VMEM((group_rows, width), BF16), pltpu.VMEM((group_rows, 2 * features), BF16)],
        8,
    )(at, by_chip.reshape(half, width), theirs.reshape(half, width), parts, *weights)
    rows = jax.ShapeDtypeStruct((tok_count, width), BF16)
    keep, send = [x.reshape(chips, tok_count, -1) for x in (keep, send)]
    pieces = call(
        pair_kernel,
        [rows] * chips,
        [IN_SMEM] + [IN_VMEM] * 4,
        [IN_VMEM] * chips,
    )(at, keep, swap(send, "expert", 1), pull, swap(pull, "expert", 1))
    back = give_back(pieces)
    _, *far = lax.optimization_barrier([pieces[0]] + mine[1:])
    mine = [by_chip] + far
    theirs = [theirs] + [swap(x, "expert", 1) for x in far]
    mine, theirs = [[x.reshape(half, width) for x in xs] for xs in (mine, theirs)]

    count = groups * group_rows
    begun = hidden_units // (2 * STEP) * STEP
    in_vmem = [pltpu.VMEM((count, hidden_units), BF16)] * 3
    *outs, grad_gate, grad_up, grad_down = call(
        far_kernel,
        in_vmem
        + [pltpu.VMEM((2, portion, count), BF16), pltpu.VMEM((count, width), BF16)]
        + [pltpu.HBM((portion, hidden_units), F32)] * 3,
        [IN_SMEM, [IN_VMEM] * groups, [IN_VMEM] * groups] + [IN_VMEM] * 4 + [[IN_VMEM] * 3],
        [IN_VMEM] * 5 + [in_hbm_spec] * 3,
        [
            [pltpu.VMEM((portion, begun), F32)] * 3,
            pltpu.SemaphoreType.DMA((begun // STEP, 3)),
        ],
        16,
    )(at, mine, theirs, parts, *weights, own)
    *grads, turned, x = outs
    logit = call(
        logit_kernel,
        small,
        [IN_SMEM, IN_VMEM, [IN_VMEM] * chips, pl.BlockSpec(memory_space=pl.ANY)],
        IN_VMEM,
    )(at, tables, back, turned)
    logits = [logit] + [swap(logit, "dp", m) for m in range(1, groups)]
    rest = hidden_units - begun
    grad_gate, grad_up, grad_down = call(
        weight_kernel,
        [pltpu.HBM((portion, hidden_units), F32)] * 3,
        [IN_VMEM, [IN_VMEM] * 3, pl.BlockSpec(memory_space=pl.ANY), [in_hbm_spec] * 3],
        [in_hbm_spec] * 3,
        [
            [pltpu.VMEM((portion, rest), F32)] * 3,
            pltpu.SemaphoreType.DMA((rest // STEP, 3)),
        ],
        16,
        {5: 0, 6: 1, 7: 2},
    )(turned, grads, logit, [grad_gate, grad_up, grad_down])
    rows = jax.ShapeDtypeStruct((tok_count, features), BF16)
    mixed, grad_tokens, router_grad = call(
        last_kernel,
        [rows] * 2 + [jax.ShapeDtypeStruct((experts, features), F32)],
        [IN_SMEM, IN_VMEM, [IN_VMEM] * groups, IN_VMEM, [IN_VMEM] * chips],
        [IN_VMEM] * 3,
    )(at, x, logits, router_t, back)
    return (mixed, grad_tokens, router_grad.T, grad_gate, grad_up, grad_down)


def solution(mesh):
    return jax.shard_map(
        local,
        mesh=mesh,
        in_specs=(
            P(("dp", "expert"), None),
            P(("dp", "expert"), None),
            P(),
            P(None, "expert"),
            P(None, "expert"),
            P(None, "expert"),
            P(("dp", "expert"), None),
        ),
        out_specs=(
            P(("dp", "expert"), None),
            P(("dp", "expert"), None),
            P(),
            P("dp", "expert"),
            P("dp", "expert"),
            P("dp", "expert"),
        ),
        check_vma=False,
    )
```

```python
import jax
import jax.numpy as jnp
from jax import lax
from jax.experimental import pallas as pl
from jax.experimental.pallas import tpu as pltpu
from jax.sharding import PartitionSpec as P

F32 = jnp.float32
BF16 = jnp.bfloat16
LANES = 128
STEP = 256
GATHER_BYTES = 8 << 20
HIGHEST = lax.Precision.HIGHEST
LAST = (((1,), (1,)), ((), ()))
FIRST = (((0,), (0,)), ((), ()))
IN_VMEM = pl.BlockSpec(memory_space=pltpu.VMEM)
IN_SMEM = pl.BlockSpec(memory_space=pltpu.SMEM)


def dot(left, right, contract=(((1,), (0,)), ((), ()))):
    return lax.dot_general(left, right, contract, preferred_element_type=F32)


def swap(x, axis, mask):
    count = lax.axis_size(axis)
    return lax.ppermute(x, axis, [(i, i ^ mask) for i in range(count)])


def in_hbm(x):
    return pltpu.with_memory_space_constraint(x, pltpu.HBM)


def three_parts(x):
    parts = []
    for _ in range(3):
        part = lax.reduce_precision(x, 8, 7)
        parts.append(part.astype(BF16))
        x = x - part
    return parts


def exact_dot(left, right, contract):
    return sum(dot(left, part, contract) for part in three_parts(right)[::-1])


def gates_of(rows, chosen, router):
    logits = exact_dot(rows, router, (((1,), (0,)), ((), ())))
    picked = chosen > 0.5
    affinity = jnp.where(picked, jax.nn.sigmoid(logits), 0.0)
    denominator = jnp.sum(affinity, axis=1, keepdims=True)
    return picked, affinity, denominator, affinity / denominator


def place_rows(x_ref, first, core, mine_ref, theirs_ref):
    half = mine_ref.shape[0]
    x_ref[pl.ds(pl.multiple_of(first + core * half, half), half), :] = mine_ref[...]
    x_ref[pl.ds(pl.multiple_of(first + (1 - core) * half, half), half), :] = theirs_ref[...]


def gate_tables(x, parts_ref, experts):
    features = parts_ref.shape[1]
    logits = dot(parts_ref[...], x[:, :features], LAST)
    logits = logits[2 * experts :] + logits[experts : 2 * experts] + logits[:experts]
    unit = lax.broadcasted_iota(jnp.int32, (experts, LANES), 0) == lax.broadcasted_iota(
        jnp.int32, (experts, LANES), 1
    )
    picked = dot(unit.astype(BF16), x[:, 2 * features :], LAST) > 0.5
    affinity = jnp.where(picked, 1.0 / (1.0 + jnp.exp(-logits)), 0.0)
    denominator = jnp.sum(affinity, axis=0, keepdims=True)
    return affinity, denominator, affinity / denominator


def slot_gates(gates, expert):
    own = lax.broadcasted_iota(jnp.int32, (gates.shape[0], LANES), 0) == expert
    return lax.dot_general(
        gates, own.astype(F32), FIRST, precision=HIGHEST, preferred_element_type=F32
    )


def hidden_dots(start, x, w_gate_ref, w_up_ref, w_down_ref):
    features = w_gate_ref.shape[0]
    at = pl.ds(start, STEP)
    gate_pre = dot(x[:, :features], w_gate_ref[:, at])
    up_pre = dot(x[:, :features], w_up_ref[:, at])
    return gate_pre, up_pre, dot(x[:, features : 2 * features], w_down_ref[:, at])


def hidden_grads(gate_pre, up_pre, raw, slot_gate):
    sigma = 1.0 / (1.0 + jnp.exp(-gate_pre))
    silu = gate_pre * sigma
    hidden = silu * up_pre
    slot = jnp.tile(slot_gate, (1, STEP // LANES))
    hidden_grad = slot * raw
    gate_grad = hidden_grad * up_pre * sigma * (1.0 + gate_pre * (1.0 - sigma))
    grads = (gate_grad, hidden_grad * silu, slot * hidden)
    return [grad.astype(BF16) for grad in grads], hidden * raw


def load_kernel(_, *refs):
    count = len(refs) // 2
    copies = [
        pltpu.make_async_copy(refs[i], refs[count + i], refs[-1].at[i]) for i in range(count)
    ]
    for copy in copies:
        copy.start()
    for copy in copies:
        copy.wait()


def message_kernel(tokens_hbm, cot_hbm, routes_hbm, out_ref, tokens_ref, cot_ref, routes_ref, sems):
    count, features = tokens_ref.shape
    pairs = ((routes_hbm, routes_ref), (tokens_hbm, tokens_ref), (cot_hbm, cot_ref))
    copies = [pltpu.make_async_copy(*pair, sems.at[i]) for i, pair in enumerate(pairs)]
    for copy in copies:
        copy.start()
    copies[0].wait()
    ids = lax.broadcasted_iota(jnp.int32, (count, LANES), 1)
    picked = jnp.zeros((count, LANES), F32)
    for k in range(routes_ref.shape[1]):
        picked += (routes_ref[:, k : k + 1] == ids).astype(F32)
    out_ref[:, 2 * features :] = picked.astype(BF16)
    copies[1].wait()
    out_ref[:, :features] = tokens_ref[...]
    copies[2].wait()
    out_ref[:, features : 2 * features] = cot_ref[...]


def order_kernel(at_ref, piece_refs, _, out_ref):
    for m, ref in enumerate(piece_refs):
        out_ref[at_ref[3] ^ m] = ref[...]


def own_kernel(
    at_ref, mine_ref, theirs_ref, parts_ref, w_gate_ref, w_up_ref, w_down_ref,
    keep_ref, send_ref, gate_grad_ref, up_grad_ref, gated_ref, pull_ref, table_ref,
    x_ref, back_ref,
):
    features, hidden_units = w_gate_ref.shape
    experts = parts_ref.shape[0] // 3
    core = at_ref[0]
    place_rows(x_ref, 0, core, mine_ref, theirs_ref)
    weights = (w_gate_ref, w_up_ref, w_down_ref)
    dots = hidden_dots(0, x_ref, *weights)
    affinity, denominator, gates = gate_tables(x_ref, parts_ref, experts)
    table_ref[0] = affinity
    table_ref[1] = gates
    table_ref[2] = jnp.broadcast_to(denominator, affinity.shape)
    slot_gate = slot_gates(gates, at_ref[1])
    pulls = jnp.zeros(slot_gate.shape, F32)
    for start in range(0, hidden_units, STEP):
        at = pl.ds(start, STEP)
        now = dots
        if start + STEP < hidden_units:
            dots = hidden_dots(start + STEP, x_ref, *weights)
        grads, pulled = hidden_grads(*now, slot_gate)
        gate_grad_ref[:, at], up_grad_ref[:, at], gated_ref[:, at] = grads
        pulls += sum(pulled[:, lane : lane + LANES] for lane in range(0, STEP, LANES))
    ones = jnp.ones((pull_ref.shape[0], LANES), F32)
    pull_ref[...] = lax.dot_general(
        ones, pulls, LAST, precision=HIGHEST, preferred_element_type=F32
    )
    for start in range(0, features, STEP):
        at = pl.ds(start, STEP)
        later = pl.ds(features + start, STEP)
        back_ref[:, at] = dot(gated_ref[...], w_down_ref[at, :], LAST).astype(BF16)
        back = dot(gate_grad_ref[...], w_gate_ref[at, :], LAST)
        back_ref[:, later] = (back + dot(up_grad_ref[...], w_up_ref[at, :], LAST)).astype(BF16)

    half = keep_ref.shape[0]
    keep_ref[...] = back_ref[pl.ds(pl.multiple_of(core * half, half), half), :]
    send_ref[...] = back_ref[pl.ds(pl.multiple_of((1 - core) * half, half), half), :]


def parts_of(x):
    parts = []
    for _ in range(3):
        parts.append(x.astype(BF16).astype(F32))
        x = x - parts[-1]
    return parts


def pair_kernel(at_ref, keep_ref, other_ref, pull_ref, other_pull_ref, *out_refs):
    features = keep_ref.shape[2]
    group_rows = pull_ref.shape[1]
    row = lax.broadcasted_iota(jnp.int32, pull_ref.shape, 0)
    pulls = jnp.where(row % 2 == at_ref[0], pull_ref[...], other_pull_ref[...])
    large, middle, low = parts_of(pulls)
    pulls = jnp.where(row < 2, large, jnp.where(row < 4, middle, low))
    tail = jnp.concatenate([pulls, jnp.zeros((row.shape[0], LANES - group_rows), F32)], axis=1)
    for m, ref in enumerate(out_refs):
        chip = at_ref[3] ^ m
        both = keep_ref[chip].astype(F32) + other_ref[chip].astype(F32)
        ref[:, :features] = both.astype(BF16)
        ref[:, features:] = tail.astype(BF16)


def logit_kernel(at_ref, table_ref, back_refs, _, out_ref):
    affinity, gates, denominator = table_ref[0], table_ref[1], table_ref[2]
    row = lax.broadcasted_iota(jnp.int32, affinity.shape, 0)
    width = back_refs[0].shape[1]
    pulls = jnp.zeros(affinity.shape, F32)
    for m, ref in enumerate(back_refs):
        tail = ref[:, width - LANES :].astype(F32)[:, : affinity.shape[1]]
        first = tail[0:1] + (tail[2:3] + tail[4:5])
        second = tail[1:2] + (tail[3:4] + tail[5:6])
        pulls = jnp.where(row // 2 == at_ref[3] ^ m, jnp.where(row % 2 == 0, first, second), pulls)
    mean_pull = jnp.sum(gates * pulls, axis=0, keepdims=True)
    out_ref[...] = (pulls - mean_pull) / denominator * affinity * (1.0 - affinity)


def send_weights(start, turned_ref, grad_refs, target_refs, out_refs, sems):
    at = pl.ds(start, STEP)
    copies = []
    for j, (grad_ref, out_ref, target_ref) in enumerate(zip(grad_refs, out_refs, target_refs)):
        here = pl.ds(start % out_ref.shape[1], STEP)
        out_ref[:, here] = dot(turned_ref[j // 2], grad_ref[:, at])
        copy = pltpu.make_async_copy(
            out_ref.at[:, here], target_ref.at[:, at], sems.at[start % out_ref.shape[1] // STEP, j]
        )
        copy.start()
        copies.append(copy)
    return copies


def far_kernel(
    at_ref, mine_refs, theirs_refs, parts_ref, w_gate_ref, w_up_ref, w_down_ref, own_refs,
    gate_grad_ref, up_grad_ref, gated_ref, turned_ref, x_ref, gate_ref, up_ref, down_ref,
    out_refs, sems,
):
    features, hidden_units = w_gate_ref.shape
    experts = parts_ref.shape[0] // 3
    grad_refs = (gate_grad_ref, up_grad_ref, gated_ref)
    target_refs = (gate_ref, up_ref, down_ref)
    portion = turned_ref.shape[1]
    group_rows = own_refs[0].shape[0]
    for m, (mine_ref, theirs_ref) in enumerate(zip(mine_refs, theirs_refs)):
        place_rows(x_ref, m * group_rows, at_ref[0], mine_ref, theirs_ref)
    first = at_ref[2] * portion
    for half in range(2):
        for row in range(0, portion, LANES):
            at = pl.ds(pl.multiple_of(half * features + first + row, LANES), LANES)
            turned_ref[half, row : row + LANES, :] = x_ref[:, at].T
    far = x_ref.at[group_rows:, :]
    weights = (w_gate_ref, w_up_ref, w_down_ref)
    dots = hidden_dots(0, far, *weights)
    slot_gate = slot_gates(gate_tables(far, parts_ref, experts)[2], at_ref[1])
    copies = []
    for start in range(0, hidden_units, STEP):
        at = pl.ds(start, STEP)
        now = dots
        if start + STEP < hidden_units:
            dots = hidden_dots(start + STEP, far, *weights)
        grads, _ = hidden_grads(*now, slot_gate)
        for grad_ref, own_ref, grad in zip(grad_refs, own_refs, grads):
            grad_ref[:group_rows, at] = own_ref[:, at]
            grad_ref[group_rows:, at] = grad
        if start < out_refs[0].shape[1]:
            copies += send_weights(start, turned_ref, grad_refs, target_refs, out_refs, sems)
    for copy in copies:
        copy.wait()


def weight_kernel(
    turned_ref, grad_refs, _, begun_refs, gate_ref, up_ref, down_ref, out_refs, sems
):
    hidden_units = grad_refs[0].shape[1]
    count = out_refs[0].shape[1]
    copies = []
    for start in range(hidden_units - count, hidden_units, STEP):
        copies += send_weights(
            start, turned_ref, grad_refs, (gate_ref, up_ref, down_ref), out_refs, sems
        )
    for copy in copies:
        copy.wait()


def last_kernel(
    at_ref, x_ref, logit_refs, router_ref, back_refs, mixed_ref, tokens_ref, router_grad_ref
):
    experts, features = router_ref.shape
    group_rows = x_ref.shape[0] // len(logit_refs)
    parts = [jnp.concatenate(parts_of(ref[...]), axis=0).astype(BF16) for ref in logit_refs]
    totals = []
    for m, part in enumerate(parts):
        total = dot(part, x_ref[m * group_rows : (m + 1) * group_rows, :features])
        totals.append(total[2 * experts :] + total[experts : 2 * experts] + total[:experts])
    while len(totals) > 1:
        totals = [totals[i] + totals[i + 1] for i in range(0, len(totals), 2)]
    router_grad_ref[...] = totals[0]
    count = mixed_ref.shape[0]
    shape = (count, group_rows)
    place = at_ref[0] * len(back_refs) + at_ref[3]
    row = lax.broadcasted_iota(jnp.int32, shape, 0) + place * count
    own = (lax.broadcasted_iota(jnp.int32, shape, 1) == row).astype(BF16)
    own_grads = dot(own, parts[0], LAST)
    back = jnp.zeros((count, features), F32)
    for e in range(experts):
        column = sum(own_grads[:, i + e : i + e + 1] for i in range(0, 3 * experts, experts))
        back += column * router_ref[e : e + 1, :]
    summed = sum(ref[...].astype(F32) for ref in back_refs)
    mixed_ref[...] = summed[:, :features].astype(BF16)
    tokens_ref[...] = (summed[:, features : 2 * features] + back).astype(BF16)


def call(kernel, out_shape, in_specs, out_specs, scratch=(), limit=4, aliases={}):
    return pl.pallas_call(
        kernel,
        out_shape=out_shape,
        in_specs=in_specs,
        out_specs=out_specs,
        scratch_shapes=scratch,
        input_output_aliases=aliases,
        compiler_params=pltpu.CompilerParams(vmem_limit_bytes=limit << 20),
        cost_estimate=pl.CostEstimate(flops=0, bytes_accessed=1, transcendentals=0),
    )


def local(tokens, routes, router, w_gate, w_up, w_down, cotangent):
    tok_count, features = tokens.shape
    experts = router.shape[1]
    hidden_units = w_gate.shape[1]
    devices = lax.axis_size("expert")
    groups = lax.axis_size("dp")
    sharing = devices // experts
    chips = devices // 2
    group_rows = devices * tok_count
    me = lax.axis_index("expert")
    group = lax.axis_index("dp")
    core, chip = me % 2, me // 2
    own_expert = me // sharing
    whole = sharing == 1 and group_rows <= LANES and groups * group_rows * features * 4 <= GATHER_BYTES

    def over_chips(x):
        out = jnp.zeros((chips,) + x.shape, x.dtype)
        for m in range(chips):
            piece = x if m == 0 else swap(x, "expert", 2 * m)
            out = lax.dynamic_update_index_in_dim(out, piece, chip ^ m, 0)
        return out

    def over_cores(x):
        other = swap(x, "expert", 1)
        return jnp.where(core == 0, jnp.stack([x, other]), jnp.stack([other, x]))

    if whole:
        return kernels_plan(tokens, routes, router, w_gate, w_up, w_down, cotangent)

    ids = jnp.arange(LANES, dtype=jnp.int32)
    picked_wide = jnp.any(routes[:, :, None] == ids[None, None, :], axis=1).astype(BF16)
    message = jnp.concatenate([tokens, cotangent, picked_wide], axis=1)
    width = message.shape[1]
    by_chip = over_chips(message)
    own = over_cores(by_chip).reshape(group_rows, width)
    rows, cot = own[:, :features], own[:, features : 2 * features]
    picked, affinity, denominator, gates = gates_of(
        rows, own[:, 2 * features : 2 * features + experts], router
    )
    slot_gate = lax.dynamic_slice_in_dim(gates, own_expert, 1, axis=1)
    gate_pre = dot(rows, w_gate)
    up_pre = dot(rows, w_up)
    sigma = jax.nn.sigmoid(gate_pre)
    silu = gate_pre * sigma
    hidden = silu * up_pre
    raw = dot(cot, w_down)
    pull = jnp.sum(hidden * raw, axis=1)
    hidden_grad = slot_gate * raw
    gate_grad = (hidden_grad * up_pre * sigma * (1.0 + gate_pre * (1.0 - sigma))).astype(BF16)
    up_grad = (hidden_grad * silu).astype(BF16)
    gated = (slot_gate * hidden).astype(BF16)
    mixed_part = dot(gated, w_down, LAST)
    input_part = dot(gate_grad, w_gate, LAST) + dot(up_grad, w_up, LAST)
    part = jnp.concatenate([mixed_part.astype(BF16), input_part.astype(BF16)], axis=1)
    part = part.reshape(2, chips, tok_count, 2 * features)
    keep = lax.dynamic_index_in_dim(part, core, 0, keepdims=False)
    send = lax.dynamic_index_in_dim(part, 1 - core, 0, keepdims=False)
    back = give_back(send_back(keep, send, chips, chip))
    total = sum(x.astype(F32) for x in back)
    pulls = over_cores(over_chips(pull))
    pulls = jnp.swapaxes(pulls, 0, 1).reshape(experts, sharing, -1)
    pulls = jnp.sum(pulls, axis=1).T
    mean_pull = jnp.sum(gates * pulls, axis=1, keepdims=True)
    logit_grad = (pulls - mean_pull) / denominator * affinity * (1.0 - affinity)
    logit_grad = jnp.where(picked, logit_grad, 0.0)
    place = core * chips + chip
    own_logit = lax.dynamic_slice_in_dim(logit_grad, place * tok_count, tok_count, axis=0)
    grad_router = lax.psum(exact_dot(tokens, own_logit, FIRST), ("dp", "expert"))
    router_back = lax.dot_general(own_logit, router, LAST, precision=HIGHEST)
    parts = [
        dot(left, right, FIRST)
        for left, right in ((rows, gate_grad), (rows, up_grad), (cot, gated))
    ]
    summed = lax.psum_scatter(
        jnp.concatenate(parts, axis=1).astype(BF16), "dp", scatter_dimension=0, tiled=True
    ).astype(F32)
    grad_gate, grad_up, grad_down = jnp.split(summed, 3, axis=1)
    mixed = total[:, :features].astype(BF16)
    grad_tokens = (total[:, features:] + router_back).astype(BF16)
    return (mixed, grad_tokens, grad_router, grad_gate, grad_up, grad_down)


def send_back(keep, send, chips, chip):
    summed = (keep.astype(F32) + swap(send, "expert", 1).astype(F32)).astype(BF16)
    return [
        lax.dynamic_index_in_dim(summed, chip ^ m, 0, keepdims=False) for m in range(chips)
    ]


def give_back(pieces):
    return [
        piece if m == 0 else swap(piece, "expert", 2 * m) for m, piece in enumerate(pieces)
    ]


def kernels_plan(tokens, routes, router, w_gate, w_up, w_down, cotangent):
    features, experts = router.shape
    hidden_units = w_gate.shape[1]
    tok_count = tokens.shape[0]
    width = 2 * features + LANES
    groups = lax.axis_size("dp")
    chips = lax.axis_size("expert") // 2
    me = lax.axis_index("expert")
    half = chips * tok_count
    group_rows = 2 * half
    portion = features // groups
    at = jnp.stack([me % 2, me, lax.axis_index("dp"), me // 2]).astype(jnp.int32)
    router_t = router.T
    weight_kinds = [pltpu.VMEM(w.shape, w.dtype) for w in (w_gate, w_up, w_down)]
    small = jax.ShapeDtypeStruct((experts, group_rows), F32)
    in_hbm_spec = pl.BlockSpec(memory_space=pltpu.HBM)

    sources = (tokens, cotangent, routes)
    message = call(
        message_kernel,
        jax.ShapeDtypeStruct((tok_count, width), BF16),
        [in_hbm_spec] * 3,
        IN_VMEM,
        [pltpu.VMEM(x.shape, x.dtype) for x in sources] + [pltpu.SemaphoreType.DMA((3,))],
    )(*[in_hbm(x) for x in sources])
    pieces = [message] + [swap(message, "expert", 2 * m) for m in range(1, chips)]
    weights = call(
        load_kernel,
        weight_kinds,
        [IN_SMEM] + [in_hbm_spec] * 3,
        [IN_VMEM] * 3,
        [pltpu.SemaphoreType.DMA((3,))],
    )(at, *[in_hbm(w) for w in (w_gate, w_up, w_down)])
    by_chip = call(
        order_kernel,
        jax.ShapeDtypeStruct((chips, tok_count, width), BF16),
        [IN_SMEM, [IN_VMEM] * chips, pl.BlockSpec(memory_space=pl.ANY)],
        IN_VMEM,
    )(at, pieces, weights[0])
    mine = [by_chip] + [swap(by_chip, "dp", m) for m in range(1, groups)]
    theirs = swap(by_chip, "expert", 1)
    _, late_router = lax.optimization_barrier([by_chip, router_t])
    parts = jnp.concatenate(three_parts(late_router), axis=0)

    rows = jax.ShapeDtypeStruct((half, 2 * features), BF16)
    grad = jax.ShapeDtypeStruct((group_rows, hidden_units), BF16)
    keep, send, *own, pull, tables = call(
        own_kernel,
        [rows] * 2 + [grad] * 3 + [small, jax.ShapeDtypeStruct((3,) + small.shape, F32)],
        [IN_SMEM] + [IN_VMEM] * 6,
        [IN_VMEM] * 7,
        [pltpu.VMEM((group_rows, width), BF16), pltpu.VMEM((group_rows, 2 * features), BF16)],
        8,
    )(at, by_chip.reshape(half, width), theirs.reshape(half, width), parts, *weights)
    rows = jax.ShapeDtypeStruct((tok_count, width), BF16)
    keep, send = [x.reshape(chips, tok_count, -1) for x in (keep, send)]
    pieces = call(
        pair_kernel,
        [rows] * chips,
        [IN_SMEM] + [IN_VMEM] * 4,
        [IN_VMEM] * chips,
    )(at, keep, swap(send, "expert", 1), pull, swap(pull, "expert", 1))
    back = give_back(pieces)
    _, *far = lax.optimization_barrier([pieces[0]] + mine[1:])
    mine = [by_chip] + far
    theirs = [theirs] + [swap(x, "expert", 1) for x in far]
    mine, theirs = [[x.reshape(half, width) for x in xs] for xs in (mine, theirs)]

    count = groups * group_rows
    begun = hidden_units // (2 * STEP) * STEP
    in_vmem = [pltpu.VMEM((count, hidden_units), BF16)] * 3
    *outs, grad_gate, grad_up, grad_down = call(
        far_kernel,
        in_vmem
        + [pltpu.VMEM((2, portion, count), BF16), pltpu.VMEM((count, width), BF16)]
        + [pltpu.HBM((portion, hidden_units), F32)] * 3,
        [IN_SMEM, [IN_VMEM] * groups, [IN_VMEM] * groups] + [IN_VMEM] * 4 + [[IN_VMEM] * 3],
        [IN_VMEM] * 5 + [in_hbm_spec] * 3,
        [
            [pltpu.VMEM((portion, begun), F32)] * 3,
            pltpu.SemaphoreType.DMA((begun // STEP, 3)),
        ],
        16,
    )(at, mine, theirs, parts, *weights, own)
    *grads, turned, x = outs
    logit = call(
        logit_kernel,
        small,
        [IN_SMEM, IN_VMEM, [IN_VMEM] * chips, pl.BlockSpec(memory_space=pl.ANY)],
        IN_VMEM,
    )(at, tables, back, turned)
    logits = [logit] + [swap(logit, "dp", m) for m in range(1, groups)]
    rest = hidden_units - begun
    grad_gate, grad_up, grad_down = call(
        weight_kernel,
        [pltpu.HBM((portion, hidden_units), F32)] * 3,
        [IN_VMEM, [IN_VMEM] * 3, pl.BlockSpec(memory_space=pl.ANY), [in_hbm_spec] * 3],
        [in_hbm_spec] * 3,
        [
            [pltpu.VMEM((portion, rest), F32)] * 3,
            pltpu.SemaphoreType.DMA((rest // STEP, 3)),
        ],
        16,
        {5: 0, 6: 1, 7: 2},
    )(turned, grads, logit, [grad_gate, grad_up, grad_down])
    rows = jax.ShapeDtypeStruct((tok_count, features), BF16)
    mixed, grad_tokens, router_grad = call(
        last_kernel,
        [rows] * 2 + [jax.ShapeDtypeStruct((experts, features), F32)],
        [IN_SMEM, IN_VMEM, [IN_VMEM] * groups, IN_VMEM, [IN_VMEM] * chips],
        [IN_VMEM] * 3,
    )(at, x, logits, router_t, back)
    return (mixed, grad_tokens, router_grad.T, grad_gate, grad_up, grad_down)


def solution(mesh):
    return jax.shard_map(
        local,
        mesh=mesh,
        in_specs=(
            P(("dp", "expert"), None),
            P(("dp", "expert"), None),
            P(),
            P(None, "expert"),
            P(None, "expert"),
            P(None, "expert"),
            P(("dp", "expert"), None),
        ),
        out_specs=(
            P(("dp", "expert"), None),
            P(("dp", "expert"), None),
            P(),
            P("dp", "expert"),
            P("dp", "expert"),
            P("dp", "expert"),
        ),
        check_vma=False,
    )
```
